32 devices in a mesh: dp: 8 (over y, x, core), expert: 4 (over z).
Axes of the slice: x: 2, y: 2, z: 4, core: 2. Of those that a mesh axis runs over, the one named last changes fastest.
Arguments:
- tokens: bfloat16 [4096, 1024], P(('dp', 'expert')), may hold values from -6 to 6
- first_gain: bfloat16 [1024], P(('dp', 'expert')), may hold values from 0.5 to 1.5
- w_qkv: bfloat16 [1024, 3072], P(('dp', 'expert')), may hold values from -0.1875 to 0.1875
- w_out: bfloat16 [1024, 1024], P(('dp', 'expert')), may hold values from -1 to 1
- second_gain: bfloat16 [1024], P(('dp', 'expert')), may hold values from 0.5 to 1.5
- w_mix: bfloat16 [1024, 2], P(('dp', 'expert')), may hold values from -0.1875 to 0.1875
- w_up: bfloat16 [1024, 4096], P(('dp', 'expert')), may hold values from -0.1875 to 0.1875
- w_down: bfloat16 [4096, 1024], P(('dp', 'expert')), may hold values from -0.1875 to 0.1875
- expert_up: bfloat16 [4, 1024, 4096], P('expert', 'dp'), may hold values from -0.1875 to 0.1875
- expert_down: bfloat16 [4, 4096, 1024], P('expert', 'dp'), may hold values from -0.1875 to 0.1875
- expert_ids: int32 [4096, 1], P(('dp', 'expert')), may hold values from 0 to 3; in each aligned block of 128 rows (0 to 127, 128 to 255, ...) at most 40 rows name the same one
- doc_lengths: int32 [8, 2], P('dp'), may hold values from 64 to 448, as said below
- out_grad: bfloat16 [4096, 1024], P(('dp', 'expert')), may hold values from -6 to 6
Outputs:
- output: bfloat16 [4096, 1024], P(('dp', 'expert'))
- tokens_grad: bfloat16 [4096, 1024], P(('dp', 'expert'))
- first_gain_grad: float32 [1024], P(('dp', 'expert'))
- w_qkv_grad: float32 [1024, 3072], P(('dp', 'expert'))
- w_out_grad: float32 [1024, 1024], P(('dp', 'expert'))
- second_gain_grad: float32 [1024], P(('dp', 'expert'))
- w_mix_grad: float32 [1024, 2], P(('dp', 'expert'))
- w_up_grad: float32 [1024, 4096], P(('dp', 'expert'))
- w_down_grad: float32 [4096, 1024], P(('dp', 'expert'))
- expert_up_grad: float32 [4, 1024, 4096], P('expert', 'dp')
- expert_down_grad: float32 [4, 4096, 1024], P('expert', 'dp')
The draws below stay inside these ranges and needn't reach their ends.
Inputs may be any that keep to these rules, and one draw needn't show every extreme that they name: `expert_ids`: in each device's 128 rows no expert is chosen more than 40 times, a bound that some block reaches in some of them. `doc_lengths`: the two lengths of a group sum to 512; the longer is exactly 448 and stands first or second.
All inputs are finite; a program needn't handle non-finite values.
Results may differ from the reference program's by a relative error of at most 0.015.
Values may be sent and summed in bfloat16 or wider, within the bound.
No kernel may reach another device: no remote copies, remote signals or barrier semaphores. Data moves between devices by JAX's collectives and lax.ppermute only.
A program may use at most 256 MiB of HBM per device.

```python
import math
from functools import partial
import jax
import jax.numpy as jnp
import numpy as np
from jax import lax

D = 1024
HEADS = 16
HEAD_DIM = 64
FF = 4096
TOK_DEV = 128
GROUP_TOK = 512
GROUPS = 8
TOKENS = 4096
EXPERTS = 4
CAP = 40
N_DP = 8
N_EXPERT = 4


def draw_doc_lengths(key, part):
    key = jax.random.fold_in(key, 7)
    flips = jax.random.randint(key, (GROUPS,), 0, 2)
    longer = GROUP_TOK - TOK_DEV // 2
    first = jnp.where(flips == 1, longer, GROUP_TOK - longer).astype(jnp.int32)
    return jnp.stack([first, (GROUP_TOK - first).astype(jnp.int32)], axis=1)


def levels(own_key, extent, cuts, smallest, high):
    loudness = 1.0
    for position, parts in cuts:
        steps = jax.random.uniform(jax.random.fold_in(jax.random.fold_in(own_key, 6), position), (parts,), jnp.float32, smallest / len(cuts), high / len(cuts))
        loudness = loudness * jnp.repeat(jnp.exp(steps), extent[position] // parts).reshape((-1,) + (1,) * (len(extent) - 1 - position))
    return loudness


def routed_block(key, own, number, rows, number_of, top, reach, lean):
    order = jax.random.permutation(key, number_of)
    crowded, ordinary = load_shares(number_of, rows * top, reach, lean, True), load_shares(number_of, rows * top, reach, lean, False)
    places = jnp.arange(number_of)

    def named(sizes, offset_by):
        used = int((sizes > 0).sum())
        fixed = max(1, used // 4)
        shifted = fixed + (places - fixed + offset_by * (used - fixed)) % max(1, number_of - fixed)
        return jnp.zeros((number_of,), jnp.int32).at[order[jnp.where(places < fixed, places, shifted)]].set(jnp.asarray(sizes, jnp.int32))

    sizes = jnp.where(number % 4 == 0, named(crowded, number // 4), named(ordinary, number - number // 4 - 1))
    mixed = jax.random.permutation(jax.random.fold_in(own, 3), number_of)
    donor, receiver = mixed[0:number_of // 2 * 2:2], mixed[1:number_of // 2 * 2:2]
    margin = jnp.minimum(sizes[donor] - 1, reach - sizes[receiver]) // 2
    margin = jnp.where((donor == order[0]) | (receiver == order[0]) | (sizes[receiver] == 0), 0, jnp.maximum(margin, 0))
    shifted = jax.random.randint(jax.random.fold_in(own, 4), (number_of // 2,), 0, 1 << 20) % (margin + 1)
    sizes = sizes.at[donor].add(-shifted).at[receiver].add(shifted)
    members = jnp.searchsorted(jnp.cumsum(sizes), jnp.arange(rows * top), side="right").astype(jnp.int32)
    table = members.reshape(top, rows).T
    table = table[jax.random.permutation(jax.random.fold_in(own, 1), rows)]
    offset_by = jax.random.randint(jax.random.fold_in(own, 2), (rows, 1), 0, top)
    return jnp.take_along_axis(table, (jnp.arange(top)[None, :] + offset_by) % top, axis=1)


def load_shares(number_of, total, most, lean, full):
    loads = [(1 << 20) // math.isqrt(standing ** lean) + 1 for standing in range(1, number_of + 1)]
    largest = most if full else min(most, max(-(-total // number_of), total * loads[0] // sum(loads)))
    least = 1 if total - largest >= number_of - 1 else 0
    holding, surplus = [largest] + [least] * (number_of - 1), total - largest - least * (number_of - 1)
    while surplus > 0:
        candidates = [i for i in range(1, number_of) if holding[i] < largest] or [i for i in range(1, number_of) if holding[i] < most]
        pool, budget = sum([loads[i] for i in candidates]), surplus
        for i in candidates:
            extra = min(most - holding[i], max(1, budget * loads[i] // pool), surplus)
            holding[i] = holding[i] + extra
            surplus = surplus - extra
    return np.array(holding)


def bell_draw(key, extent, deviation, reach, shards=(), kind=jnp.bfloat16):
    entries = jax.random.normal(key, extent, jnp.float32) * deviation
    if len(shards) > 0:
        entries = levels(key, extent, shards, -0.22, 0.18) * entries
    return jnp.clip(entries, min=-reach, max=reach).astype(kind)


def setup_inputs(seed: int = 0) -> dict:
    splits = jax.random.split(jax.random.key(seed), 14)
    tokens = bell_draw(splits[0], (TOKENS, D), 1.0, 6.0, ((0, 32),))
    first_gain = jnp.clip(1.0 + 0.1 * jax.random.normal(splits[1], (D,), jnp.float32), 0.5, 1.5).astype(jnp.bfloat16)
    w_qkv = bell_draw(splits[2], (D, 3 * D), D ** -0.5, 0.1875, ((0, 32),))
    w_out = bell_draw(splits[3], (D, D), (D // 32) ** -0.5, 1.0, ((0, 32),))
    second_gain = jnp.clip(1.0 + 0.1 * jax.random.normal(splits[4], (D,), jnp.float32), 0.5, 1.5).astype(jnp.bfloat16)
    w_mix = bell_draw(splits[5], (D, 2), D ** -0.5, 0.1875, ((0, 32),))
    w_up = bell_draw(splits[6], (D, FF), D ** -0.5, 0.1875, ((0, 32),))
    w_down = bell_draw(splits[7], (FF, D), (FF // 4) ** -0.5, 0.1875, ((0, 32),))
    expert_up = bell_draw(splits[8], (EXPERTS, D, FF), D ** -0.5, 0.1875, ((0, 4), (1, 8)))
    expert_down = bell_draw(splits[9], (EXPERTS, FF, D), (FF // 4) ** -0.5, 0.1875, ((0, 4), (1, 8)))
    expert_ids_keys = jax.random.split(jax.random.fold_in(splits[10], 1), TOKENS // TOK_DEV)
    expert_ids_turns = jax.random.permutation(jax.random.fold_in(splits[10], 3), TOKENS // TOK_DEV)
    expert_ids = jax.vmap(lambda own, number: routed_block(jax.random.fold_in(splits[10], 2), own, number, TOK_DEV, EXPERTS, 1, CAP, 1))(expert_ids_keys, expert_ids_turns).reshape((TOKENS, 1))
    doc_lengths = draw_doc_lengths(jax.random.fold_in(splits[13], 71), 0)
    out_grad = bell_draw(splits[12], (TOKENS, D), 1.0, 6.0, ((0, 32),))
    return {"tokens": tokens, "first_gain": first_gain, "w_qkv": w_qkv, "w_out": w_out, "second_gain": second_gain, "w_mix": w_mix, "w_up": w_up, "w_down": w_down, "expert_up": expert_up, "expert_down": expert_down, "expert_ids": expert_ids, "doc_lengths": doc_lengths, "out_grad": out_grad}


PRECISE = lax.Precision.HIGHEST
EPSILON = 1e-05
SCORE_SCALE = 0.125
MASK_VALUE = -1e+30

@jax.custom_vjp
def low(v):
    return lax.optimization_barrier(v.astype(jnp.bfloat16)).astype(jnp.float32)

@jax.custom_vjp
def low_back(v):
    return v

def low_keep(v):
    return (low(v), None)

def low_pass(kept, grad):
    return (grad,)

def back_keep(v):
    return (v, None)

def back_low(kept, grad):
    return (low(grad),)
low.defvjp(low_keep, low_pass)
low_back.defvjp(back_keep, back_low)

def norm_rows(values, gain_vec):
    row_mean = lax.optimization_barrier(jnp.mean(values, axis=-1, keepdims=True))
    centred = values - row_mean
    spread = lax.optimization_barrier(jnp.mean(centred * centred, axis=-1, keepdims=True))
    return centred * lax.rsqrt(spread + EPSILON) * gain_vec

def smooth(values):
    return jax.nn.gelu(values, approximate=True)

def matmul_hi(left_mat, right_mat):
    return jnp.dot(left_mat, right_mat, precision=PRECISE, preferred_element_type=jnp.float32)

def group_attention(group_item):
    query, key_heads, value_heads, doc_split = group_item
    key_total = query.shape[0]
    block_size = min(512, key_total)
    key_pos = jnp.arange(key_total, dtype=jnp.int32)

    def one_block(block_index):
        query_block = lax.dynamic_slice_in_dim(query, (block_index * block_size).astype(jnp.int32), block_size, 0)
        query_pos = (block_index * block_size + jnp.arange(block_size, dtype=jnp.int32)).astype(jnp.int32)
        scores = low_back(jnp.einsum('qhd,khd->hqk', query_block, key_heads, precision=PRECISE) * SCORE_SCALE)
        allowed = (query_pos[:, None] >= key_pos[None, :]) & ((query_pos[:, None] >= doc_split) == (key_pos[None, :] >= doc_split))
        scores = jnp.where(allowed[None], scores, MASK_VALUE)
        probs = jax.nn.softmax(scores, axis=-1)
        return jnp.einsum('hqk,khd->qhd', low(probs), value_heads, precision=PRECISE)
    return lax.map(jax.checkpoint(one_block), jnp.arange(key_total // block_size, dtype=jnp.int32))

def serve_expert(group_item):
    rows_in, up_matrix, down_matrix = group_item
    upper_proj = low_back(matmul_hi(rows_in, up_matrix))
    return matmul_hi(low(smooth(upper_proj)), down_matrix)

def forward(slot_index, doc_splits, tokens, first_gain, w_qkv, w_out, second_gain, w_mix, w_up, w_down, expert_up, expert_down):
    first_normed = norm_rows(tokens, first_gain)
    qkv = low_back(low(matmul_hi(low(first_normed), w_qkv)))
    grouped = qkv.reshape(GROUPS, GROUP_TOK, 3, HEADS, HEAD_DIM)
    attended = lax.map(jax.checkpoint(group_attention), (grouped[:, :, 0], grouped[:, :, 1], grouped[:, :, 2], doc_splits))
    attended = low_back(low(attended.reshape(GROUPS * GROUP_TOK, D)))
    middle = tokens + low_back(matmul_hi(attended, w_out))
    ffn_input = low(norm_rows(middle, second_gain))
    coeffs = jax.nn.softmax(low_back(matmul_hi(ffn_input, w_mix)), axis=-1)
    dense_out = low_back(matmul_hi(low(smooth(low_back(matmul_hi(ffn_input, w_up)))), w_down))
    routed_in = low_back(ffn_input)
    limit = N_DP * N_EXPERT * CAP
    routed = jnp.zeros((EXPERTS * limit, D), jnp.float32).at[slot_index].set(routed_in).reshape(EXPERTS, limit, D)
    served = lax.map(jax.checkpoint(serve_expert), (routed, expert_up, expert_down))
    expert_rows = low_back(low(served.reshape(EXPERTS * limit, D)[slot_index]))
    return middle + coeffs[:, 0:1] * dense_out + coeffs[:, 1:2] * expert_rows

def reference(tokens, first_gain, w_qkv, w_out, second_gain, w_mix, w_up, w_down, expert_up, expert_down, expert_ids, doc_lengths, out_grad):
    expert_choice = expert_ids[:, 0].astype(jnp.int32)
    onehot = (expert_choice[:, None] == jnp.arange(EXPERTS, dtype=jnp.int32)[None, :]).astype(jnp.int32)
    slot_rank = lax.optimization_barrier(jnp.sum((jnp.cumsum(onehot, axis=0) - 1) * onehot, axis=1))
    slot_index = (expert_choice * (N_DP * N_EXPERT * CAP) + slot_rank).astype(jnp.int32)
    doc_splits = doc_lengths[:, 0].astype(jnp.int32)
    float_args = tuple((v.astype(jnp.float32) for v in (tokens, first_gain, w_qkv, w_out, second_gain, w_mix, w_up, w_down, expert_up, expert_down)))
    output, pullback = jax.vjp(partial(forward, slot_index, doc_splits), *float_args)
    gradients = pullback(out_grad.astype(jnp.float32))
    return (output.astype(jnp.bfloat16), gradients[0].astype(jnp.bfloat16), gradients[1], gradients[2], gradients[3], gradients[4], gradients[5], gradients[6], gradients[7], gradients[8], gradients[9])
```

```python
import jax
import jax.numpy as jnp
from jax import lax
from jax.sharding import Mesh
from jax.sharding import PartitionSpec as P

HEAD_DIM = 64
EPSILON = 1e-05
SCORE_SCALE = 0.125
MASK_VALUE = -1e30
F32 = jnp.float32
BF16 = jnp.bfloat16
DP = ("chip", "core")
LANES = 128


def norm_parts(values):
    row_mean = jnp.mean(values, axis=-1, keepdims=True)
    centred = values - row_mean
    spread = jnp.mean(centred * centred, axis=-1, keepdims=True)
    inverse = lax.rsqrt(spread + EPSILON)
    return (centred * inverse, inverse)


def norm_back(grad, normed, inverse, gain):
    scaled = grad * gain
    return inverse * (
        scaled
        - jnp.mean(scaled, axis=-1, keepdims=True)
        - normed * jnp.mean(scaled * normed, axis=-1, keepdims=True)
    )


def smooth(values):
    return jax.nn.gelu(values, approximate=True)


def smooth_back(values, grad):
    return jax.vjp(smooth, values)[1](grad)[0]


def dot(left, right):
    return jnp.dot(left, right, preferred_element_type=F32)


def dot_rt(left, right):
    return lax.dot_general(left, right, (((1,), (1,)), ((), ())), preferred_element_type=F32)


def dot_lt(left, right):
    return lax.dot_general(left, right, (((0,), (0,)), ((), ())), preferred_element_type=F32)


def gather(values, axes):
    return lax.all_gather(values, axes, axis=0, tiled=True)


def scatter_sum(values, axes):
    return lax.psum_scatter(values, axes, scatter_dimension=0, tiled=True)


def swap(values, axis):
    return lax.all_to_all(values, axis, split_axis=0, concat_axis=0, tiled=True)


def other_core(values):
    return lax.ppermute(values, "core", [(0, 1), (1, 0)])


def high_low(values):
    high = values.astype(BF16)
    return (high, (values - high.astype(F32)).astype(BF16))


def shards(
    tokens,
    first_gain,
    w_qkv,
    w_out,
    second_gain,
    w_mix,
    w_up,
    w_down,
    expert_up,
    expert_down,
    expert_ids,
    doc_lengths,
    out_grad,
):
    rows, width = tokens.shape
    n_chip, n_core, n_exp = (lax.axis_size(a) for a in ("chip", "core", "expert"))
    n_dp = n_chip * n_core
    group = rows * n_exp
    heads = width // HEAD_DIM // n_exp
    head_cols = heads * HEAD_DIM
    w_rows = w_qkv.shape[0]
    dense_rows = w_down.shape[0]
    dense_cols = n_dp * dense_rows
    exp_rows = expert_up.shape[1]
    exp_cols = expert_down.shape[1]
    ex = lax.axis_index("expert")
    core = lax.axis_index("core")
    start = ex * rows
    capacity = n_exp * max(2, 5 * rows // (4 * n_exp))

    exp_split = (
        expert_up[0]
        .reshape(exp_rows, n_chip, n_core, exp_cols)
        .transpose(2, 0, 1, 3)
        .reshape(n_core, exp_rows, n_chip * exp_cols)
    )
    own_half = jnp.where(core == 0, exp_split[0], exp_split[1])
    sent_half = jnp.where(core == 0, exp_split[1], exp_split[0])
    got_half = other_core(sent_half)
    chip_up = jnp.concatenate(
        [jnp.where(core == 0, own_half, got_half), jnp.where(core == 0, got_half, own_half)], axis=0
    )
    up_expert = gather(chip_up, "chip")
    down_expert = gather(expert_down[0], "chip")

    qkv_blocks = (
        w_qkv.reshape(w_rows, 3, n_exp, head_cols)
        .transpose(2, 0, 1, 3)
        .reshape(n_exp, w_rows, 3 * head_cols)
    )
    small = jnp.concatenate([first_gain[:, None], second_gain[:, None], w_mix], axis=1)
    small = jnp.pad(small, ((0, 0), (0, LANES - 4)))
    small = jnp.broadcast_to(small[None], (n_exp, w_rows, LANES))
    up_blocks = (
        w_up.reshape(w_rows, n_dp, n_exp, dense_rows)
        .transpose(2, 0, 1, 3)
        .reshape(n_exp, w_rows, dense_cols)
    )
    dealt = swap(jnp.concatenate([qkv_blocks, small, up_blocks], axis=2), "expert")
    dealt = dealt.reshape(n_exp * w_rows, 3 * head_cols + LANES + dense_cols)
    first_all = gather(dealt[:, : 3 * head_cols + LANES], DP)
    qkv_matrix = first_all[:, : 3 * head_cols]
    small_all = first_all[:, 3 * head_cols : 3 * head_cols + 4].astype(F32)
    gain_one = small_all[:, 0][None, :]
    gain_two = small_all[:, 1][None, :]
    mix_matrix = first_all[:, 3 * head_cols + 2 : 3 * head_cols + 4]
    mix_rows = small_all[:, 2:4].T
    up_matrix = gather(dealt[:, 3 * head_cols + LANES :], DP)
    down_matrix = gather(w_down, DP)
    out_matrix = gather(w_out, ("chip", "core", "expert"))

    inputs = gather(tokens, "expert").astype(F32)
    id_row = jnp.pad(expert_ids[:, 0].astype(BF16)[None], ((0, 7), (0, width - rows)))
    grad_pack = gather(jnp.concatenate([out_grad, id_row], axis=0), "expert")
    grad_pack = grad_pack.reshape(n_exp, rows + 8, width)
    grad_low = grad_pack[:, :rows].reshape(group, width)
    choice = grad_pack[:, rows, :rows].reshape(group)
    grad_output = grad_low.astype(F32)

    normed_one, inverse_one = norm_parts(inputs)
    attn_input = (normed_one * gain_one).astype(BF16)
    qkv = dot(attn_input, qkv_matrix).astype(BF16)
    query = qkv[:, :head_cols].reshape(group, heads, HEAD_DIM)
    keys = qkv[:, head_cols : 2 * head_cols].reshape(group, heads, HEAD_DIM)
    vals = qkv[:, 2 * head_cols :].reshape(group, heads, HEAD_DIM)
    doc_split = doc_lengths[0, 0]
    place = jnp.arange(group, dtype=jnp.int32)
    allowed = (place[:, None] >= place[None, :]) & (
        (place[:, None] >= doc_split) == (place[None, :] >= doc_split)
    )
    scores = jnp.einsum("qhd,khd->hqk", query, keys, preferred_element_type=F32) * SCORE_SCALE
    probs = jax.nn.softmax(jnp.where(allowed[None], scores, MASK_VALUE), axis=-1)
    probs_low = probs.astype(BF16)
    attended_own = jnp.einsum("hqk,khd->qhd", probs_low, vals, preferred_element_type=F32)
    attended_own = attended_own.reshape(group, head_cols).astype(BF16)
    attended = lax.all_gather(attended_own, "expert", axis=1, tiled=True)

    middle = inputs + dot(attended, out_matrix)
    normed_two, inverse_two = norm_parts(middle)
    ffn_input = (normed_two * gain_two).astype(BF16)
    coeffs = jax.nn.softmax(dot(ffn_input, mix_matrix), axis=-1)

    ddense = (coeffs[:, 0:1] * grad_output).astype(BF16)
    dexpert = (coeffs[:, 1:2] * grad_output).astype(BF16)
    dense_pre = dot(ffn_input, up_matrix)
    dense_act = smooth(dense_pre).astype(BF16)
    dense_part = dot(dense_act, down_matrix)
    dense_dpre = smooth_back(dense_pre, dot_rt(ddense, down_matrix)).astype(BF16)
    dffn_part = dot_rt(dense_dpre, up_matrix)
    down_part = dot_lt(dense_act, ddense).astype(BF16)
    up_part = dot_lt(ffn_input, dense_dpre).astype(BF16)

    chosen = choice == ex.astype(BF16)
    slot = jnp.where(chosen, jnp.cumsum(chosen.astype(jnp.int32)) - 1, -1)
    pick = (jnp.arange(capacity, dtype=jnp.int32)[:, None] == slot[None, :]).astype(BF16)
    rows_in = dot(pick, ffn_input).astype(BF16)
    rows_grad = dot(pick, dexpert).astype(BF16)
    pair = other_core(jnp.concatenate([rows_in, rows_grad], axis=1))
    rows_in = jnp.concatenate([rows_in, pair[:, :width]], axis=0)
    rows_grad = jnp.concatenate([rows_grad, pair[:, width:]], axis=0)
    exp_pre = dot(rows_in, up_expert)
    exp_act = smooth(exp_pre).astype(BF16)
    exp_part = dot(exp_act, down_expert)
    exp_dpre = smooth_back(exp_pre, dot_rt(rows_grad, down_expert)).astype(BF16)
    din_part = dot_rt(exp_dpre, up_expert)
    back = jnp.concatenate([exp_part[capacity:], din_part[capacity:]], axis=1).astype(BF16)
    back = other_core(back).astype(F32)
    exp_out = (exp_part[:capacity] + back[:, :width]).astype(BF16)
    exp_din = (din_part[:capacity] + back[:, width:]).astype(BF16)
    exp_rows_all = dot_lt(pick, exp_out)
    din_all = dot_lt(pick, exp_din)
    down_exp_part = dot_lt(exp_act, rows_grad).astype(BF16)
    up_exp_part = dot_lt(rows_in, exp_dpre).astype(BF16)

    dffn_part = dffn_part + din_all
    dcoeff = [
        jnp.sum(grad_output * dense_part, axis=1).reshape(n_exp, rows),
        jnp.sum(grad_output * exp_rows_all, axis=1).reshape(n_exp, rows),
    ]
    extra = jnp.concatenate([p for d in dcoeff for p in high_low(d)], axis=1)
    extra = jnp.pad(extra[:, None, :], ((0, 0), (0, 7), (0, width - 4 * rows)))
    payload = jnp.concatenate([dffn_part.astype(BF16).reshape(n_exp, rows, width), extra], axis=1)
    arrived = jnp.sum(swap(payload, "expert").astype(F32), axis=0)
    dffn = arrived[:rows]
    tail = arrived[rows]
    dcoeffs = jnp.stack(
        [tail[:rows] + tail[rows : 2 * rows], tail[2 * rows : 3 * rows] + tail[3 * rows : 4 * rows]],
        axis=1,
    )
    out_part = (coeffs[:, 0:1] * dense_part + coeffs[:, 1:2] * exp_rows_all).astype(BF16)
    out_sum = jnp.sum(swap(out_part.reshape(n_exp, rows, width), "expert").astype(F32), axis=0)

    def mine(values):
        return lax.dynamic_slice_in_dim(values, start, rows, 0)

    output = (mine(middle) + out_sum).astype(BF16)
    coeffs_own = mine(coeffs)
    dlogits = (
        coeffs_own * (dcoeffs - jnp.sum(coeffs_own * dcoeffs, axis=1, keepdims=True))
    ).astype(BF16)
    dlog = dlogits.astype(F32)
    dffn = dffn + dlog[:, 0:1] * mix_rows[0:1] + dlog[:, 1:2] * mix_rows[1:2]
    normed_own = mine(normed_two)
    dmiddle = out_grad.astype(F32) + norm_back(dffn, normed_own, mine(inverse_two), gain_two)
    gain_two_part = jnp.sum(dffn * normed_own, axis=0)
    mix_part = dot_lt(mine(ffn_input), dlogits)
    dmid_low = dmiddle.astype(BF16)
    out_weight_part = dot_lt(mine(attended), dmid_low).astype(BF16)
    dattended = dot_rt(dmid_low, out_matrix).astype(BF16)
    dattended = swap(
        dattended.reshape(rows, n_exp, head_cols).transpose(1, 0, 2), "expert"
    ).reshape(group, heads, HEAD_DIM)

    dprobs = jnp.einsum("qhd,khd->hqk", dattended, vals, preferred_element_type=F32)
    delta = jnp.sum(probs * dprobs, axis=-1, keepdims=True)
    dscores = (probs * (dprobs - delta)).astype(BF16)
    dquery = jnp.einsum("hqk,khd->qhd", dscores, keys, preferred_element_type=F32) * SCORE_SCALE
    dkeys = jnp.einsum("hqk,qhd->khd", dscores, query, preferred_element_type=F32) * SCORE_SCALE
    dvals = jnp.einsum("hqk,qhd->khd", probs_low, dattended, preferred_element_type=F32)
    dqkv = jnp.concatenate(
        [g.reshape(group, head_cols) for g in (dquery, dkeys, dvals)], axis=1
    ).astype(BF16)
    dattn_part = dot_rt(dqkv, qkv_matrix)
    gain_one_part = jnp.sum(dattn_part * normed_one, axis=0)
    qkv_part = dot_lt(attn_input, dqkv).astype(BF16)
    dattn = jnp.sum(
        swap(dattn_part.astype(BF16).reshape(n_exp, rows, width), "expert").astype(F32), axis=0
    )
    tokens_grad = (
        dmiddle + norm_back(dattn, mine(normed_one), mine(inverse_one), gain_one)
    ).astype(BF16)

    up_exp_sum = scatter_sum(up_exp_part, "chip")
    down_exp_sum = scatter_sum(down_exp_part, "chip")
    own_rows = jnp.where(core == 0, up_exp_sum[:exp_rows], up_exp_sum[exp_rows:])
    sent_rows = jnp.where(core == 0, up_exp_sum[exp_rows:], up_exp_sum[:exp_rows])
    got_rows = other_core(sent_rows)
    exp_up_grad = jnp.stack(
        [jnp.where(core == 0, own_rows, got_rows), jnp.where(core == 0, got_rows, own_rows)], axis=0
    ).reshape(n_core, exp_rows, n_chip, exp_cols)
    exp_up_grad = exp_up_grad.transpose(1, 2, 0, 3).reshape(1, exp_rows, n_dp * exp_cols)
    down_sum = scatter_sum(down_part, DP)
    up_sum = scatter_sum(up_part, DP)
    up_sum = swap(up_sum.reshape(n_exp, w_rows, dense_cols), "expert")
    up_sum = (
        up_sum.reshape(n_exp, w_rows, n_dp, dense_rows)
        .transpose(1, 2, 0, 3)
        .reshape(w_rows, n_exp * dense_cols)
    )
    out_weight_sum = scatter_sum(scatter_sum(out_weight_part, DP), "expert")
    small_part = jnp.concatenate([gain_one_part[:, None], gain_two_part[:, None], mix_part], axis=1)
    small_part = jnp.pad(small_part.astype(BF16), ((0, 0), (0, LANES - 4)))
    qkv_sum = scatter_sum(jnp.concatenate([qkv_part, small_part], axis=1), DP)
    qkv_sum = swap(qkv_sum.reshape(n_exp, w_rows, 3 * head_cols + LANES), "expert").astype(F32)
    small_sum = jnp.sum(qkv_sum[:, :, 3 * head_cols : 3 * head_cols + 4], axis=0)
    qkv_sum = (
        qkv_sum[:, :, : 3 * head_cols]
        .reshape(n_exp, w_rows, 3, head_cols)
        .transpose(1, 2, 0, 3)
        .reshape(w_rows, 3 * width)
    )
    return (
        output,
        tokens_grad,
        small_sum[:, 0],
        qkv_sum,
        out_weight_sum.astype(F32),
        small_sum[:, 1],
        small_sum[:, 2:4],
        up_sum.astype(F32),
        down_sum.astype(F32),
        exp_up_grad.astype(F32),
        down_exp_sum.astype(F32)[None],
    )


def solution(mesh):
    n_dp, n_exp = (mesh.shape["dp"], mesh.shape["expert"])
    fine = Mesh(mesh.devices.reshape(n_dp // 2, 2, n_exp), ("chip", "core", "expert"))
    every = ("chip", "core", "expert")
    by_rows = P(every, None)
    by_expert = P("expert", DP, None)
    return jax.shard_map(
        shards,
        mesh=fine,
        in_specs=(
            by_rows,
            P(every),
            by_rows,
            by_rows,
            P(every),
            by_rows,
            by_rows,
            by_rows,
            by_expert,
            by_expert,
            by_rows,
            P(DP, None),
            by_rows,
        ),
        out_specs=(
            by_rows,
            by_rows,
            P(every),
            by_rows,
            by_rows,
            P(every),
            by_rows,
            by_rows,
            by_rows,
            by_expert,
            by_expert,
        ),
        check_vma=False,
    )
```

```python
import jax
import jax.numpy as jnp
from jax import lax
from jax.experimental import pallas as pl
from jax.experimental.pallas import tpu as pltpu
from jax.sharding import Mesh
from jax.sharding import PartitionSpec as P

HEAD_DIM = 64
EPSILON = 1e-05
SCORE_SCALE = 0.125
MASK_VALUE = -1e30
F32 = jnp.float32
BF16 = jnp.bfloat16
DP = ("chip", "core")
LANES = 128
PAD = 16
TANH_SCALE = 0.7978845608028654
TANH_CUBE = 0.044715
VMEM_LIMIT = 60 << 20


def dot(left, right):
    return jnp.dot(left, right, preferred_element_type=F32)


def dot_rt(left, right):
    return lax.dot_general(left, right, (((1,), (1,)), ((), ())), preferred_element_type=F32)


def dot_lt(left, right):
    return lax.dot_general(left, right, (((0,), (0,)), ((), ())), preferred_element_type=F32)


def norm_parts(values):
    row_mean = jnp.mean(values, axis=-1, keepdims=True)
    centred = values - row_mean
    spread = jnp.mean(centred * centred, axis=-1, keepdims=True)
    inverse = lax.rsqrt(spread + EPSILON)
    return (centred * inverse, inverse)


def norm_back(grad, normed, inverse, gain):
    scaled = grad * gain
    return inverse * (
        scaled
        - jnp.mean(scaled, axis=-1, keepdims=True)
        - normed * jnp.mean(scaled * normed, axis=-1, keepdims=True)
    )


def after(values, *earlier):
    return lax.optimization_barrier((values,) + earlier)[0]


def swap(values, axis):
    return lax.all_to_all(values, axis, split_axis=0, concat_axis=0, tiled=True)


def share(values, axis):
    copies = lax.axis_size(axis)
    return swap(jnp.broadcast_to(values[None], (copies,) + values.shape), axis)


def other_core(values):
    return lax.ppermute(values, "core", [(0, 1), (1, 0)])


def by_core(core, first, second):
    return (jnp.where(core == 0, first, second), jnp.where(core == 0, second, first))


def flip(values, bit):
    chips = range(lax.axis_size("chip"))
    return lax.ppermute(values, "chip", [(i, i ^ bit) for i in chips])


def by_bit(bit, first, second):
    return by_core(lax.axis_index("chip") & bit, first, second)


def chip_bits():
    bits = []
    while 1 << len(bits) < lax.axis_size("chip"):
        bits.append(1 << len(bits))
    return bits


def spread(values, bits):
    shape, have = (values.shape, [])
    for bit in bits:
        at = len([b for b in have if b > bit])
        have.append(bit)
        values = jnp.stack(by_bit(bit, values, flip(values, bit)), axis=at)
    return values.reshape((-1,) + shape)


def gather_chip(arrays):
    joined = jnp.concatenate(arrays, axis=0)
    bits = chip_bits()
    cut = joined.shape[1] // 2 // LANES * LANES
    return [spread(joined[:, :cut], bits), spread(joined[:, cut:], bits[::-1])]


def join_cores(arrays, own, core):
    other = [other_core(part) for part in own]
    results, low = ([], 0)
    for array in arrays:
        high = low + array.shape[0]
        parts = [
            jnp.stack(by_core(core, mine[:, low:high], theirs[:, low:high]), axis=1)
            for mine, theirs in zip(own, other, strict=True)
        ]
        results.append(jnp.concatenate(parts, axis=-1).reshape(-1, array.shape[1]))
        low = high
    return results


def gather_small(values, axes, copies):
    count, cols = values.shape
    step = min(count, max(16, ((1 << 20) - 1) // (2 * copies * cols) // 16 * 16))
    return [
        lax.all_gather(values[k : k + step], axes, axis=0, tiled=True).reshape(copies, -1, cols)
        for k in range(0, count, step)
    ]


def sum_core(values, core):
    own, sent = by_core(core, values[:, 0], values[:, 1])
    return own.astype(F32) + other_core(sent).astype(F32)


def sum_chip(values, bits, gates):
    left = sorted(bits, reverse=True)
    values = values.reshape((2,) * len(left) + values.shape[1:])
    gates = list(gates) + [None] * len(bits)
    for bit, gate in zip(bits, gates, strict=False):
        at = left.index(bit)
        left.remove(bit)
        low, high = (lax.index_in_dim(values, k, at, False) for k in (0, 1))
        keep, send = by_bit(bit, low, high)
        got = flip(send.astype(BF16), bit)
        if gate is not None:
            got = after(got, gate)
        values = keep.astype(F32) + got.astype(F32)
    return values


def whole(shape):
    return pl.BlockSpec(shape, lambda *at: (0,) * len(shape), pipeline_mode=pl.Buffered(1))


def by_rows(tile, cols):
    return pl.BlockSpec((tile, cols), lambda t: (t, 0))


def shape_of(shape, kind):
    return jax.ShapeDtypeStruct(shape, kind)


def call(body, flops, out_shape, operands, in_specs, out_specs, grid=(1,), scratch=()):
    sizes = [o.size * o.dtype.itemsize for o in list(operands) + list(out_shape)]
    return pl.pallas_call(
        body,
        grid=grid,
        in_specs=in_specs,
        out_specs=out_specs,
        out_shape=out_shape,
        scratch_shapes=list(scratch),
        compiler_params=pltpu.CompilerParams(vmem_limit_bytes=VMEM_LIMIT),
        cost_estimate=pl.CostEstimate(flops=flops, bytes_accessed=sum(sizes), transcendentals=0),
    )(*operands)


def enter_body(x_ref, gain_ref, *refs):
    parts, (qkv_ref, attn_ref, w_ref) = (refs[:-3], refs[-3:])
    width, cols = w_ref.shape
    copies = parts[0].shape[0]
    matrix = jnp.concatenate([p[...] for p in parts], axis=1)[:, : width // copies]
    matrix = matrix.reshape(width, cols)
    w_ref[...] = matrix
    normed, unused = norm_parts(x_ref[...].astype(F32))
    attn_input = (normed * gain_ref[...]).astype(BF16)
    attn_ref[...] = attn_input
    qkv_ref[...] = dot(attn_input, matrix).astype(BF16)


def enter(inputs, gain, parts):
    group, width = inputs.shape
    cols = parts[0].shape[2]
    tile = min(512, group)
    return call(
        enter_body,
        2 * group * width * cols,
        [
            shape_of((group, cols), BF16),
            shape_of((group, width), BF16),
            shape_of((width, cols), BF16),
        ],
        [inputs, gain] + parts,
        [by_rows(tile, width), whole(gain.shape)] + [whole(p.shape) for p in parts],
        [by_rows(tile, cols), by_rows(tile, width), whole((width, cols))],
        grid=(group // tile,),
    )


def seen(split, query_axis, shape, first_query):
    query = first_query + lax.broadcasted_iota(jnp.int32, shape, query_axis)
    key = lax.broadcasted_iota(jnp.int32, shape, 1 - query_axis)
    return (query >= key) & ((query >= split) == (key >= split))


def attend_body(split_ref, q_ref, k_ref, v_ref, out_ref):
    tile, cols = q_ref.shape
    allowed = seen(split_ref[0], 0, (tile, k_ref.shape[0]), pl.program_id(1) * tile)
    for h in range(cols // HEAD_DIM):
        at = slice(h * HEAD_DIM, (h + 1) * HEAD_DIM)
        scores = dot_rt(q_ref[:, at], k_ref[:, at]) * SCORE_SCALE
        scores = jnp.where(allowed, scores, MASK_VALUE)
        weights = jnp.exp(scores - jnp.max(scores, axis=1, keepdims=True))
        probs = weights * (1.0 / jnp.sum(weights, axis=1, keepdims=True))
        out_ref[:, at] = dot(probs.astype(BF16), v_ref[:, at]).astype(BF16)


def attend_back_body(
    split_ref, q_ref, k_ref, v_ref, grad_ref, dq_ref, dk_ref, dv_ref, dk_sum, dv_sum
):
    tile, cols = q_ref.shape
    step = pl.program_id(1)
    allowed = seen(split_ref[0], 1, (k_ref.shape[0], tile), step * tile)
    for h in range(cols // HEAD_DIM):
        at = slice(h * HEAD_DIM, (h + 1) * HEAD_DIM)
        query, keys, vals, grad = (r[:, at] for r in (q_ref, k_ref, v_ref, grad_ref))
        scores = jnp.where(allowed, dot_rt(keys, query) * SCORE_SCALE, MASK_VALUE)
        weights = jnp.exp(scores - jnp.max(scores, axis=0, keepdims=True))
        probs = weights * (1.0 / jnp.sum(weights, axis=0, keepdims=True))
        dprobs = dot_rt(vals, grad)
        delta = jnp.sum(probs * dprobs, axis=0, keepdims=True)
        dscores = (probs * (dprobs - delta)).astype(BF16)
        dq_ref[:, at] = (dot_lt(dscores, keys) * SCORE_SCALE).astype(BF16)
        dk_new = dot(dscores, query) * SCORE_SCALE
        dv_new = dot(probs.astype(BF16), grad)

        @pl.when(step == 0)
        def first():
            dk_sum[:, at] = dk_new
            dv_sum[:, at] = dv_new

        @pl.when(step > 0)
        def later():
            dk_sum[:, at] += dk_new
            dv_sum[:, at] += dv_new

    @pl.when(step == pl.num_programs(1) - 1)
    def last():
        dk_ref[...] = dk_sum[...].astype(BF16)
        dv_ref[...] = dv_sum[...].astype(BF16)


def attention_parts(qkv, head_cols):
    group = qkv.shape[0]
    cols = min(LANES, head_cols)
    pairs = head_cols // cols
    tile = min(512, group)
    if head_cols % LANES == 0:
        operands, shift = ([qkv] * 3, pairs)
    else:
        operands = [qkv[:, k * head_cols : (k + 1) * head_cols] for k in range(3)]
        shift = 0
    specs = [
        pl.BlockSpec(memory_space=pltpu.SMEM),
        pl.BlockSpec((tile, cols), lambda p, t: (t, p)),
        pl.BlockSpec((group, cols), lambda p, t: (0, shift + p)),
        pl.BlockSpec((group, cols), lambda p, t: (0, 2 * shift + p)),
    ]
    by_tile = pl.BlockSpec((tile, cols), lambda p, t: (t, p))
    by_pair = pl.BlockSpec((group, cols), lambda p, t: (0, p))
    return (operands, specs, by_tile, by_pair, (pairs, group // tile), cols)


def attend(qkv, split, head_cols):
    group = qkv.shape[0]
    operands, specs, by_tile, unused, grid, cols = attention_parts(qkv, head_cols)
    return call(
        attend_body,
        4 * group * group * head_cols,
        [shape_of((group, head_cols), BF16)],
        [split] + operands,
        specs,
        [by_tile],
        grid=grid,
    )[0]


def attend_back(qkv, grad, split, head_cols):
    group = qkv.shape[0]
    operands, specs, by_tile, by_pair, grid, cols = attention_parts(qkv, head_cols)
    return call(
        attend_back_body,
        10 * group * group * head_cols,
        [shape_of((group, head_cols), BF16)] * 3,
        [split] + operands + [grad],
        specs + [by_tile],
        [by_tile, by_pair, by_pair],
        grid=grid,
        scratch=[pltpu.VMEM((group, cols), F32)] * 2,
    )


def middle_body(att_ref, x_ref, w_ref, gain_ref, mix_ref, middle_ref, ffn_ref, coeff_ref):
    n_exp, unused, head_cols = att_ref.shape
    middle = x_ref[...].astype(F32)
    for j in range(n_exp):
        middle = middle + dot(att_ref[j], w_ref[j * head_cols : (j + 1) * head_cols])
    middle_ref[...] = middle
    normed, unused = norm_parts(middle)
    ffn_input = (normed * gain_ref[...]).astype(BF16)
    ffn_ref[...] = ffn_input
    logits = dot_rt(ffn_input, mix_ref[...])
    first, second = (logits[:, 0:1], logits[:, 1:2])
    top = jnp.maximum(first, second)
    first, second = (jnp.exp(first - top), jnp.exp(second - top))
    coeff_ref[...] = jnp.concatenate([first, second], axis=1) / (first + second)


def to_middle(attended, inputs, matrix, gain, mix):
    n_exp, group, head_cols = attended.shape
    width = matrix.shape[0]
    tile = min(512, group)
    return call(
        middle_body,
        2 * group * width * width,
        [shape_of((group, width), F32), shape_of((group, width), BF16), shape_of((group, 2), F32)],
        [attended, inputs, matrix, gain, mix],
        [
            pl.BlockSpec((n_exp, tile, head_cols), lambda t: (0, t, 0)),
            by_rows(tile, width),
            whole(matrix.shape),
            whole(gain.shape),
            whole(mix.shape),
        ],
        [by_rows(tile, width), by_rows(tile, width), by_rows(tile, 2)],
        grid=(group // tile,),
    )


def pick_body(slot_ref, ffn_ref, grad_ref, coeff_ref, out_ref):
    capacity = out_ref.shape[1]
    shape = (capacity, ffn_ref.shape[0])
    pick = (lax.broadcasted_iota(jnp.int32, shape, 0) == slot_ref[...]).astype(F32).astype(BF16)
    dexpert = (coeff_ref[:, 1:2] * grad_ref[...].astype(F32)).astype(BF16)
    out_ref[0] = dot(pick, ffn_ref[...]).astype(BF16)
    out_ref[1] = dot(pick, dexpert).astype(BF16)


def pick_rows(slot, ffn_input, grad, coeffs, capacity):
    group, width = ffn_input.shape
    operands = [slot.reshape(1, group), ffn_input, grad, coeffs]
    return call(
        pick_body,
        4 * group * width * capacity,
        [shape_of((2, capacity, width), BF16)],
        operands,
        [whole(o.shape) for o in operands],
        [whole((2, capacity, width))],
    )[0]


def hidden_step(rows_in, rows_grad, up, down, out_sum, din_sum):
    pre = dot(rows_in, up)
    square = pre * pre
    bent = jnp.tanh(TANH_SCALE * pre * (1.0 + TANH_CUBE * square))
    half = 0.5 * (1.0 + bent)
    act = (pre * half).astype(BF16)
    slope = half + 0.5 * pre * (1.0 - bent * bent) * TANH_SCALE * (1.0 + 3.0 * TANH_CUBE * square)
    dpre = (slope * dot_rt(rows_grad, down)).astype(BF16)
    out_new = dot(act, down)
    din_new = dot_rt(dpre, up)

    @pl.when(pl.program_id(0) == 0)
    def first():
        out_sum[...] = out_new
        din_sum[...] = din_new

    @pl.when(pl.program_id(0) > 0)
    def later():
        out_sum[...] += out_new
        din_sum[...] += din_new

    return (dot_lt(rows_in, dpre).astype(BF16), dot_lt(act, rows_grad).astype(BF16))


def expert_body(
    own_ref, got_ref, up_ref, down_ref, keep_ref, send_ref, grads_ref, rows_in, rows_grad, outs, dins
):
    n_chip, pair_rows, cols = up_ref.shape
    capacity, width = own_ref.shape[1:]
    chunk = pl.program_id(0)

    @pl.when(chunk == 0)
    def begin():
        rows_in[:capacity] = own_ref[0]
        rows_in[capacity:] = got_ref[0]
        rows_grad[:capacity] = own_ref[1]
        rows_grad[capacity:] = got_ref[1]

    up = up_ref[...].reshape(width, cols)
    dup, ddown = hidden_step(rows_in[...], rows_grad[...], up, down_ref[0], outs, dins)
    per = width // cols
    low = pl.multiple_of(chunk // per * pair_rows, pair_rows)
    left = pl.multiple_of(chunk % per * cols, cols)
    grads_ref[:, pl.ds(low, pair_rows), pl.ds(left, cols)] = dup.reshape(n_chip, pair_rows, cols)
    grads_ref[pl.ds(chunk, 1), grads_ref.shape[1] - cols :, :] = ddown[None]

    @pl.when(chunk == pl.num_programs(0) - 1)
    def last():
        for k, total in enumerate((outs, dins)):
            keep_ref[k] = total[:capacity]
            send_ref[k] = total[capacity:].astype(BF16)


def expert_ffn(own, got, up, down, pair_rows):
    unused, capacity, width = own.shape
    n_chip, exp_cols, unused = down.shape
    grads = (n_chip, up.shape[1] + exp_cols, width)
    per = width // exp_cols
    count = 2 * capacity
    return call(
        expert_body,
        12 * count * width * n_chip * exp_cols,
        [shape_of(own.shape, F32), shape_of(own.shape, BF16), shape_of(grads, BF16)],
        [own, got, up, down],
        [
            whole(own.shape),
            whole(own.shape),
            pl.BlockSpec((n_chip, pair_rows, exp_cols), lambda c: (0, c // per, c % per)),
            pl.BlockSpec((1, exp_cols, width), lambda c: (c, 0, 0)),
        ],
        [whole(own.shape), whole(own.shape), whole(grads)],
        grid=(n_chip,),
        scratch=[pltpu.VMEM((count, width), BF16)] * 2 + [pltpu.VMEM((count, width), F32)] * 2,
    )


def dense_body(
    x_ref,
    g_ref,
    coeff_ref,
    slot_ref,
    own_ref,
    back_ref,
    up_ref,
    down_ref,
    pay_ref,
    out_ref,
    dup_ref,
    ddown_ref,
    ddense,
    outs,
    dins,
):
    group, width = x_ref.shape
    n_exp, padded, unused = pay_ref.shape
    rows = padded - PAD
    capacity = own_ref.shape[1]

    @pl.when(pl.program_id(0) == 0)
    def begin():
        ddense[...] = (coeff_ref[:, 0:1] * g_ref[...].astype(F32)).astype(BF16)

    dup_ref[...], ddown_ref[...] = hidden_step(
        x_ref[...], ddense[...], up_ref[...], down_ref[...], outs, dins
    )

    @pl.when(pl.program_id(0) == pl.num_programs(0) - 1)
    def last():
        exp_out, exp_din = (
            (own_ref[k] + back_ref[k].astype(F32)).astype(BF16) for k in range(2)
        )
        for j in range(n_exp):
            at = slice(j * rows, (j + 1) * rows)
            shape = (rows, capacity)
            place = (lax.broadcasted_iota(jnp.int32, shape, 1) == slot_ref[at]).astype(F32)
            place = place.astype(BF16)
            exp_rows = dot(place, exp_out)
            grad = g_ref[at].astype(F32)
            dense = outs[at]
            pay_ref[j, :rows] = (dins[at] + dot(place, exp_din)).astype(BF16)
            coeff = coeff_ref[at]
            out_ref[j] = (coeff[:, 0:1] * dense + coeff[:, 1:2] * exp_rows).astype(BF16)
            sums = [
                jnp.sum(grad * v, axis=1, keepdims=True) * jnp.ones((1, LANES), F32)
                for v in (dense, exp_rows)
            ]
            lines = [jnp.transpose(v)[:PAD] for v in sums]
            high = [v.astype(BF16).astype(F32) for v in lines]
            index = lax.broadcasted_iota(jnp.int32, (PAD, rows), 0)
            extra = jnp.where(
                index == 0,
                high[0],
                jnp.where(
                    index == 1,
                    lines[0] - high[0],
                    jnp.where(
                        index == 2,
                        high[1],
                        jnp.where(index == 3, lines[1] - high[1], 0.0),
                    ),
                ),
            )
            pay_ref[j, rows:] = jnp.concatenate(
                [extra, jnp.zeros((PAD, width - rows), F32)], axis=1
            ).astype(BF16)


def dense_ffn(ffn_input, grad, coeffs, slot, own, back, up, down, rows):
    group, width = ffn_input.shape
    hidden = down.shape[0]
    step = 2 * LANES
    n_exp = group // rows
    operands = [ffn_input, grad, coeffs, slot.reshape(group, 1), own, back]
    return call(
        dense_body,
        12 * group * width * hidden,
        [
            shape_of((n_exp, rows + PAD, width), BF16),
            shape_of((n_exp, rows, width), BF16),
            shape_of((width, hidden), BF16),
            shape_of((hidden, width), BF16),
        ],
        operands + [up, down],
        [whole(o.shape) for o in operands]
        + [
            pl.BlockSpec((width, step), lambda c: (0, c)),
            pl.BlockSpec((step, width), lambda c: (c, 0)),
        ],
        [
            whole((n_exp, rows + PAD, width)),
            whole((n_exp, rows, width)),
            pl.BlockSpec((width, step), lambda c: (0, c)),
            pl.BlockSpec((step, width), lambda c: (c, 0)),
        ],
        grid=(hidden // step,),
        scratch=[pltpu.VMEM((group, width), BF16)] + [pltpu.VMEM((group, width), F32)] * 2,
    )


def middle_back_body(
    pay_ref,
    middle_ref,
    coeff_ref,
    g_ref,
    gain_ref,
    mix_ref,
    w_ref,
    dmid_ref,
    low_ref,
    datt_ref,
    small_ref,
):
    rows, width = middle_ref.shape
    n_exp = pay_ref.shape[0]
    head_cols = datt_ref.shape[2]
    total = pay_ref[0].astype(F32)
    for j in range(1, n_exp):
        total = total + pay_ref[j].astype(F32)
    dffn = total[:rows]
    lines = jnp.concatenate([total[rows:, :rows], jnp.zeros((rows - PAD, rows), F32)], axis=0)
    lines = jnp.transpose(lines)
    dcoeff = [lines[:, 2 * k : 2 * k + 1] + lines[:, 2 * k + 1 : 2 * k + 2] for k in range(2)]
    coeff = [coeff_ref[:, k : k + 1] for k in range(2)]
    inner = coeff[0] * dcoeff[0] + coeff[1] * dcoeff[1]
    dlogit = [(c * (d - inner)).astype(BF16).astype(F32) for c, d in zip(coeff, dcoeff, strict=True)]
    mix = mix_ref[...].astype(F32)
    dffn = dffn + dlogit[0] * mix[0:1] + dlogit[1] * mix[1:2]
    normed, inverse = norm_parts(middle_ref[...])
    gain = gain_ref[...]
    dmiddle = g_ref[...].astype(F32) + norm_back(dffn, normed, inverse, gain)
    dmid_ref[...] = dmiddle
    low = dmiddle.astype(BF16)
    low_ref[...] = low
    datt = dot_rt(low, w_ref[...]).astype(BF16)
    for j in range(n_exp):
        datt_ref[j] = datt[:, j * head_cols : (j + 1) * head_cols]
    lane = lax.broadcasted_iota(jnp.int32, (rows, LANES), 1)
    pair = jnp.where(lane == 0, dlogit[0], jnp.where(lane == 1, dlogit[1], 0.0)).astype(BF16)
    dmix = dot_lt(pair, (normed * gain).astype(BF16))
    dgain = jnp.sum(dffn * normed, axis=0, keepdims=True)
    nothing = jnp.zeros((1, width), F32)
    small_ref[...] = jnp.concatenate([nothing, dgain, dmix[:2], jnp.zeros((4, width), F32)], axis=0)


def middle_back(arrived, middle, coeffs, grad, gain, mix, matrix, head_cols):
    rows, width = middle.shape
    n_exp = arrived.shape[0]
    operands = [arrived, middle, coeffs, grad, gain, mix, matrix]
    shapes = [
        shape_of((rows, width), F32),
        shape_of((rows, width), BF16),
        shape_of((n_exp, rows, head_cols), BF16),
        shape_of((8, width), F32),
    ]
    return call(
        middle_back_body,
        2 * rows * width * width,
        shapes,
        operands,
        [whole(o.shape) for o in operands],
        [whole(o.shape) for o in shapes],
    )


def out_grad_body(att_ref, low_ref, grad_ref):
    n_exp, unused, head_cols = att_ref.shape
    for j in range(n_exp):
        grad_ref[j * head_cols : (j + 1) * head_cols] = dot_lt(att_ref[j], low_ref[...]).astype(BF16)


def attn_input_back_body(dq_ref, dk_ref, dv_ref, w_ref, x_ref, dattn_ref, small_ref):
    grads = jnp.concatenate([dq_ref[...], dk_ref[...], dv_ref[...]], axis=1)
    dattn = dot_rt(grads, w_ref[...])
    dattn_ref[...] = dattn.astype(BF16)
    normed, unused = norm_parts(x_ref[...].astype(F32))
    dgain = jnp.sum(dattn * normed, axis=0, keepdims=True)
    dgain = jnp.concatenate([dgain, jnp.zeros((7, dgain.shape[1]), F32)], axis=0)

    @pl.when(pl.program_id(0) == 0)
    def first():
        small_ref[...] = dgain

    @pl.when(pl.program_id(0) > 0)
    def later():
        small_ref[...] += dgain


def attn_input_back(dparts, matrix, inputs):
    group, width = inputs.shape
    head_cols = dparts[0].shape[1]
    tile = min(512, group)
    return call(
        attn_input_back_body,
        6 * group * width * head_cols,
        [shape_of((group, width), BF16), shape_of((8, width), F32)],
        list(dparts) + [matrix, inputs],
        [by_rows(tile, head_cols)] * 3 + [whole(matrix.shape), by_rows(tile, width)],
        [by_rows(tile, width), whole((8, width))],
        grid=(group // tile,),
    )


def qkv_grad_body(x_ref, dq_ref, dk_ref, dv_ref, grad_ref):
    rows_in = x_ref[...]
    grad_ref[...] = jnp.concatenate(
        [dot_lt(rows_in, r[...]).astype(BF16) for r in (dq_ref, dk_ref, dv_ref)], axis=1
    )


def leave_body(pay_ref, x_ref, gain_ref, dmid_ref, out_ref):
    dattn = pay_ref[0].astype(F32)
    for j in range(1, pay_ref.shape[0]):
        dattn = dattn + pay_ref[j].astype(F32)
    normed, inverse = norm_parts(x_ref[...].astype(F32))
    out_ref[...] = (dmid_ref[...] + norm_back(dattn, normed, inverse, gain_ref[...])).astype(BF16)


def simple(body, flops, shape, operands):
    return call(
        body,
        flops,
        [shape],
        operands,
        [whole(o.shape) for o in operands],
        [whole(shape.shape)],
    )[0]


def shards(
    tokens,
    first_gain,
    w_qkv,
    w_out,
    second_gain,
    w_mix,
    w_up,
    w_down,
    expert_up,
    expert_down,
    expert_ids,
    doc_lengths,
    out_grad,
):
    rows, width = tokens.shape
    n_chip, n_core, n_exp = (lax.axis_size(a) for a in ("chip", "core", "expert"))
    n_dp = n_chip * n_core
    group = rows * n_exp
    head_cols = width // n_exp
    qkv_cols = 3 * head_cols
    w_rows = w_qkv.shape[0]
    block = n_exp * w_rows
    dense_rows = w_down.shape[0]
    dense_cols = n_dp * dense_rows
    exp_rows = expert_up.shape[1]
    exp_cols = expert_down.shape[1]
    ex = lax.axis_index("expert")
    core = lax.axis_index("core")
    capacity = n_exp * max(2, 5 * rows // (4 * n_exp))
    bits = chip_bits()

    exp_split = (
        expert_up[0]
        .reshape(exp_rows, n_chip, n_core, exp_cols)
        .transpose(2, 0, 1, 3)
        .reshape(n_core, exp_rows, n_chip * exp_cols)
    )
    own_half, sent_half = by_core(core, exp_split[0], exp_split[1])
    chip_up = jnp.concatenate(by_core(core, own_half, other_core(sent_half)), axis=0)
    pair_rows = n_core * exp_rows
    n_block = n_chip * exp_cols // width
    up_rows = n_block * pair_rows
    chip_up = chip_up.reshape(pair_rows, n_block, width).transpose(1, 0, 2)
    down_all = lax.all_gather(expert_down[0], "chip", axis=0, tiled=True)
    down_all = down_all.reshape(n_chip, exp_cols, width)

    qkv_blocks = w_qkv.reshape(w_rows, 3, n_exp, head_cols).transpose(2, 0, 1, 3)
    small = jnp.stack([first_gain, second_gain, w_mix[:, 0], w_mix[:, 1]])
    small = jnp.concatenate(
        [
            jnp.pad(small, ((0, 0), (0, qkv_cols - w_rows))),
            jnp.pad(expert_ids[:, 0].astype(BF16)[None], ((0, 3), (0, qkv_cols - rows))),
        ]
    )
    dealt = jnp.concatenate(
        [
            qkv_blocks.reshape(n_exp, w_rows, qkv_cols),
            jnp.broadcast_to(small[None], (n_exp, 8, qkv_cols)),
        ],
        axis=1,
    )
    out_rows = jnp.broadcast_to(jnp.pad(w_out, ((0, 8), (0, 0)))[None], (n_exp, w_rows + 8, width))
    dealt = swap(jnp.concatenate([dealt, out_rows], axis=2), "expert")
    out_own = dealt[:, :w_rows, qkv_cols:].reshape(block, width)
    chip_up = after(chip_up.reshape(up_rows, width), dealt)
    up_all = lax.all_gather(chip_up, "chip", axis=0, tiled=True)
    up_all = up_all.reshape(n_chip, up_rows, width)
    choice = after(dealt[:, w_rows + 4, :rows].astype(F32)).astype(jnp.int32).reshape(group)
    small = dealt[:, w_rows : w_rows + 4, :w_rows].transpose(1, 0, 2).reshape(4, block)
    first_own = jnp.concatenate(
        [
            dealt[:, :w_rows, :qkv_cols].reshape(block, qkv_cols),
            jnp.pad(small, ((0, 4), (0, qkv_cols - block))),
        ]
    )
    group_tokens = share(after(tokens, dealt), "expert")
    first_parts = gather_small(first_own, DP, n_dp)
    small = first_parts[-1][:, -8:-4, :block].transpose(1, 0, 2).reshape(4, width)
    gain_one = small[0:1].astype(F32)
    gain_two = small[1:2].astype(F32)
    mix_rows = jnp.pad(small[2:4], ((0, PAD - 2), (0, 0)))

    if dense_rows == block:
        joined = [after(out_own, first_parts), w_down]
    else:
        joined = [after(out_own, first_parts)]
    out_halves = gather_chip(joined)
    group_tokens = after(group_tokens, first_parts, gain_one)
    inputs = group_tokens.reshape(group, width)

    up_blocks = w_up.reshape(w_rows, n_dp, n_exp, dense_rows).transpose(2, 0, 1, 3)
    up_own = swap(
        after(up_blocks.reshape(n_exp, w_rows, dense_cols), group_tokens), "expert"
    )

    qkv, attn_input, qkv_matrix = enter(inputs, gain_one, first_parts)
    doc_split = doc_lengths[0, :1]
    attended_own = attend(qkv, doc_split, head_cols)
    attended_own, up_own, out_halves = lax.optimization_barrier((attended_own, up_own, out_halves))
    attended_all = share(attended_own, "expert")
    up_matrix = lax.all_gather(up_own.reshape(block, dense_cols), DP, axis=0, tiled=True)
    if dense_rows == block:
        out_matrix, down_matrix = join_cores(joined, out_halves, core)
    else:
        out_matrix = join_cores(joined, out_halves, core)[0]
        down_matrix = lax.all_gather(w_down, DP, axis=0, tiled=True)
    chosen = choice == ex
    slot = jnp.where(chosen, jnp.cumsum(chosen.astype(jnp.int32)) - 1, -1)
    attended_all = after(attended_all, out_matrix, slot)
    middle, ffn_input, coeffs = to_middle(attended_all, inputs, out_matrix, gain_two, mix_rows)

    grad_all = share(after(out_grad, attended_all), "expert").reshape(group, width)
    grad_all = after(grad_all, ffn_input)

    own_rows = pick_rows(slot, ffn_input, grad_all, coeffs, capacity)
    exp_keep, exp_send, exp_grads = expert_ffn(
        own_rows, other_core(own_rows), up_all, down_all, pair_rows
    )
    exp_back = other_core(exp_send)
    payload, out_part, up_part, down_part = dense_ffn(
        ffn_input, grad_all, coeffs, slot, exp_keep, exp_back, up_matrix, down_matrix, rows
    )
    exp_sum = lax.psum_scatter(
        exp_grads.reshape(-1, width), "chip", scatter_dimension=0, tiled=True
    )

    def mine(values, size=rows):
        return lax.dynamic_slice_in_dim(values, ex * size, size, 0)

    arrived = swap(payload, "expert")
    middle_own, coeffs_own = (mine(middle), mine(coeffs))
    att_own = lax.dynamic_slice_in_dim(attended_all, ex * rows, rows, 1)
    up_core = sum_core(up_part.reshape(n_chip, n_core, block, dense_cols), core)
    down_core = sum_core(down_part.reshape(n_chip, n_core, dense_rows, width), core)
    arrived = after(arrived, middle_own, coeffs_own, att_own, up_core, down_core)
    dmiddle, dmid_low, datt, small_two = middle_back(
        arrived, middle_own, coeffs_own, out_grad, gain_two, mix_rows, out_matrix, head_cols
    )
    dattended = swap(datt, "expert")
    out_sum = swap(after(out_part, dattended), "expert")
    dattended = dattended.reshape(group, head_cols)
    dparts = attend_back(qkv, dattended, doc_split, head_cols)
    dattn_part, small_one = attn_input_back(dparts, qkv_matrix, inputs)
    dattn_part, out_sum = lax.optimization_barrier((dattn_part, out_sum))
    dattn = swap(dattn_part.reshape(n_exp, rows, width), "expert")
    up_sum = sum_chip(up_core, bits, [out_sum, dattn])
    down_sum = sum_chip(down_core, bits[::-1], [out_sum, dattn])
    qkv_part = simple(
        qkv_grad_body,
        2 * group * width * qkv_cols,
        shape_of((width, qkv_cols), BF16),
        [after(attn_input, out_sum)] + list(dparts),
    )
    small_sum = (small_one + small_two).astype(BF16).reshape(8, n_dp, block).transpose(1, 0, 2)
    qkv_part = jnp.concatenate(
        [
            qkv_part.reshape(n_dp, block, qkv_cols),
            jnp.pad(small_sum, ((0, 0), (0, 0), (0, qkv_cols - block))),
        ],
        axis=1,
    )
    qkv_sum = sum_chip(
        sum_core(qkv_part.reshape(n_chip, n_core, block + 8, qkv_cols), core), bits[::-1], [dattn]
    )
    out_weight = simple(
        out_grad_body,
        2 * rows * width * width,
        shape_of((width, width), BF16),
        [after(att_own, out_sum), dmid_low],
    )
    out_core = sum_core(out_weight.reshape(n_chip, n_core, block, width), core)
    out_weight_sum = sum_chip(out_core, bits, [dattn])
    out_total = jnp.sum(out_sum.astype(F32), axis=0) + middle_own
    small_sum = qkv_sum[block : block + 4, :block].reshape(4, n_exp, w_rows).transpose(1, 0, 2)
    small_sum = jnp.pad(small_sum, ((0, 0), (0, 4), (0, qkv_cols - w_rows)))
    others = jnp.concatenate(
        [
            out_weight_sum.reshape(n_exp, w_rows, width),
            up_sum.reshape(n_exp, w_rows, dense_cols),
        ],
        axis=2,
    )
    tail = jnp.concatenate(
        [
            jnp.concatenate([qkv_sum[:block].reshape(n_exp, w_rows, qkv_cols), small_sum], axis=1),
            jnp.pad(others, ((0, 0), (0, 8), (0, 0))),
        ],
        axis=2,
    ).astype(BF16)
    tail = swap(after(tail, dattn), "expert")
    tokens_grad = simple(
        leave_body, 0, shape_of((rows, width), BF16), [dattn, tokens, gain_one, dmiddle]
    )

    exp_sum = after(exp_sum, dattn)
    up_exp_sum = exp_sum[:up_rows].reshape(n_block, n_core, exp_rows, width)
    own_exp, sent_exp = by_core(core, up_exp_sum[:, 0], up_exp_sum[:, 1])
    halves = jnp.stack(by_core(core, own_exp, other_core(sent_exp)))
    exp_up_grad = halves.transpose(2, 0, 1, 3).reshape(exp_rows, n_core, n_chip, exp_cols)
    exp_up_grad = exp_up_grad.transpose(0, 2, 1, 3).reshape(1, exp_rows, n_dp * exp_cols)
    exp_up_grad = exp_up_grad.astype(F32)
    exp_down_grad = exp_sum[up_rows:].astype(F32)[None]
    tail = after(tail, exp_up_grad, exp_down_grad, tokens_grad, out_total, down_sum)
    up_grad = tail[:, :w_rows, qkv_cols + width :].reshape(n_exp, w_rows, n_dp, dense_rows)
    up_grad = up_grad.transpose(1, 2, 0, 3)
    qkv_grad = tail[:, :w_rows, :qkv_cols].reshape(n_exp, w_rows, 3, head_cols)
    small_sum = jnp.sum(tail[:, w_rows : w_rows + 4, :w_rows].astype(F32), axis=0)
    return (
        out_total.astype(BF16),
        tokens_grad,
        small_sum[0],
        qkv_grad.transpose(1, 2, 0, 3).reshape(w_rows, 3 * width).astype(F32),
        jnp.sum(tail[:, :w_rows, qkv_cols : qkv_cols + width].astype(F32), axis=0),
        small_sum[1],
        small_sum[2:4].T,
        up_grad.reshape(w_rows, n_exp * dense_cols).astype(F32),
        down_sum,
        exp_up_grad,
        exp_down_grad,
    )


def solution(mesh):
    n_dp, n_exp = (mesh.shape["dp"], mesh.shape["expert"])
    fine = Mesh(mesh.devices.reshape(n_dp // 2, 2, n_exp), ("chip", "core", "expert"))
    every = ("chip", "core", "expert")
    rows = P(every, None)
    expert = P("expert", DP, None)
    return jax.shard_map(
        shards,
        mesh=fine,
        in_specs=(
            rows,
            P(every),
            rows,
            rows,
            P(every),
            rows,
            rows,
            rows,
            expert,
            expert,
            rows,
            P(DP, None),
            rows,
        ),
        out_specs=(
            rows,
            rows,
            P(every),
            rows,
            rows,
            P(every),
            rows,
            rows,
            rows,
            expert,
            expert,
        ),
        check_vma=False,
    )
```

```python
import jax
import jax.numpy as jnp
from jax import lax
from jax.experimental import pallas as pl
from jax.experimental.pallas import tpu as pltpu
from jax.sharding import Mesh
from jax.sharding import PartitionSpec as P

HEAD_DIM = 64
EPSILON = 1e-05
SCORE_SCALE = 0.125
MASK_VALUE = -1e30
F32 = jnp.float32
BF16 = jnp.bfloat16
DP = ("chip", "core")
LANES = 128
PAD = 16
TANH_SCALE = 0.7978845608028654
TANH_CUBE = 0.044715
VMEM_LIMIT = 60 << 20
FLOPS_US = 1.15e9
LAST = 0


def dot(left, right):
    return jnp.dot(left, right, preferred_element_type=F32)


def dot_rt(left, right):
    return lax.dot_general(left, right, (((1,), (1,)), ((), ())), preferred_element_type=F32)


def dot_lt(left, right):
    return lax.dot_general(left, right, (((0,), (0,)), ((), ())), preferred_element_type=F32)


def norm_parts(values):
    row_mean = jnp.mean(values, axis=-1, keepdims=True)
    centred = values - row_mean
    spread = jnp.mean(centred * centred, axis=-1, keepdims=True)
    inverse = lax.rsqrt(spread + EPSILON)
    return (centred * inverse, inverse)


def norm_back(grad, normed, inverse, gain):
    scaled = grad * gain
    return inverse * (
        scaled
        - jnp.mean(scaled, axis=-1, keepdims=True)
        - normed * jnp.mean(scaled * normed, axis=-1, keepdims=True)
    )


def after(values, *earlier):
    return lax.optimization_barrier((values,) + earlier)[0]


def swap(values, axis):
    return lax.all_to_all(values, axis, split_axis=0, concat_axis=0, tiled=True)


def share(values, axis):
    copies = lax.axis_size(axis)
    return swap(jnp.broadcast_to(values[None], (copies,) + values.shape), axis)


def turn(values, step):
    count = lax.axis_size("expert")
    return lax.ppermute(values, "expert", [(i, (i + step) % count) for i in range(count)])


def turn_all(pieces):
    return [pieces[0]] + [turn(piece, k) for k, piece in enumerate(pieces) if k]


def other_core(values):
    return lax.ppermute(values, "core", [(0, 1), (1, 0)])


def by_core(core, first, second):
    return (jnp.where(core == 0, first, second), jnp.where(core == 0, second, first))


def flip(values, bit):
    chips = range(lax.axis_size("chip"))
    return lax.ppermute(values, "chip", [(i, i ^ bit) for i in chips])


def by_bit(bit, first, second):
    return by_core(lax.axis_index("chip") & bit, first, second)


def chip_bits():
    bits = []
    while 1 << len(bits) < lax.axis_size("chip"):
        bits.append(1 << len(bits))
    return bits


def gather_small(values, axes, copies):
    count, cols = values.shape
    step = min(count, max(16, ((1 << 20) - 1) // (2 * copies * cols) // 16 * 16))
    return [
        lax.all_gather(values[k : k + step], axes, axis=0, tiled=True).reshape(copies, -1, cols)
        for k in range(0, count, step)
    ]


def sum_core(values, core):
    own, sent = by_core(core, values[:, 0], values[:, 1])
    return own.astype(F32) + other_core(sent).astype(F32)


class Fold:
    def __init__(self, pair):
        bits = chip_bits()
        self.orders = [list(bits), list(bits[::-1])]
        self.left = [sorted(bits, reverse=True) for k in range(2)]
        self.pair = [v.reshape((2,) * len(bits) + v.shape[1:]) for v in pair]

    def send(self):
        self.keeps, self.gots = ([], [])
        for k in range(2):
            bit = self.orders[k].pop(0)
            at = self.left[k].index(bit)
            self.left[k].remove(bit)
            low, high = (lax.index_in_dim(self.pair[k], side, at, False) for side in (0, 1))
            keep, sent = by_bit(bit, low, high)
            self.keeps.append(keep)
            self.gots.append(flip(sent.astype(BF16), bit))

    def meet(self, *others):
        gots = lax.optimization_barrier((*self.gots, *others))
        self.pair = [
            keep.astype(F32) + got.astype(F32)
            for keep, got in zip(self.keeps, gots[:2], strict=True)
        ]
        return gots[2:]


def whole(shape):
    return pl.BlockSpec(shape, lambda *at: (0,) * len(shape), pipeline_mode=pl.Buffered(1))


def by_rows(tile, cols):
    return pl.BlockSpec((tile, cols), lambda t: (t, 0))


def shape_of(shape, kind):
    return jax.ShapeDtypeStruct(shape, kind)


def call(body, weight, out_shape, operands, in_specs, out_specs, grid=(1,), scratch=()):
    return pl.pallas_call(
        body,
        grid=grid,
        in_specs=in_specs,
        out_specs=out_specs,
        out_shape=out_shape,
        scratch_shapes=list(scratch),
        compiler_params=pltpu.CompilerParams(vmem_limit_bytes=VMEM_LIMIT),
        cost_estimate=pl.CostEstimate(
            flops=int(weight * FLOPS_US), bytes_accessed=0, transcendentals=0
        ),
    )(*operands)


def enter_body(x_ref, gain_ref, *refs):
    parts, (qkv_ref, attn_ref, w_ref) = (refs[:-3], refs[-3:])
    width, cols = w_ref.shape
    copies = parts[0].shape[0]
    matrix = jnp.concatenate([p[...] for p in parts], axis=1)[:, : width // copies]
    matrix = matrix.reshape(width, cols)
    w_ref[...] = matrix
    normed, unused = norm_parts(x_ref[...].astype(F32))
    attn_input = (normed * gain_ref[...]).astype(BF16)
    attn_ref[...] = attn_input
    qkv_ref[...] = dot(attn_input, matrix).astype(BF16)


def enter(inputs, gain, parts):
    group, width = inputs.shape
    cols = parts[0].shape[2]
    tile = min(512, group)
    return call(
        enter_body,
        0,
        [
            shape_of((group, cols), BF16),
            shape_of((group, width), BF16),
            shape_of((width, cols), BF16),
        ],
        [inputs, gain] + parts,
        [by_rows(tile, width), whole(gain.shape)] + [whole(p.shape) for p in parts],
        [by_rows(tile, cols), by_rows(tile, width), whole((width, cols))],
        grid=(group // tile,),
    )


def seen(split, query_axis, shape, first_query):
    query = first_query + lax.broadcasted_iota(jnp.int32, shape, query_axis)
    key = lax.broadcasted_iota(jnp.int32, shape, 1 - query_axis)
    return (query >= key) & ((query >= split) == (key >= split))


def attend_body(split_ref, q_ref, k_ref, v_ref, out_ref):
    tile, cols = q_ref.shape
    allowed = seen(split_ref[0], 0, (tile, k_ref.shape[0]), pl.program_id(1) * tile)
    for h in range(cols // HEAD_DIM):
        at = slice(h * HEAD_DIM, (h + 1) * HEAD_DIM)
        scores = dot_rt(q_ref[:, at], k_ref[:, at]) * SCORE_SCALE
        scores = jnp.where(allowed, scores, MASK_VALUE)
        weights = jnp.exp(scores - jnp.max(scores, axis=1, keepdims=True))
        probs = weights * (1.0 / jnp.sum(weights, axis=1, keepdims=True))
        out_ref[:, at] = dot(probs.astype(BF16), v_ref[:, at]).astype(BF16)


def attend_back_body(
    split_ref, q_ref, k_ref, v_ref, grad_ref, dq_ref, dk_ref, dv_ref, dk_sum, dv_sum
):
    tile, cols = q_ref.shape
    step = pl.program_id(1)
    allowed = seen(split_ref[0], 1, (k_ref.shape[0], tile), step * tile)
    for h in range(cols // HEAD_DIM):
        at = slice(h * HEAD_DIM, (h + 1) * HEAD_DIM)
        query, keys, vals, grad = (r[:, at] for r in (q_ref, k_ref, v_ref, grad_ref))
        scores = jnp.where(allowed, dot_rt(keys, query) * SCORE_SCALE, MASK_VALUE)
        weights = jnp.exp(scores - jnp.max(scores, axis=0, keepdims=True))
        probs = weights * (1.0 / jnp.sum(weights, axis=0, keepdims=True))
        dprobs = dot_rt(vals, grad)
        delta = jnp.sum(probs * dprobs, axis=0, keepdims=True)
        dscores = (probs * (dprobs - delta)).astype(BF16)
        dq_ref[:, at] = (dot_lt(dscores, keys) * SCORE_SCALE).astype(BF16)
        dk_new = dot(dscores, query) * SCORE_SCALE
        dv_new = dot(probs.astype(BF16), grad)

        @pl.when(step == 0)
        def first():
            dk_sum[:, at] = dk_new
            dv_sum[:, at] = dv_new

        @pl.when(step > 0)
        def later():
            dk_sum[:, at] += dk_new
            dv_sum[:, at] += dv_new

    @pl.when(step == pl.num_programs(1) - 1)
    def last():
        dk_ref[...] = dk_sum[...].astype(BF16)
        dv_ref[...] = dv_sum[...].astype(BF16)


def attention_parts(qkv, head_cols):
    group = qkv.shape[0]
    cols = min(LANES, head_cols)
    pairs = head_cols // cols
    tile = min(512, group)
    if head_cols % LANES == 0:
        operands, shift = ([qkv] * 3, pairs)
    else:
        operands = [qkv[:, k * head_cols : (k + 1) * head_cols] for k in range(3)]
        shift = 0
    specs = [
        pl.BlockSpec(memory_space=pltpu.SMEM),
        pl.BlockSpec((tile, cols), lambda p, t: (t, p)),
        pl.BlockSpec((group, cols), lambda p, t: (0, shift + p)),
        pl.BlockSpec((group, cols), lambda p, t: (0, 2 * shift + p)),
    ]
    by_tile = pl.BlockSpec((tile, cols), lambda p, t: (t, p))
    by_pair = pl.BlockSpec((group, cols), lambda p, t: (0, p))
    return (operands, specs, by_tile, by_pair, (pairs, group // tile), cols)


def attend(qkv, split, head_cols):
    group = qkv.shape[0]
    operands, specs, by_tile, unused, grid, cols = attention_parts(qkv, head_cols)
    return call(
        attend_body,
        0,
        [shape_of((group, head_cols), BF16)],
        [split] + operands,
        specs,
        [by_tile],
        grid=grid,
    )[0]


def attend_back(qkv, grad, split, head_cols):
    group = qkv.shape[0]
    operands, specs, by_tile, by_pair, grid, cols = attention_parts(qkv, head_cols)
    return call(
        attend_back_body,
        20,
        [shape_of((group, head_cols), BF16)] * 3,
        [split] + operands + [grad],
        specs + [by_tile],
        [by_tile, by_pair, by_pair],
        grid=grid,
        scratch=[pltpu.VMEM((group, cols), F32)] * 2,
    )


def middle_body(att_ref, x_ref, w_ref, gain_ref, mix_ref, middle_ref, ffn_ref, coeff_ref):
    n_exp, unused, head_cols = att_ref.shape
    middle = x_ref[...].astype(F32)
    for j in range(n_exp):
        middle = middle + dot(att_ref[j], w_ref[j * head_cols : (j + 1) * head_cols])
    middle_ref[...] = middle
    normed, unused = norm_parts(middle)
    ffn_input = (normed * gain_ref[...]).astype(BF16)
    ffn_ref[...] = ffn_input
    logits = dot_rt(ffn_input, mix_ref[...])
    first, second = (logits[:, 0:1], logits[:, 1:2])
    top = jnp.maximum(first, second)
    first, second = (jnp.exp(first - top), jnp.exp(second - top))
    coeff_ref[...] = jnp.concatenate([first, second], axis=1) / (first + second)


def to_middle(attended, inputs, matrix, gain, mix):
    n_exp, group, head_cols = attended.shape
    width = matrix.shape[0]
    tile = min(512, group)
    return call(
        middle_body,
        0,
        [shape_of((group, width), F32), shape_of((group, width), BF16), shape_of((group, 2), F32)],
        [attended, inputs, matrix, gain, mix],
        [
            pl.BlockSpec((n_exp, tile, head_cols), lambda t: (0, t, 0)),
            by_rows(tile, width),
            whole(matrix.shape),
            whole(gain.shape),
            whole(mix.shape),
        ],
        [by_rows(tile, width), by_rows(tile, width), by_rows(tile, 2)],
        grid=(group // tile,),
    )


def pick_body(slot_ref, ffn_ref, grad_ref, coeff_ref, out_ref):
    capacity = out_ref.shape[1]
    shape = (capacity, ffn_ref.shape[0])
    pick = (lax.broadcasted_iota(jnp.int32, shape, 0) == slot_ref[...]).astype(F32).astype(BF16)
    dexpert = (coeff_ref[:, 1:2] * grad_ref[...].astype(F32)).astype(BF16)
    out_ref[0] = dot(pick, ffn_ref[...]).astype(BF16)
    out_ref[1] = dot(pick, dexpert).astype(BF16)


def pick_rows(slot, ffn_input, grad, coeffs, capacity):
    group, width = ffn_input.shape
    operands = [slot.reshape(1, group), ffn_input, grad, coeffs]
    return call(
        pick_body,
        0,
        [shape_of((2, capacity, width), BF16)],
        operands,
        [whole(o.shape) for o in operands],
        [whole((2, capacity, width))],
    )[0]


def bend(pre):
    square = pre * pre
    bent = jnp.tanh(TANH_SCALE * pre * (1.0 + TANH_CUBE * square))
    half = 0.5 * (1.0 + bent)
    slope = half + 0.5 * pre * (1.0 - bent * bent) * TANH_SCALE * (1.0 + 3.0 * TANH_CUBE * square)
    return ((pre * half).astype(BF16), slope)


def add_step(total, new):
    @pl.when(pl.program_id(0) == 0)
    def first():
        total[...] = new

    @pl.when(pl.program_id(0) > 0)
    def later():
        total[...] += new


def hidden_back(rows_in, rows_grad, up, down, din_sum):
    act, slope = bend(dot(rows_in, up))
    dpre = (slope * dot_rt(rows_grad, down)).astype(BF16)
    add_step(din_sum, dot_rt(dpre, up))
    return (act, dpre)


def fill_rows(own_ref, got_ref, rows_in, rows_grad):
    capacity = own_ref.shape[1]

    @pl.when(pl.program_id(0) == 0)
    def begin():
        rows_in[:capacity] = own_ref[0]
        rows_in[capacity:] = got_ref[0]
        rows_grad[:capacity] = own_ref[1]
        rows_grad[capacity:] = got_ref[1]


def expert_body(
    own_ref,
    got_ref,
    up_ref,
    down_ref,
    keep_ref,
    send_ref,
    act_ref,
    dpre_ref,
    rows_in,
    rows_grad,
    outs,
    dins,
):
    width = own_ref.shape[2]
    capacity = own_ref.shape[1]
    fill_rows(own_ref, got_ref, rows_in, rows_grad)
    up = up_ref[...].reshape(width, -1)
    act, dpre_ref[...] = hidden_back(rows_in[...], rows_grad[...], up, down_ref[0], dins)
    add_step(outs, dot(act, down_ref[0]))
    act_ref[...] = act

    @pl.when(pl.program_id(0) == pl.num_programs(0) - 1)
    def last():
        for k, total in enumerate((outs, dins)):
            keep_ref[k] = total[:capacity]
            send_ref[k] = total[capacity:].astype(BF16)


def expert_grad_body(own_ref, got_ref, act_ref, dpre_ref, grads_ref, turned, rows_grad):
    n_chip, packed, width = grads_ref.shape
    cols = act_ref.shape[1]
    per = width // cols
    pair_rows = width // n_chip
    chunk = pl.program_id(0)
    capacity = own_ref.shape[1]

    @pl.when(chunk == 0)
    def begin():
        rows_in = jnp.concatenate([own_ref[0], got_ref[0]], axis=0)
        turned[...] = jnp.transpose(rows_in.astype(F32)).astype(BF16)
        rows_grad[:capacity] = own_ref[1]
        rows_grad[capacity:] = got_ref[1]

    dup = dot(turned[...], dpre_ref[...]).astype(BF16)
    ddown = dot_lt(act_ref[...], rows_grad[...]).astype(BF16)
    low = pl.multiple_of(chunk // per * pair_rows, pair_rows)
    left = pl.multiple_of(chunk % per * cols, cols)
    grads_ref[:, pl.ds(low, pair_rows), pl.ds(left, cols)] = dup.reshape(n_chip, pair_rows, cols)
    grads_ref[pl.ds(chunk, 1), packed - cols :, :] = ddown[None]


def expert_ffn(own, got, up, down, pair_rows):
    unused, capacity, width = own.shape
    n_chip, exp_cols, unused = down.shape
    per = width // exp_cols
    count = 2 * capacity
    hidden = n_chip * exp_cols
    by_cols = pl.BlockSpec((count, exp_cols), lambda c: (0, c))
    return call(
        expert_body,
        0,
        [
            shape_of(own.shape, F32),
            shape_of(own.shape, BF16),
            shape_of((count, hidden), BF16),
            shape_of((count, hidden), BF16),
        ],
        [own, got, up, down],
        [
            whole(own.shape),
            whole(own.shape),
            pl.BlockSpec((n_chip, pair_rows, exp_cols), lambda c: (0, c // per, c % per)),
            pl.BlockSpec((1, exp_cols, width), lambda c: (c, 0, 0)),
        ],
        [whole(own.shape), whole(own.shape), by_cols, by_cols],
        grid=(n_chip,),
        scratch=[pltpu.VMEM((count, width), BF16)] * 2 + [pltpu.VMEM((count, width), F32)] * 2,
    )


def expert_grad(own, got, act, dpre, n_chip):
    unused, capacity, width = own.shape
    count, hidden = act.shape
    cols = hidden // n_chip
    packed = (n_chip, hidden // n_chip + hidden // n_chip, width)
    by_cols = pl.BlockSpec((count, cols), lambda c: (0, c))
    return call(
        expert_grad_body,
        0,
        [shape_of(packed, BF16)],
        [own, got, act, dpre],
        [whole(own.shape), whole(own.shape), by_cols, by_cols],
        [whole(packed)],
        grid=(n_chip,),
        scratch=[pltpu.VMEM((width, count), BF16), pltpu.VMEM((count, width), BF16)],
    )[0]


def dense_body(ex_ref, x_ref, g_ref, coeff_ref, up_ref, down_ref, *refs):
    outs, (pay_ref, act_ref, dpre_ref, ddense_ref, dense, dins) = (refs[:-6], refs[-6:])
    n_exp, padded, width = pay_ref.shape
    rows = padded - PAD

    @pl.when(pl.program_id(0) == 0)
    def begin():
        ddense_ref[...] = (coeff_ref[:, 0:1] * g_ref[...].astype(F32)).astype(BF16)

    up = up_ref[...].reshape(width, -1)
    down = down_ref[...].reshape(-1, width)
    act, dpre_ref[...] = hidden_back(x_ref[...], ddense_ref[...], up, down, dins)
    act_ref[...] = act
    add_step(dense, dot(act, down))

    @pl.when(pl.program_id(0) == pl.num_programs(0) - 1)
    def last():
        for k, out_ref in enumerate(outs):
            to = lax.rem(ex_ref[0] + k, len(outs))
            at = pl.ds(pl.multiple_of(to * rows, rows), rows)
            out_ref[...] = (coeff_ref[at, 0:1] * dense[at]).astype(BF16)
        for j in range(n_exp):
            at = slice(j * rows, (j + 1) * rows)
            pay_ref[j, :rows] = dins[at].astype(BF16)
            sums = jnp.sum(g_ref[at].astype(F32) * dense[at], axis=1, keepdims=True)
            line = jnp.transpose(sums * jnp.ones((1, LANES), F32))[:PAD]
            high = line.astype(BF16).astype(F32)
            index = lax.broadcasted_iota(jnp.int32, (PAD, rows), 0)
            extra = jnp.where(index == 0, high, jnp.where(index == 1, line - high, 0.0))
            pay_ref[j, rows:] = jnp.concatenate(
                [extra, jnp.zeros((PAD, width - rows), F32)], axis=1
            ).astype(BF16)


def dense_grad_body(x_ref, g_ref, act_ref, dpre_ref, dup_ref, ddown_ref):
    dup_ref[...] = dot_lt(x_ref[...], dpre_ref[...]).astype(BF16)
    ddown_ref[...] = dot_lt(act_ref[...], g_ref[...]).astype(BF16)


def dense_ffn(ex, ffn_input, grad, coeffs, weights, specs, hidden, rows):
    group, width = ffn_input.shape
    step = 2 * LANES
    count = group // rows
    operands = [ffn_input, grad, coeffs]
    padded = (count, rows + PAD, width)
    by_cols = pl.BlockSpec((group, step), lambda c: (0, c))
    return call(
        dense_body,
        0,
        [shape_of((rows, width), BF16)] * count
        + [shape_of(padded, BF16)]
        + [shape_of((group, hidden), BF16)] * 2
        + [shape_of((group, width), BF16)],
        [ex] + operands + weights,
        [pl.BlockSpec(memory_space=pltpu.SMEM)] + [whole(o.shape) for o in operands] + specs,
        [whole((rows, width))] * count
        + [whole(padded), by_cols, by_cols, whole((group, width))],
        grid=(hidden // step,),
        scratch=[pltpu.VMEM((group, width), F32)] * 2,
    )


def dense_grad(ffn_input, ddense, act, dpre):
    group, width = ffn_input.shape
    hidden = act.shape[1]
    step = 2 * LANES
    by_cols = pl.BlockSpec((group, step), lambda c: (0, c))
    return call(
        dense_grad_body,
        0,
        [shape_of((width, hidden), BF16), shape_of((hidden, width), BF16)],
        [ffn_input, ddense, act, dpre],
        [whole(ffn_input.shape), whole(ddense.shape), by_cols, by_cols],
        [
            pl.BlockSpec((width, step), lambda c: (0, c)),
            pl.BlockSpec((step, width), lambda c: (c, 0)),
        ],
        grid=(hidden // step,),
    )


def middle_back_body(
    ex_ref, pay_ref, slot_ref, middle_ref, coeff_ref, g_ref, gain_ref, mix_ref, w_ref, *refs
):
    rets, (dmid_ref, low_ref, datt_ref, small_ref, base_ref) = (refs[:-5], refs[-5:])
    rows, width = middle_ref.shape
    n_exp = pay_ref.shape[0]
    head_cols = datt_ref.shape[2]
    total = pay_ref[0].astype(F32)
    for j in range(1, n_exp):
        total = total + pay_ref[j].astype(F32)
    capacity = rets[0].shape[1]
    exp_rows, exp_din = (jnp.zeros((rows, width), F32) for k in range(2))
    index = lax.broadcasted_iota(jnp.int32, (rows, capacity), 1)
    for k, ret_ref in enumerate(rets):
        source = lax.rem(ex_ref[0] + n_exp - k, n_exp)
        place = (index + source * capacity == slot_ref[...]).astype(F32).astype(BF16)
        exp_rows = exp_rows + dot(place, ret_ref[0])
        exp_din = exp_din + dot(place, ret_ref[1])
    dffn = total[:rows] + exp_din
    lines = jnp.concatenate([total[rows:, :rows], jnp.zeros((rows - PAD, rows), F32)], axis=0)
    lines = jnp.transpose(lines)
    grad = g_ref[...].astype(F32)
    dcoeff = [lines[:, 0:1] + lines[:, 1:2], jnp.sum(grad * exp_rows, axis=1, keepdims=True)]
    coeff = [coeff_ref[:, k : k + 1] for k in range(2)]
    base_ref[...] = middle_ref[...] + coeff[1] * exp_rows
    inner = coeff[0] * dcoeff[0] + coeff[1] * dcoeff[1]
    dlogit = [(c * (d - inner)).astype(BF16).astype(F32) for c, d in zip(coeff, dcoeff, strict=True)]
    mix = mix_ref[...].astype(F32)
    dffn = dffn + dlogit[0] * mix[0:1] + dlogit[1] * mix[1:2]
    normed, inverse = norm_parts(middle_ref[...])
    gain = gain_ref[...]
    dmiddle = grad + norm_back(dffn, normed, inverse, gain)
    dmid_ref[...] = dmiddle
    low = dmiddle.astype(BF16)
    low_ref[...] = low
    datt = dot_rt(low, w_ref[...]).astype(BF16)
    for j in range(n_exp):
        datt_ref[j] = datt[:, j * head_cols : (j + 1) * head_cols]
    lane = lax.broadcasted_iota(jnp.int32, (rows, LANES), 1)
    pair = jnp.where(lane == 0, dlogit[0], jnp.where(lane == 1, dlogit[1], 0.0)).astype(BF16)
    dmix = dot_lt(pair, (normed * gain).astype(BF16))
    dgain = jnp.sum(dffn * normed, axis=0, keepdims=True)
    nothing = jnp.zeros((1, width), F32)
    small_ref[...] = jnp.concatenate([nothing, dgain, dmix[:2], jnp.zeros((4, width), F32)], axis=0)


def middle_back(ex, arrived, returned, slot, middle, coeffs, grad, gain, mix, matrix, head_cols):
    rows, width = middle.shape
    n_exp = arrived.shape[0]
    operands = [arrived, slot, middle, coeffs, grad, gain, mix, matrix] + list(returned)
    shapes = [
        shape_of((rows, width), F32),
        shape_of((rows, width), BF16),
        shape_of((n_exp, rows, head_cols), BF16),
        shape_of((8, width), F32),
        shape_of((rows, width), F32),
    ]
    return call(
        middle_back_body,
        0,
        shapes,
        [ex] + operands,
        [pl.BlockSpec(memory_space=pltpu.SMEM)] + [whole(o.shape) for o in operands],
        [whole(o.shape) for o in shapes],
    )


def out_grad_body(att_ref, low_ref, grad_ref):
    n_exp, unused, head_cols = att_ref.shape
    for j in range(n_exp):
        grad_ref[j * head_cols : (j + 1) * head_cols] = dot_lt(att_ref[j], low_ref[...]).astype(BF16)


def attn_input_back_body(ex_ref, dq_ref, dk_ref, dv_ref, w_ref, x_ref, *refs):
    pays, (small_ref,) = (refs[:-1], refs[-1:])
    rows, width = pays[0].shape
    dgain = jnp.zeros((1, width), F32)
    for k, pay_ref in enumerate(pays):
        to = lax.rem(ex_ref[0] + k, len(pays))
        at = pl.ds(pl.multiple_of(to * rows, rows), rows)
        grads = jnp.concatenate([dq_ref[at], dk_ref[at], dv_ref[at]], axis=1)
        dattn = dot_rt(grads, w_ref[...])
        pay_ref[...] = dattn.astype(BF16)
        normed, unused = norm_parts(x_ref[at].astype(F32))
        dgain = dgain + jnp.sum(dattn * normed, axis=0, keepdims=True)
    small_ref[...] = jnp.concatenate([dgain, jnp.zeros((7, width), F32)], axis=0)


def attn_input_back(ex, dparts, matrix, inputs, rows):
    group, width = inputs.shape
    head_cols = dparts[0].shape[1]
    operands = list(dparts) + [matrix, inputs]
    shapes = [shape_of((rows, width), BF16)] * (group // rows) + [shape_of((8, width), F32)]
    return call(
        attn_input_back_body,
        0,
        shapes,
        [ex] + operands,
        [pl.BlockSpec(memory_space=pltpu.SMEM)] + [whole(o.shape) for o in operands],
        [whole(o.shape) for o in shapes],
    )


def qkv_grad_body(x_ref, dq_ref, dk_ref, dv_ref, grad_ref):
    rows_in = x_ref[...]
    grad_ref[...] = jnp.concatenate(
        [dot_lt(rows_in, r[...]).astype(BF16) for r in (dq_ref, dk_ref, dv_ref)], axis=1
    )


def leave_body(x_ref, gain_ref, dmid_ref, *refs):
    pays, out_ref = (refs[:-1], refs[-1])
    dattn = pays[0][...].astype(F32)
    for pay_ref in pays[1:]:
        dattn = dattn + pay_ref[...].astype(F32)
    normed, inverse = norm_parts(x_ref[...].astype(F32))
    out_ref[...] = (dmid_ref[...] + norm_back(dattn, normed, inverse, gain_ref[...])).astype(BF16)


def simple(body, weight, shape, operands):
    return call(
        body,
        weight,
        [shape],
        operands,
        [whole(o.shape) for o in operands],
        [whole(shape.shape)],
    )[0]


def shards(
    tokens,
    first_gain,
    w_qkv,
    w_out,
    second_gain,
    w_mix,
    w_up,
    w_down,
    expert_up,
    expert_down,
    expert_ids,
    doc_lengths,
    out_grad,
):
    rows, width = tokens.shape
    n_chip, n_core, n_exp = (lax.axis_size(a) for a in ("chip", "core", "expert"))
    n_dp = n_chip * n_core
    group = rows * n_exp
    head_cols = width // n_exp
    qkv_cols = 3 * head_cols
    w_rows = w_qkv.shape[0]
    block = n_exp * w_rows
    dense_rows = w_down.shape[0]
    dense_cols = n_dp * dense_rows
    exp_rows = expert_up.shape[1]
    exp_cols = expert_down.shape[1]
    ex = lax.axis_index("expert")
    ex_line = jnp.full((1,), ex, jnp.int32)
    core = lax.axis_index("core")
    share_cap = max(2, 5 * rows // (4 * n_exp))
    capacity = n_exp * share_cap
    bits = chip_bits()

    exp_split = (
        expert_up[0]
        .reshape(exp_rows, n_chip, n_core, exp_cols)
        .transpose(2, 0, 1, 3)
        .reshape(n_core, exp_rows, n_chip * exp_cols)
    )
    own_half, sent_half = by_core(core, exp_split[0], exp_split[1])
    chip_up = jnp.concatenate(by_core(core, own_half, other_core(sent_half)), axis=0)
    pair_rows = n_core * exp_rows
    n_block = n_chip * exp_cols // width
    up_rows = n_block * pair_rows
    chip_up = chip_up.reshape(pair_rows, n_block, width).transpose(1, 0, 2)
    down_all = lax.all_gather(expert_down[0], "chip", axis=0, tiled=True)
    down_all = down_all.reshape(n_chip, exp_cols, width)

    qkv_blocks = w_qkv.reshape(w_rows, 3, n_exp, head_cols).transpose(2, 0, 1, 3)
    small = jnp.stack([first_gain, second_gain, w_mix[:, 0], w_mix[:, 1]])
    small = jnp.concatenate(
        [
            jnp.pad(small, ((0, w_rows - 4), (0, LANES - w_rows))),
            jnp.pad(expert_ids[:, 0].astype(BF16)[None], ((0, w_rows - 1), (0, LANES - rows))),
        ],
        axis=1,
    )
    up_blocks = w_up.reshape(w_rows, n_dp, n_exp, dense_rows).transpose(2, 0, 1, 3)
    others = jnp.concatenate([w_out, small], axis=1)
    dealt = swap(
        jnp.concatenate(
            [
                qkv_blocks.reshape(n_exp, w_rows, qkv_cols),
                up_blocks.reshape(n_exp, w_rows, dense_cols),
                jnp.broadcast_to(others[None], (n_exp,) + others.shape),
            ],
            axis=2,
        ),
        "expert",
    )
    at = [qkv_cols, qkv_cols + dense_cols, qkv_cols + dense_cols + width]
    up_own = dealt[:, :, at[0] : at[1]].reshape(block, dense_cols)
    out_own = dealt[:, :, at[1] : at[2]].reshape(block, width)
    choice = after(dealt[:, 0, at[2] + LANES : at[2] + LANES + rows].astype(F32)).astype(jnp.int32)
    small = dealt[:, :4, at[2] : at[2] + w_rows].transpose(1, 0, 2).reshape(4, block)
    first_own = jnp.concatenate(
        [
            dealt[:, :, :qkv_cols].reshape(block, qkv_cols),
            jnp.pad(small, ((0, 4), (0, qkv_cols - block))),
        ]
    )
    group_tokens = share(after(tokens, dealt), "expert")
    first_parts = gather_small(first_own, DP, n_dp)
    small = first_parts[-1][:, -8:-4, :block].transpose(1, 0, 2).reshape(4, width)
    gain_one = small[0:1].astype(F32)
    gain_two = small[1:2].astype(F32)
    mix_rows = jnp.pad(small[2:4], ((0, PAD - 2), (0, 0)))

    group_tokens = after(group_tokens, first_parts, gain_one)
    inputs = group_tokens.reshape(group, width)
    step = 2 * LANES
    if dense_cols == width and dense_rows == block:
        dense_pack = after(jnp.concatenate([out_own, up_own, w_down], axis=0), inputs, down_all)
        dense_all = lax.all_gather(dense_pack, DP, axis=0, tiled=True)
        dense_all = dense_all.reshape(n_dp, 3, block, width)
        out_matrix = dense_all[:, 0].reshape(width, width)
        up_matrix = down_matrix = dense_all
        up_spec = pl.BlockSpec((n_dp, 1, block, step), lambda c: (0, 1, 0, c))
        down_spec = pl.BlockSpec((step // block, 1, block, width), lambda c: (c, 2, 0, 0))
    else:
        out_matrix, up_matrix, down_matrix = (
            lax.all_gather(w, DP, axis=0, tiled=True) for w in (out_own, up_own, w_down)
        )
        up_spec = pl.BlockSpec((width, step), lambda c: (0, c))
        down_spec = pl.BlockSpec((step, width), lambda c: (c, 0))
    chip_up = after(chip_up.reshape(up_rows, width), inputs)
    up_all = lax.all_gather(chip_up, "chip", axis=0, tiled=True)
    up_all = up_all.reshape(n_chip, up_rows, width)

    grad_all = share(after(out_grad, inputs), "expert").reshape(group, width)

    qkv, attn_input, qkv_matrix = enter(inputs, gain_one, first_parts)
    doc_split = doc_lengths[0, :1]
    attended_own = attend(qkv, doc_split, head_cols)
    attended_own, grad_all = lax.optimization_barrier((attended_own, grad_all))
    attended_all = share(attended_own, "expert")
    same = (choice[:, :, None] == choice[:, None, :]).astype(jnp.int32)
    earlier = jnp.arange(rows)[None, None, :] < jnp.arange(rows)[None, :, None]
    rank = jnp.sum(jnp.where(earlier, same, 0), axis=2)
    first_slot = jnp.arange(n_exp, dtype=jnp.int32)[:, None] * share_cap
    slot = jnp.where(choice == ex, first_slot + rank, -1).reshape(1, group)
    slot_own = lax.dynamic_slice_in_dim(choice * share_cap + rank, ex, 1, 0).reshape(rows, 1)
    slot, slot_own = lax.optimization_barrier((slot, slot_own))
    attended_all = after(attended_all, out_matrix, slot)
    middle, ffn_input, coeffs = to_middle(attended_all, inputs, out_matrix, gain_two, mix_rows)


    weights, specs = ([up_matrix, down_matrix], [up_spec, down_spec])
    *out_parts, payload, dense_act, dense_dpre, ddense = dense_ffn(
        ex_line, ffn_input, grad_all, coeffs, weights, specs, dense_cols, rows
    )
    arrived = swap(payload, "expert")
    own_rows = pick_rows(slot, ffn_input, grad_all, coeffs, capacity)
    own_rows = after(own_rows, payload)
    up_part, down_part = dense_grad(ffn_input, ddense, dense_act, dense_dpre)
    got_rows, up_part, down_part = lax.optimization_barrier(
        (other_core(own_rows), up_part, down_part)
    )
    exp_keep, exp_send, exp_act, exp_dpre = expert_ffn(
        own_rows, got_rows, up_all, down_all, pair_rows
    )
    exp_back = other_core(exp_send)
    returned = []
    for k in range(n_exp):
        low = lax.rem(ex + k, n_exp) * share_cap
        piece = [lax.dynamic_slice_in_dim(v, low, share_cap, 1) for v in (exp_keep, exp_back)]
        returned.append((piece[0] + piece[1].astype(F32)).astype(BF16))
    exp_grads = expert_grad(own_rows, got_rows, exp_act, exp_dpre, n_chip)
    arrived, exp_grads, *returned = lax.optimization_barrier((arrived, exp_grads, *returned))
    returned = turn_all(returned)
    exp_sum = lax.psum_scatter(
        exp_grads.reshape(-1, width), "chip", scatter_dimension=0, tiled=True
    )

    def mine(values, size=rows):
        return lax.dynamic_slice_in_dim(values, ex * size, size, 0)

    middle_own, coeffs_own = (mine(middle), mine(coeffs))
    att_own = lax.dynamic_slice_in_dim(attended_all, ex * rows, rows, 1)
    up_core = sum_core(up_part.reshape(n_chip, n_core, block, dense_cols), core)
    down_core = sum_core(down_part.reshape(n_chip, n_core, dense_rows, width), core)
    returned[0] = after(returned[0], middle_own, coeffs_own, att_own, up_core, down_core)
    dense_fold = Fold((up_core, down_core))
    dense_fold.send()
    dmiddle, dmid_low, datt, small_two, out_base = middle_back(
        ex_line,
        arrived,
        returned,
        slot_own,
        middle_own,
        coeffs_own,
        out_grad,
        gain_two,
        mix_rows,
        out_matrix,
        head_cols,
    )
    dattended = swap(datt, "expert")
    dattended = dattended.reshape(group, head_cols)
    (dattended,) = dense_fold.meet(dattended)
    out_sums = turn_all([after(piece, dattended) for piece in out_parts])

    dparts = attend_back(qkv, dattended, doc_split, head_cols)
    *dattn_parts, small_one = attn_input_back(ex_line, dparts, qkv_matrix, inputs, rows)
    while dense_fold.orders[0]:
        dense_fold.send()
        met = dense_fold.meet(*dattn_parts, *out_sums)
        dattn_parts, out_sums = (met[:n_exp], met[n_exp:])
    up_sum, down_sum = dense_fold.pair
    dattn = turn_all(dattn_parts)
    out_weight = simple(
        out_grad_body,
        0,
        shape_of((width, width), BF16),
        [after(att_own, dparts[0]), dmid_low],
    )
    out_core = sum_core(out_weight.reshape(n_chip, n_core, block, width), core)
    qkv_part = simple(
        qkv_grad_body,
        20,
        shape_of((width, qkv_cols), BF16),
        [after(attn_input, dattn_parts[0])] + list(dparts),
    )
    small_sum = (small_one + small_two).astype(BF16).reshape(8, n_dp, block).transpose(1, 0, 2)
    qkv_part = jnp.concatenate(
        [
            qkv_part.reshape(n_dp, block, qkv_cols),
            jnp.pad(small_sum, ((0, 0), (0, 0), (0, qkv_cols - block))),
        ],
        axis=1,
    )
    qkv_core = sum_core(qkv_part.reshape(n_chip, n_core, block + 8, qkv_cols), core)
    fold = Fold((out_core, qkv_core))
    fold.send()
    dattn = fold.meet(*dattn)
    while fold.orders[0]:
        fold.send()
        fold.meet()
    out_weight_sum, qkv_sum = fold.pair
    out_total = out_base
    for piece in out_sums:
        out_total = out_total + piece.astype(F32)
    small_sum = qkv_sum[block : block + 4, :block].reshape(4, n_exp, w_rows).transpose(1, 0, 2)
    small_sum = jnp.pad(small_sum, ((0, 0), (0, w_rows - 4), (0, LANES - w_rows)))
    tail = jnp.concatenate(
        [
            qkv_sum[:block].reshape(n_exp, w_rows, qkv_cols),
            out_weight_sum.reshape(n_exp, w_rows, width),
            small_sum,
            up_sum.reshape(n_exp, w_rows, dense_cols),
        ],
        axis=2,
    ).astype(BF16)
    tail_sent = after(tail, *dattn)
    tail = swap(tail_sent, "expert")
    tokens_grad = simple(
        leave_body, LAST, shape_of((rows, width), BF16), [tokens, gain_one, dmiddle] + list(dattn)
    )

    exp_sum = after(exp_sum, tail_sent)
    up_exp_sum = exp_sum[:up_rows].reshape(n_block, n_core, exp_rows, width)
    own_exp, sent_exp = by_core(core, up_exp_sum[:, 0], up_exp_sum[:, 1])
    halves = jnp.stack(by_core(core, own_exp, other_core(sent_exp)))
    exp_up_grad = halves.transpose(2, 0, 1, 3).reshape(exp_rows, n_core, n_chip, exp_cols)
    exp_up_grad = exp_up_grad.transpose(0, 2, 1, 3).reshape(1, exp_rows, n_dp * exp_cols)
    exp_up_grad = exp_up_grad.astype(F32)
    exp_down_grad = exp_sum[up_rows:].astype(F32)[None]
    tail = after(tail, exp_up_grad, exp_down_grad, tokens_grad, out_total, down_sum)
    up_grad = tail[:, :, qkv_cols + width + LANES :].reshape(n_exp, w_rows, n_dp, dense_rows)
    up_grad = up_grad.transpose(1, 2, 0, 3).reshape(w_rows, n_exp * dense_cols).astype(F32)
    qkv_grad = tail[:, :, :qkv_cols].reshape(n_exp, w_rows, 3, head_cols)
    small_sum = jnp.sum(tail[:, :4, qkv_cols + width : qkv_cols + width + w_rows].astype(F32), axis=0)
    return (
        out_total.astype(BF16),
        tokens_grad,
        small_sum[0],
        qkv_grad.transpose(1, 2, 0, 3).reshape(w_rows, 3 * width).astype(F32),
        jnp.sum(tail[:, :, qkv_cols : qkv_cols + width].astype(F32), axis=0),
        small_sum[1],
        small_sum[2:4].T,
        up_grad,
        down_sum,
        exp_up_grad,
        exp_down_grad,
    )


def solution(mesh):
    n_dp, n_exp = (mesh.shape["dp"], mesh.shape["expert"])
    fine = Mesh(mesh.devices.reshape(n_dp // 2, 2, n_exp), ("chip", "core", "expert"))
    every = ("chip", "core", "expert")
    rows = P(every, None)
    expert = P("expert", DP, None)
    return jax.shard_map(
        shards,
        mesh=fine,
        in_specs=(
            rows,
            P(every),
            rows,
            rows,
            P(every),
            rows,
            rows,
            rows,
            expert,
            expert,
            rows,
            P(DP, None),
            rows,
        ),
        out_specs=(
            rows,
            rows,
            P(every),
            rows,
            rows,
            P(every),
            rows,
            rows,
            rows,
            expert,
            expert,
        ),
        check_vma=False,
    )
```

```python
import jax
import jax.numpy as jnp
from jax import lax
from jax.experimental import pallas as pl
from jax.experimental.pallas import tpu as pltpu
from jax.sharding import Mesh
from jax.sharding import PartitionSpec as P

HEAD_DIM = 64
EPSILON = 1e-05
SCORE_SCALE = 0.125
MASK_VALUE = -1e30
F32 = jnp.float32
BF16 = jnp.bfloat16
DP = ("chip", "core")
LANES = 128
PAD = 16
TANH_SCALE = 0.7978845608028654
TANH_CUBE = 0.044715
VMEM_LIMIT = 60 << 20
FLOPS_US = 1.15e9
LAST = 0


def dot(left, right):
    return jnp.dot(left, right, preferred_element_type=F32)


def dot_rt(left, right):
    return lax.dot_general(left, right, (((1,), (1,)), ((), ())), preferred_element_type=F32)


def dot_lt(left, right):
    return lax.dot_general(left, right, (((0,), (0,)), ((), ())), preferred_element_type=F32)


def norm_parts(values):
    row_mean = jnp.mean(values, axis=-1, keepdims=True)
    centred = values - row_mean
    spread = jnp.mean(centred * centred, axis=-1, keepdims=True)
    inverse = lax.rsqrt(spread + EPSILON)
    return (centred * inverse, inverse)


def norm_back(grad, normed, inverse, gain):
    scaled = grad * gain
    return inverse * (
        scaled
        - jnp.mean(scaled, axis=-1, keepdims=True)
        - normed * jnp.mean(scaled * normed, axis=-1, keepdims=True)
    )


def after(values, *earlier):
    return lax.optimization_barrier((values,) + earlier)[0]


def swap(values, axis):
    return lax.all_to_all(values, axis, split_axis=0, concat_axis=0, tiled=True)


def share(values, axis):
    copies = lax.axis_size(axis)
    return swap(jnp.broadcast_to(values[None], (copies,) + values.shape), axis)


def turn(values, step):
    count = lax.axis_size("expert")
    return lax.ppermute(values, "expert", [(i, (i + step) % count) for i in range(count)])


def turn_all(pieces):
    return [pieces[0]] + [turn(piece, k) for k, piece in enumerate(pieces) if k]


def other_core(values):
    return lax.ppermute(values, "core", [(0, 1), (1, 0)])


def by_core(core, first, second):
    return (jnp.where(core == 0, first, second), jnp.where(core == 0, second, first))


def flip(values, bit):
    chips = range(lax.axis_size("chip"))
    return lax.ppermute(values, "chip", [(i, i ^ bit) for i in chips])


def by_bit(bit, first, second):
    return by_core(lax.axis_index("chip") & bit, first, second)


def chip_bits():
    bits = []
    while 1 << len(bits) < lax.axis_size("chip"):
        bits.append(1 << len(bits))
    return bits


def gather_small(values, axes, copies):
    count, cols = values.shape
    step = min(count, max(16, ((1 << 20) - 1) // (2 * copies * cols) // 16 * 16))
    return [
        lax.all_gather(values[k : k + step], axes, axis=0, tiled=True).reshape(copies, -1, cols)
        for k in range(0, count, step)
    ]


def sum_core(values, core):
    own, sent = by_core(core, values[:, 0], values[:, 1])
    return own.astype(F32) + other_core(sent).astype(F32)


class Fold:
    def __init__(self, pair):
        bits = chip_bits()
        self.orders = [list(bits), list(bits[::-1])]
        self.left = [sorted(bits, reverse=True) for k in range(2)]
        self.pair = [v.reshape((2,) * len(bits) + v.shape[1:]) for v in pair]

    def send(self):
        self.keeps, self.gots = ([], [])
        for k in range(2):
            bit = self.orders[k].pop(0)
            at = self.left[k].index(bit)
            self.left[k].remove(bit)
            low, high = (lax.index_in_dim(self.pair[k], side, at, False) for side in (0, 1))
            keep, sent = by_bit(bit, low, high)
            self.keeps.append(keep)
            self.gots.append(flip(sent.astype(BF16), bit))

    def meet(self, *others):
        gots = lax.optimization_barrier((*self.gots, *others))
        self.pair = [
            keep.astype(F32) + got.astype(F32)
            for keep, got in zip(self.keeps, gots[:2], strict=True)
        ]
        return gots[2:]


def whole(shape):
    return pl.BlockSpec(shape, lambda *at: (0,) * len(shape), pipeline_mode=pl.Buffered(1))


def by_rows(tile, cols):
    return pl.BlockSpec((tile, cols), lambda t: (t, 0))


def shape_of(shape, kind):
    return jax.ShapeDtypeStruct(shape, kind)


def call(body, weight, out_shape, operands, in_specs, out_specs, grid=(1,), scratch=()):
    return pl.pallas_call(
        body,
        grid=grid,
        in_specs=in_specs,
        out_specs=out_specs,
        out_shape=out_shape,
        scratch_shapes=list(scratch),
        compiler_params=pltpu.CompilerParams(vmem_limit_bytes=VMEM_LIMIT),
        cost_estimate=pl.CostEstimate(
            flops=int(weight * FLOPS_US), bytes_accessed=0, transcendentals=0
        ),
    )(*operands)


def enter_body(x_ref, gain_ref, *refs):
    parts, (qkv_ref, attn_ref, w_ref) = (refs[:-3], refs[-3:])
    width, cols = w_ref.shape
    copies = parts[0].shape[0]
    matrix = jnp.concatenate([p[...] for p in parts], axis=1)[:, : width // copies]
    matrix = matrix.reshape(width, cols)
    w_ref[...] = matrix
    normed, unused = norm_parts(x_ref[...].astype(F32))
    attn_input = (normed * gain_ref[...]).astype(BF16)
    attn_ref[...] = attn_input
    qkv_ref[...] = dot(attn_input, matrix).astype(BF16)


def enter(inputs, gain, parts):
    group, width = inputs.shape
    cols = parts[0].shape[2]
    tile = min(512, group)
    return call(
        enter_body,
        0,
        [
            shape_of((group, cols), BF16),
            shape_of((group, width), BF16),
            shape_of((width, cols), BF16),
        ],
        [inputs, gain] + parts,
        [by_rows(tile, width), whole(gain.shape)] + [whole(p.shape) for p in parts],
        [by_rows(tile, cols), by_rows(tile, width), whole((width, cols))],
        grid=(group // tile,),
    )


def seen(split, query_axis, shape, first_query):
    query = first_query + lax.broadcasted_iota(jnp.int32, shape, query_axis)
    key = lax.broadcasted_iota(jnp.int32, shape, 1 - query_axis)
    return (query >= key) & ((query >= split) == (key >= split))


def attend_body(split_ref, q_ref, k_ref, v_ref, out_ref):
    tile, cols = q_ref.shape
    allowed = seen(split_ref[0], 0, (tile, k_ref.shape[0]), pl.program_id(1) * tile)
    for h in range(cols // HEAD_DIM):
        at = slice(h * HEAD_DIM, (h + 1) * HEAD_DIM)
        scores = dot_rt(q_ref[:, at], k_ref[:, at]) * SCORE_SCALE
        scores = jnp.where(allowed, scores, MASK_VALUE)
        weights = jnp.exp(scores - jnp.max(scores, axis=1, keepdims=True))
        probs = weights * (1.0 / jnp.sum(weights, axis=1, keepdims=True))
        result = dot(probs.astype(BF16), v_ref[:, at]).astype(BF16)
        for j in range(out_ref.shape[0]):
            out_ref[j, :, at] = result


def attend_back_body(
    split_ref, q_ref, k_ref, v_ref, grad_ref, dq_ref, dk_ref, dv_ref, dk_sum, dv_sum
):
    tile, cols = q_ref.shape
    step = pl.program_id(1)
    allowed = seen(split_ref[0], 1, (k_ref.shape[0], tile), step * tile)
    for h in range(cols // HEAD_DIM):
        at = slice(h * HEAD_DIM, (h + 1) * HEAD_DIM)
        query, keys, vals, grad = (r[:, at] for r in (q_ref, k_ref, v_ref, grad_ref))
        scores = jnp.where(allowed, dot_rt(keys, query) * SCORE_SCALE, MASK_VALUE)
        weights = jnp.exp(scores - jnp.max(scores, axis=0, keepdims=True))
        probs = weights * (1.0 / jnp.sum(weights, axis=0, keepdims=True))
        dprobs = dot_rt(vals, grad)
        delta = jnp.sum(probs * dprobs, axis=0, keepdims=True)
        dscores = (probs * (dprobs - delta)).astype(BF16)
        dq_ref[:, at] = (dot_lt(dscores, keys) * SCORE_SCALE).astype(BF16)
        dk_new = dot(dscores, query) * SCORE_SCALE
        dv_new = dot(probs.astype(BF16), grad)

        @pl.when(step == 0)
        def first():
            dk_sum[:, at] = dk_new
            dv_sum[:, at] = dv_new

        @pl.when(step > 0)
        def later():
            dk_sum[:, at] += dk_new
            dv_sum[:, at] += dv_new

    @pl.when(step == pl.num_programs(1) - 1)
    def last():
        dk_ref[...] = dk_sum[...].astype(BF16)
        dv_ref[...] = dv_sum[...].astype(BF16)


def attention_parts(qkv, head_cols):
    group = qkv.shape[0]
    cols = min(LANES, head_cols)
    pairs = head_cols // cols
    tile = min(512, group)
    if head_cols % LANES == 0:
        operands, shift = ([qkv] * 3, pairs)
    else:
        operands = [qkv[:, k * head_cols : (k + 1) * head_cols] for k in range(3)]
        shift = 0
    specs = [
        pl.BlockSpec(memory_space=pltpu.SMEM),
        pl.BlockSpec((tile, cols), lambda p, t: (t, p)),
        pl.BlockSpec((group, cols), lambda p, t: (0, shift + p)),
        pl.BlockSpec((group, cols), lambda p, t: (0, 2 * shift + p)),
    ]
    by_tile = pl.BlockSpec((tile, cols), lambda p, t: (t, p))
    by_pair = pl.BlockSpec((group, cols), lambda p, t: (0, p))
    return (operands, specs, by_tile, by_pair, (pairs, group // tile), cols)


def attend(qkv, split, head_cols, copies):
    group = qkv.shape[0]
    tile = min(512, group)
    operands, specs, unused, unused, grid, cols = attention_parts(qkv, head_cols)
    return call(
        attend_body,
        0,
        [shape_of((copies, group, head_cols), BF16)],
        [split] + operands,
        specs,
        [pl.BlockSpec((copies, tile, cols), lambda p, t: (0, t, p))],
        grid=grid,
    )[0]


def attend_back(qkv, grad, split, head_cols):
    group = qkv.shape[0]
    operands, specs, by_tile, by_pair, grid, cols = attention_parts(qkv, head_cols)
    return call(
        attend_back_body,
        20,
        [shape_of((group, head_cols), BF16)] * 3,
        [split] + operands + [grad],
        specs + [by_tile],
        [by_tile, by_pair, by_pair],
        grid=grid,
        scratch=[pltpu.VMEM((group, cols), F32)] * 2,
    )


def middle_body(att_ref, x_ref, w_ref, gain_ref, mix_ref, middle_ref, ffn_ref, coeff_ref):
    n_exp, unused, head_cols = att_ref.shape
    middle = x_ref[...].astype(F32)
    for j in range(n_exp):
        middle = middle + dot(att_ref[j], w_ref[j * head_cols : (j + 1) * head_cols])
    middle_ref[...] = middle
    normed, unused = norm_parts(middle)
    ffn_input = (normed * gain_ref[...]).astype(BF16)
    ffn_ref[...] = ffn_input
    logits = dot_rt(ffn_input, mix_ref[...])
    first, second = (logits[:, 0:1], logits[:, 1:2])
    top = jnp.maximum(first, second)
    first, second = (jnp.exp(first - top), jnp.exp(second - top))
    coeff_ref[...] = jnp.concatenate([first, second], axis=1) / (first + second)


def to_middle(attended, inputs, matrix, gain, mix):
    n_exp, group, head_cols = attended.shape
    width = matrix.shape[0]
    tile = min(512, group)
    return call(
        middle_body,
        0,
        [shape_of((group, width), F32), shape_of((group, width), BF16), shape_of((group, 2), F32)],
        [attended, inputs, matrix, gain, mix],
        [
            pl.BlockSpec((n_exp, tile, head_cols), lambda t: (0, t, 0)),
            by_rows(tile, width),
            whole(matrix.shape),
            whole(gain.shape),
            whole(mix.shape),
        ],
        [by_rows(tile, width), by_rows(tile, width), by_rows(tile, 2)],
        grid=(group // tile,),
    )


def pick_body(slot_ref, ffn_ref, grad_ref, coeff_ref, out_ref):
    capacity = out_ref.shape[1]
    shape = (capacity, ffn_ref.shape[0])
    pick = (lax.broadcasted_iota(jnp.int32, shape, 0) == slot_ref[...]).astype(F32).astype(BF16)
    dexpert = (coeff_ref[:, 1:2] * grad_ref[...].astype(F32)).astype(BF16)
    out_ref[0] = dot(pick, ffn_ref[...]).astype(BF16)
    out_ref[1] = dot(pick, dexpert).astype(BF16)


def pick_rows(slot, ffn_input, grad, coeffs, capacity):
    group, width = ffn_input.shape
    operands = [slot.reshape(1, group), ffn_input, grad, coeffs]
    return call(
        pick_body,
        0,
        [shape_of((2, capacity, width), BF16)],
        operands,
        [whole(o.shape) for o in operands],
        [whole((2, capacity, width))],
    )[0]


def bend(pre):
    square = pre * pre
    bent = jnp.tanh(TANH_SCALE * pre * (1.0 + TANH_CUBE * square))
    half = 0.5 * (1.0 + bent)
    slope = half + 0.5 * pre * (1.0 - bent * bent) * TANH_SCALE * (1.0 + 3.0 * TANH_CUBE * square)
    return ((pre * half).astype(BF16), slope)


def add_step(total, new):
    @pl.when(pl.program_id(0) == 0)
    def first():
        total[...] = new

    @pl.when(pl.program_id(0) > 0)
    def later():
        total[...] += new


def hidden_back(rows_in, rows_grad, up, down, din_sum):
    act, slope = bend(dot(rows_in, up))
    dpre = (slope * dot_rt(rows_grad, down)).astype(BF16)
    add_step(din_sum, dot_rt(dpre, up))
    return (act, dpre)


def fill_rows(own_ref, got_ref, rows_in, rows_grad):
    capacity = own_ref.shape[1]

    @pl.when(pl.program_id(0) == 0)
    def begin():
        rows_in[:capacity] = own_ref[0]
        rows_in[capacity:] = got_ref[0]
        rows_grad[:capacity] = own_ref[1]
        rows_grad[capacity:] = got_ref[1]


def expert_body(
    own_ref,
    got_ref,
    up_ref,
    down_ref,
    keep_ref,
    send_ref,
    act_ref,
    dpre_ref,
    rows_in,
    rows_grad,
    outs,
    dins,
):
    width = own_ref.shape[2]
    capacity = own_ref.shape[1]
    fill_rows(own_ref, got_ref, rows_in, rows_grad)
    up = up_ref[...].reshape(width, -1)
    act, dpre_ref[...] = hidden_back(rows_in[...], rows_grad[...], up, down_ref[0], dins)
    add_step(outs, dot(act, down_ref[0]))
    act_ref[...] = act

    @pl.when(pl.program_id(0) == pl.num_programs(0) - 1)
    def last():
        for k, total in enumerate((outs, dins)):
            keep_ref[k] = total[:capacity]
            send_ref[k] = total[capacity:].astype(BF16)


def expert_grad_body(own_x, got_x, own_g, got_g, act_ref, dpre_ref, grads_ref):
    width = grads_ref.shape[2]
    rows_in = jnp.concatenate([own_x[0], got_x[0]], axis=0)
    rows_grad = jnp.concatenate([own_g[0], got_g[0]], axis=0)
    dup = dot_lt(rows_in, dpre_ref[...]).astype(BF16)
    pair_rows, hidden = dup.shape
    up_rows = hidden // width * pair_rows
    for k in range(hidden // width):
        at = slice(k * pair_rows, (k + 1) * pair_rows)
        grads_ref[0, at] = dup[:, k * width : (k + 1) * width]
    grads_ref[0, up_rows:] = dot_lt(act_ref[...], rows_grad).astype(BF16)


def expert_ffn(own, got, up, down, pair_rows):
    unused, capacity, width = own.shape
    n_chip, exp_cols, unused = down.shape
    per = width // exp_cols
    count = 2 * capacity
    hidden = n_chip * exp_cols
    by_cols = pl.BlockSpec((count, exp_cols), lambda c: (0, c))
    return call(
        expert_body,
        0,
        [
            shape_of(own.shape, F32),
            shape_of(own.shape, BF16),
            shape_of((count, hidden), BF16),
            shape_of((count, hidden), BF16),
        ],
        [own, got, up, down],
        [
            whole(own.shape),
            whole(own.shape),
            pl.BlockSpec((n_chip, pair_rows, exp_cols), lambda c: (0, c // per, c % per)),
            pl.BlockSpec((1, exp_cols, width), lambda c: (c, 0, 0)),
        ],
        [whole(own.shape), whole(own.shape), by_cols, by_cols],
        grid=(n_chip,),
        scratch=[pltpu.VMEM((count, width), BF16)] * 2 + [pltpu.VMEM((count, width), F32)] * 2,
    )


def expert_grad(own, got, act, dpre, n_chip):
    unused, capacity, width = own.shape
    count, hidden = act.shape
    cols, pair_rows = (hidden // n_chip, width // n_chip)
    rows = hidden // width * pair_rows + cols
    by_width = pl.BlockSpec((1, capacity, pair_rows), lambda d: (0, 0, d))
    second = pl.BlockSpec((1, capacity, width), lambda d: (1, 0, 0))
    return call(
        expert_grad_body,
        0,
        [shape_of((n_chip, rows, width), BF16)],
        [own, got, own, got, act, dpre],
        [
            by_width,
            by_width,
            second,
            second,
            pl.BlockSpec((count, cols), lambda d: (0, d)),
            whole(dpre.shape),
        ],
        [pl.BlockSpec((1, rows, width), lambda d: (d, 0, 0))],
        grid=(n_chip,),
    )[0]


def dense_body(ex_ref, x_ref, g_ref, coeff_ref, up_ref, down_ref, *refs):
    outs, (pay_ref, act_ref, dpre_ref, ddense_ref, dense, dins) = (refs[:-6], refs[-6:])
    n_exp, padded, width = pay_ref.shape
    rows = padded - PAD

    @pl.when(pl.program_id(0) == 0)
    def begin():
        ddense_ref[...] = (coeff_ref[:, 0:1] * g_ref[...].astype(F32)).astype(BF16)

    up = up_ref[...].reshape(width, -1)
    down = down_ref[...].reshape(-1, width)
    act, dpre_ref[...] = hidden_back(x_ref[...], ddense_ref[...], up, down, dins)
    act_ref[...] = act
    add_step(dense, dot(act, down))

    @pl.when(pl.program_id(0) == pl.num_programs(0) - 1)
    def last():
        for k, out_ref in enumerate(outs):
            to = lax.rem(ex_ref[0] + k, len(outs))
            at = pl.ds(pl.multiple_of(to * rows, rows), rows)
            out_ref[...] = (coeff_ref[at, 0:1] * dense[at]).astype(BF16)
        for j in range(n_exp):
            at = slice(j * rows, (j + 1) * rows)
            pay_ref[j, :rows] = dins[at].astype(BF16)
            sums = jnp.sum(g_ref[at].astype(F32) * dense[at], axis=1, keepdims=True)
            line = jnp.transpose(sums * jnp.ones((1, LANES), F32))[:PAD]
            high = line.astype(BF16).astype(F32)
            index = lax.broadcasted_iota(jnp.int32, (PAD, rows), 0)
            extra = jnp.where(index == 0, high, jnp.where(index == 1, line - high, 0.0))
            pay_ref[j, rows:] = jnp.concatenate(
                [extra, jnp.zeros((PAD, width - rows), F32)], axis=1
            ).astype(BF16)


def dense_grad_body(x_ref, g_ref, act_ref, dpre_ref, dup_ref, ddown_ref):
    dup_ref[...] = dot_lt(x_ref[...], dpre_ref[...]).astype(BF16)
    ddown_ref[...] = dot_lt(act_ref[...], g_ref[...]).astype(BF16)


def dense_ffn(ex, ffn_input, grad, coeffs, weights, specs, hidden, rows):
    group, width = ffn_input.shape
    step = 2 * LANES
    count = group // rows
    operands = [ffn_input, grad, coeffs]
    padded = (count, rows + PAD, width)
    by_cols = pl.BlockSpec((group, step), lambda c: (0, c))
    return call(
        dense_body,
        0,
        [shape_of((rows, width), BF16)] * count
        + [shape_of(padded, BF16)]
        + [shape_of((group, hidden), BF16)] * 2
        + [shape_of((group, width), BF16)],
        [ex] + operands + weights,
        [pl.BlockSpec(memory_space=pltpu.SMEM)] + [whole(o.shape) for o in operands] + specs,
        [whole((rows, width))] * count
        + [whole(padded), by_cols, by_cols, whole((group, width))],
        grid=(hidden // step,),
        scratch=[pltpu.VMEM((group, width), F32)] * 2,
    )


def dense_pack_body(core_ref, x_ref, g_ref, act_ref, dpre_ref, keep_ref, send_ref):
    n_chip, unused, block, unused = keep_ref.shape
    step = act_ref.shape[1]
    chunk = pl.program_id(0)
    left = pl.ds(pl.multiple_of(chunk * step, step), step)
    first_core = core_ref[0] == 0
    dup = dot_lt(x_ref[...], dpre_ref[...]).astype(BF16).reshape(n_chip, 2, block, step)
    ddown = dot_lt(act_ref[...], g_ref[...]).astype(BF16)
    keep_ref[:, 0, :, left] = jnp.where(first_core, dup[:, 0], dup[:, 1])
    send_ref[:, 0, :, left] = jnp.where(first_core, dup[:, 1], dup[:, 0])
    at = pl.ds(chunk, 1)
    keep_ref[at, 1] = jnp.where(first_core, ddown[:block], ddown[block:])[None]
    send_ref[at, 1] = jnp.where(first_core, ddown[block:], ddown[:block])[None]


def dense_split(core, ffn_input, ddense, act, dpre, shape):
    group, step = (ffn_input.shape[0], 2 * LANES)
    by_cols = pl.BlockSpec((group, step), lambda c: (0, c))
    return call(
        dense_pack_body,
        0,
        [shape_of(shape, BF16)] * 2,
        [core, ffn_input, ddense, act, dpre],
        [
            pl.BlockSpec(memory_space=pltpu.SMEM),
            whole(ffn_input.shape),
            whole(ddense.shape),
            by_cols,
            by_cols,
        ],
        [whole(shape)] * 2,
        grid=(act.shape[1] // step,),
    )


def dense_grad(ffn_input, ddense, act, dpre):
    group, width = ffn_input.shape
    hidden = act.shape[1]
    step = 2 * LANES
    by_cols = pl.BlockSpec((group, step), lambda c: (0, c))
    return call(
        dense_grad_body,
        0,
        [shape_of((width, hidden), BF16), shape_of((hidden, width), BF16)],
        [ffn_input, ddense, act, dpre],
        [whole(ffn_input.shape), whole(ddense.shape), by_cols, by_cols],
        [
            pl.BlockSpec((width, step), lambda c: (0, c)),
            pl.BlockSpec((step, width), lambda c: (c, 0)),
        ],
        grid=(hidden // step,),
    )


def middle_back_body(
    ex_ref, pay_ref, slot_ref, middle_ref, coeff_ref, g_ref, gain_ref, mix_ref, w_ref, *refs
):
    rets, (dmid_ref, low_ref, datt_ref, small_ref, base_ref) = (refs[:-5], refs[-5:])
    rows, width = middle_ref.shape
    n_exp = pay_ref.shape[0]
    head_cols = datt_ref.shape[2]
    total = pay_ref[0].astype(F32)
    for j in range(1, n_exp):
        total = total + pay_ref[j].astype(F32)
    capacity = rets[0].shape[1]
    exp_rows, exp_din = (jnp.zeros((rows, width), F32) for k in range(2))
    index = lax.broadcasted_iota(jnp.int32, (rows, capacity), 1)
    for k, ret_ref in enumerate(rets):
        source = lax.rem(ex_ref[0] + n_exp - k, n_exp)
        place = (index + source * capacity == slot_ref[...]).astype(F32).astype(BF16)
        exp_rows = exp_rows + dot(place, ret_ref[0])
        exp_din = exp_din + dot(place, ret_ref[1])
    dffn = total[:rows] + exp_din
    lines = jnp.concatenate([total[rows:, :rows], jnp.zeros((rows - PAD, rows), F32)], axis=0)
    lines = jnp.transpose(lines)
    grad = g_ref[...].astype(F32)
    dcoeff = [lines[:, 0:1] + lines[:, 1:2], jnp.sum(grad * exp_rows, axis=1, keepdims=True)]
    coeff = [coeff_ref[:, k : k + 1] for k in range(2)]
    base_ref[...] = middle_ref[...] + coeff[1] * exp_rows
    inner = coeff[0] * dcoeff[0] + coeff[1] * dcoeff[1]
    dlogit = [(c * (d - inner)).astype(BF16).astype(F32) for c, d in zip(coeff, dcoeff, strict=True)]
    mix = mix_ref[...].astype(F32)
    dffn = dffn + dlogit[0] * mix[0:1] + dlogit[1] * mix[1:2]
    normed, inverse = norm_parts(middle_ref[...])
    gain = gain_ref[...]
    dmiddle = grad + norm_back(dffn, normed, inverse, gain)
    dmid_ref[...] = dmiddle
    low = dmiddle.astype(BF16)
    low_ref[...] = low
    datt = dot_rt(low, w_ref[...]).astype(BF16)
    for j in range(n_exp):
        datt_ref[j] = datt[:, j * head_cols : (j + 1) * head_cols]
    lane = lax.broadcasted_iota(jnp.int32, (rows, LANES), 1)
    pair = jnp.where(lane == 0, dlogit[0], jnp.where(lane == 1, dlogit[1], 0.0)).astype(BF16)
    dmix = dot_lt(pair, (normed * gain).astype(BF16))
    dgain = jnp.sum(dffn * normed, axis=0, keepdims=True)
    nothing = jnp.zeros((1, width), F32)
    small_ref[...] = jnp.concatenate([nothing, dgain, dmix[:2], jnp.zeros((4, width), F32)], axis=0)


def middle_back(ex, arrived, returned, slot, middle, coeffs, grad, gain, mix, matrix, head_cols):
    rows, width = middle.shape
    n_exp = arrived.shape[0]
    operands = [arrived, slot, middle, coeffs, grad, gain, mix, matrix] + list(returned)
    shapes = [
        shape_of((rows, width), F32),
        shape_of((rows, width), BF16),
        shape_of((n_exp, rows, head_cols), BF16),
        shape_of((8, width), F32),
        shape_of((rows, width), F32),
    ]
    return call(
        middle_back_body,
        0,
        shapes,
        [ex] + operands,
        [pl.BlockSpec(memory_space=pltpu.SMEM)] + [whole(o.shape) for o in operands],
        [whole(o.shape) for o in shapes],
    )


def split_cores(core_ref, grads, keep_ref, send_ref):
    n_chip, block = keep_ref.shape[:2]
    grads = grads.reshape(n_chip, 2, block, grads.shape[-1])
    first_core = core_ref[0] == 0
    keep_ref[...] = jnp.where(first_core, grads[:, 0], grads[:, 1])
    send_ref[...] = jnp.where(first_core, grads[:, 1], grads[:, 0])


def out_grad_body(core_ref, att_ref, low_ref, keep_ref, send_ref):
    grads = [dot_lt(att_ref[j], low_ref[...]).astype(BF16) for j in range(att_ref.shape[0])]
    split_cores(core_ref, jnp.concatenate(grads, axis=0), keep_ref, send_ref)


def attn_input_back_body(ex_ref, dq_ref, dk_ref, dv_ref, w_ref, *pays):
    rows = pays[0].shape[0]
    for k, pay_ref in enumerate(pays):
        to = lax.rem(ex_ref[0] + k, len(pays))
        at = pl.ds(pl.multiple_of(to * rows, rows), rows)
        grads = jnp.concatenate([dq_ref[at], dk_ref[at], dv_ref[at]], axis=1)
        pay_ref[...] = dot_rt(grads, w_ref[...]).astype(BF16)


def qkv_grad_body(
    core_ref, x_ref, w_ref, gain_ref, small_ref, dq_ref, dk_ref, dv_ref, keep_ref, send_ref
):
    n_chip, padded, cols = keep_ref.shape
    block = padded - PAD
    rows_in = x_ref[...]
    grads = jnp.concatenate([dot_lt(rows_in, r[...]) for r in (dq_ref, dk_ref, dv_ref)], axis=1)
    width = grads.shape[0]
    dgain = jnp.sum(grads * w_ref[...].astype(F32), axis=1, keepdims=True)
    dgain = jnp.transpose(dgain * jnp.ones((1, LANES), F32))[:8] / gain_ref[...]
    index = lax.broadcasted_iota(jnp.int32, (8, width), 0)
    small = jnp.where(index == 0, dgain, small_ref[...])
    small = jnp.concatenate([small, jnp.zeros((PAD - 8, width), F32)], axis=0)
    first_core = core_ref[0] == 0
    for chip in range(n_chip):
        pair = []
        for core in range(2):
            low = (2 * chip + core) * block
            edge = jnp.concatenate(
                [small[:, low : low + block], jnp.zeros((PAD, cols - block), F32)], axis=1
            )
            pair.append(jnp.concatenate([grads[low : low + block], edge], axis=0).astype(BF16))
        keep_ref[chip] = jnp.where(first_core, pair[0], pair[1])
        send_ref[chip] = jnp.where(first_core, pair[1], pair[0])


def scalar_call(body, shapes, scalar, operands, weight=0):
    return call(
        body,
        weight,
        shapes,
        [scalar] + operands,
        [pl.BlockSpec(memory_space=pltpu.SMEM)] + [whole(o.shape) for o in operands],
        [whole(o.shape) for o in shapes],
    )


def expert_end_body(core_ref, own_ref, got_ref, down_ref, up_out, down_out):
    cols = down_ref.shape[0]
    per = own_ref.shape[2] // cols
    first_core = core_ref[0] == 0
    for k in range(own_ref.shape[0] * per):
        at = slice(k % per * cols, (k % per + 1) * cols)
        mine, theirs = (r[k // per, :, at].astype(F32) for r in (own_ref, got_ref))
        low = 2 * k * cols
        up_out[:, low : low + cols] = jnp.where(first_core, mine, theirs)
        up_out[:, low + cols : low + 2 * cols] = jnp.where(first_core, theirs, mine)
    down_out[...] = down_ref[...].astype(F32)


def leave_body(x_ref, gain_ref, dmid_ref, *refs):
    pays, out_ref = (refs[:-1], refs[-1])
    dattn = pays[0][...].astype(F32)
    for pay_ref in pays[1:]:
        dattn = dattn + pay_ref[...].astype(F32)
    normed, inverse = norm_parts(x_ref[...].astype(F32))
    out_ref[...] = (dmid_ref[...] + norm_back(dattn, normed, inverse, gain_ref[...])).astype(BF16)


def simple(body, weight, shape, operands):
    return call(
        body,
        weight,
        [shape],
        operands,
        [whole(o.shape) for o in operands],
        [whole(shape.shape)],
    )[0]


def shards(
    tokens,
    first_gain,
    w_qkv,
    w_out,
    second_gain,
    w_mix,
    w_up,
    w_down,
    expert_up,
    expert_down,
    expert_ids,
    doc_lengths,
    out_grad,
):
    rows, width = tokens.shape
    n_chip, n_core, n_exp = (lax.axis_size(a) for a in ("chip", "core", "expert"))
    n_dp = n_chip * n_core
    group = rows * n_exp
    head_cols = width // n_exp
    qkv_cols = 3 * head_cols
    w_rows = w_qkv.shape[0]
    block = n_exp * w_rows
    dense_rows = w_down.shape[0]
    dense_cols = n_dp * dense_rows
    exp_rows = expert_up.shape[1]
    exp_cols = expert_down.shape[1]
    ex = lax.axis_index("expert")
    ex_line = jnp.full((1,), ex, jnp.int32)
    core = lax.axis_index("core")
    core_line = jnp.full((1,), core, jnp.int32)
    share_cap = max(2, 5 * rows // (4 * n_exp))
    capacity = n_exp * share_cap
    bits = chip_bits()

    exp_split = (
        expert_up[0]
        .reshape(exp_rows, n_chip, n_core, exp_cols)
        .transpose(2, 0, 1, 3)
        .reshape(n_core, exp_rows, n_chip * exp_cols)
    )
    own_half, sent_half = by_core(core, exp_split[0], exp_split[1])
    chip_up = jnp.concatenate(by_core(core, own_half, other_core(sent_half)), axis=0)
    pair_rows = n_core * exp_rows
    n_block = n_chip * exp_cols // width
    up_rows = n_block * pair_rows
    chip_up = chip_up.reshape(pair_rows, n_block, width).transpose(1, 0, 2)
    down_all = lax.all_gather(expert_down[0], "chip", axis=0, tiled=True)
    down_all = down_all.reshape(n_chip, exp_cols, width)

    qkv_blocks = w_qkv.reshape(w_rows, 3, n_exp, head_cols).transpose(2, 0, 1, 3)
    small = jnp.stack([first_gain, second_gain, w_mix[:, 0], w_mix[:, 1]])
    small = jnp.concatenate(
        [
            jnp.pad(small, ((0, w_rows - 4), (0, LANES - w_rows))),
            jnp.pad(expert_ids[:, 0].astype(BF16)[None], ((0, w_rows - 1), (0, LANES - rows))),
        ],
        axis=1,
    )
    up_blocks = w_up.reshape(w_rows, n_dp, n_exp, dense_rows).transpose(2, 0, 1, 3)
    others = jnp.concatenate([w_out, small], axis=1)
    dealt = swap(
        jnp.concatenate(
            [
                qkv_blocks.reshape(n_exp, w_rows, qkv_cols),
                up_blocks.reshape(n_exp, w_rows, dense_cols),
                jnp.broadcast_to(others[None], (n_exp,) + others.shape),
            ],
            axis=2,
        ),
        "expert",
    )
    at = [qkv_cols, qkv_cols + dense_cols, qkv_cols + dense_cols + width]
    up_own = dealt[:, :, at[0] : at[1]].reshape(block, dense_cols)
    out_own = dealt[:, :, at[1] : at[2]].reshape(block, width)
    chip_up = chip_up.reshape(up_rows, width)
    grad_copies = jnp.broadcast_to(out_grad[None], (n_exp,) + out_grad.shape)
    dealt, chip_up, grad_copies = lax.optimization_barrier((dealt, chip_up, grad_copies))
    choice = after(dealt[:, 0, at[2] + LANES : at[2] + LANES + rows].astype(F32)).astype(jnp.int32)
    small = dealt[:, :4, at[2] : at[2] + w_rows].transpose(1, 0, 2).reshape(4, block)
    first_own = jnp.concatenate(
        [
            dealt[:, :, :qkv_cols].reshape(block, qkv_cols),
            jnp.pad(small, ((0, 4), (0, qkv_cols - block))),
        ]
    )
    group_tokens = share(after(tokens, dealt), "expert")
    first_parts = gather_small(first_own, DP, n_dp)
    small = first_parts[-1][:, -8:-4, :block].transpose(1, 0, 2).reshape(4, width)
    gain_one = small[0:1].astype(F32)
    gain_two = small[1:2].astype(F32)
    mix_rows = jnp.pad(small[2:4], ((0, PAD - 2), (0, 0)))

    group_tokens = after(group_tokens, first_parts, gain_one)
    inputs = group_tokens.reshape(group, width)
    step = 2 * LANES
    if dense_cols == width and dense_rows == block:
        dense_pack = after(jnp.concatenate([out_own, up_own, w_down], axis=0), inputs, down_all)
        dense_all = lax.all_gather(dense_pack, DP, axis=0, tiled=True)
        dense_all = dense_all.reshape(n_dp, 3, block, width)
        out_matrix = dense_all[:, 0].reshape(width, width)
        up_matrix = down_matrix = dense_all
        up_spec = pl.BlockSpec((n_dp, 1, block, step), lambda c: (0, 1, 0, c))
        down_spec = pl.BlockSpec((step // block, 1, block, width), lambda c: (c, 2, 0, 0))
    else:
        out_matrix, up_matrix, down_matrix = (
            lax.all_gather(w, DP, axis=0, tiled=True) for w in (out_own, up_own, w_down)
        )
        up_spec = pl.BlockSpec((width, step), lambda c: (0, c))
        down_spec = pl.BlockSpec((step, width), lambda c: (c, 0))
    chip_up = after(chip_up, inputs)
    up_all = lax.all_gather(chip_up, "chip", axis=0, tiled=True)
    up_all = up_all.reshape(n_chip, up_rows, width)

    grad_all = swap(after(grad_copies, inputs), "expert").reshape(group, width)

    qkv, attn_input, qkv_matrix = enter(inputs, gain_one, first_parts)
    doc_split = doc_lengths[0, :1]
    attended_own = attend(qkv, doc_split, head_cols, n_exp)
    attended_own, grad_all = lax.optimization_barrier((attended_own, grad_all))
    attended_all = swap(attended_own, "expert")
    same = (choice[:, :, None] == choice[:, None, :]).astype(jnp.int32)
    earlier = jnp.arange(rows)[None, None, :] < jnp.arange(rows)[None, :, None]
    rank = jnp.sum(jnp.where(earlier, same, 0), axis=2)
    first_slot = jnp.arange(n_exp, dtype=jnp.int32)[:, None] * share_cap
    slot = jnp.where(choice == ex, first_slot + rank, -1).reshape(1, group)
    slot_own = lax.dynamic_slice_in_dim(choice * share_cap + rank, ex, 1, 0).reshape(rows, 1)
    slot, slot_own = lax.optimization_barrier((slot, slot_own))
    attended_all = after(attended_all, out_matrix, slot)
    middle, ffn_input, coeffs = to_middle(attended_all, inputs, out_matrix, gain_two, mix_rows)


    weights, specs = ([up_matrix, down_matrix], [up_spec, down_spec])
    *out_parts, payload, dense_act, dense_dpre, ddense = dense_ffn(
        ex_line, ffn_input, grad_all, coeffs, weights, specs, dense_cols, rows
    )
    arrived = swap(payload, "expert")
    own_rows = pick_rows(after(slot, payload), ffn_input, grad_all, coeffs, capacity)
    joined = dense_cols == width and dense_rows == block and step == 2 * block
    if joined:
        shape = (n_chip, 2, block, width)
        grads = dense_split(core_line, ffn_input, ddense, dense_act, dense_dpre, shape)
    else:
        grads = dense_grad(ffn_input, ddense, dense_act, dense_dpre)
    got_rows, *grads = lax.optimization_barrier((other_core(own_rows), *grads))
    if joined:
        dense_core = (grads[0].astype(F32) + other_core(grads[1]).astype(F32)).astype(BF16)
        got_rows, dense_core = lax.optimization_barrier((got_rows, dense_core))
        dense_sum = lax.psum_scatter(
            dense_core.reshape(-1, width), "chip", scatter_dimension=0, tiled=True
        )
        up_sum, down_sum = (dense_sum[:block], dense_sum[block:])
    else:
        up_sum, down_sum = (
            lax.psum_scatter(g, DP, scatter_dimension=0, tiled=True) for g in grads
        )
    exp_keep, exp_send, exp_act, exp_dpre = expert_ffn(
        own_rows, got_rows, up_all, down_all, pair_rows
    )
    exp_back = other_core(exp_send)
    returned = []
    for k in range(n_exp):
        low = lax.rem(ex + k, n_exp) * share_cap
        piece = [lax.dynamic_slice_in_dim(v, low, share_cap, 1) for v in (exp_keep, exp_back)]
        returned.append((piece[0] + piece[1].astype(F32)).astype(BF16))
    exp_grads = expert_grad(
        own_rows, got_rows, exp_act, exp_dpre, n_chip
    )
    arrived, exp_grads, *returned = lax.optimization_barrier((arrived, exp_grads, *returned))
    returned = turn_all(returned)
    exp_sum = lax.psum_scatter(
        exp_grads.reshape(-1, width), "chip", scatter_dimension=0, tiled=True
    )

    def mine(values, size=rows):
        return lax.dynamic_slice_in_dim(values, ex * size, size, 0)

    middle_own, coeffs_own = (mine(middle), mine(coeffs))
    att_own = lax.dynamic_slice_in_dim(attended_all, ex * rows, rows, 1)
    returned[0] = after(returned[0], middle_own, coeffs_own, att_own)
    dmiddle, dmid_low, datt, small_two, out_base = middle_back(
        ex_line,
        arrived,
        returned,
        slot_own,
        middle_own,
        coeffs_own,
        out_grad,
        gain_two,
        mix_rows,
        out_matrix,
        head_cols,
    )
    dattended = swap(datt, "expert")
    out_keep, out_send = scalar_call(
        out_grad_body,
        [shape_of((n_chip, block, width), BF16)] * 2,
        core_line,
        [att_own, dmid_low],
    )
    dattended, out_keep, out_send = lax.optimization_barrier((dattended, out_keep, out_send))
    dattended = dattended.reshape(group, head_cols)
    out_sums = turn_all([after(piece, dattended) for piece in out_parts])

    dparts = attend_back(qkv, dattended, doc_split, head_cols)
    qkv_shape = shape_of((n_chip, block + PAD, qkv_cols), BF16)
    qkv_keep, qkv_send = scalar_call(
        qkv_grad_body,
        [qkv_shape] * 2,
        core_line,
        [attn_input, qkv_matrix, gain_one, small_two] + list(dparts),
    )
    dparts = [after(dparts[0], qkv_keep), dparts[1], dparts[2]]
    dattn_parts = scalar_call(
        attn_input_back_body,
        [shape_of((rows, width), BF16)] * n_exp,
        ex_line,
        dparts + [qkv_matrix],
    )
    met = lax.optimization_barrier((*dattn_parts, *out_sums))
    dattn_parts, out_sums = (met[:n_exp], met[n_exp:])
    dattn = turn_all(dattn_parts)
    qkv_send = after(qkv_send, dattn_parts[0])
    qkv_core = qkv_keep.astype(F32) + other_core(qkv_send).astype(F32)
    out_core = out_keep.astype(F32) + other_core(out_send).astype(F32)
    fold = Fold((out_core, qkv_core))
    fold.send()
    dattn = fold.meet(*dattn)
    while fold.orders[0]:
        fold.send()
        fold.meet()
    out_weight_sum, qkv_sum = fold.pair
    out_total = out_base
    for piece in out_sums:
        out_total = out_total + piece.astype(F32)
    small_sum = qkv_sum[block : block + 4, :block].reshape(4, n_exp, w_rows).transpose(1, 0, 2)
    small_sum = jnp.pad(small_sum, ((0, 0), (0, w_rows - 4), (0, LANES - w_rows)))
    tail = jnp.concatenate(
        [
            qkv_sum[:block].reshape(n_exp, w_rows, qkv_cols),
            out_weight_sum.reshape(n_exp, w_rows, width),
            small_sum,
            up_sum.astype(F32).reshape(n_exp, w_rows, dense_cols),
        ],
        axis=2,
    ).astype(BF16)
    tail_sent = after(tail, *dattn)
    tail = swap(tail_sent, "expert")
    tokens_grad = simple(
        leave_body, LAST, shape_of((rows, width), BF16), [tokens, gain_one, dmiddle] + list(dattn)
    )

    exp_sum = after(exp_sum, tail_sent)
    up_exp_sum = exp_sum[:up_rows].reshape(n_block, n_core, exp_rows, width)
    own_exp = lax.dynamic_index_in_dim(up_exp_sum, core, 1, False)
    sent_exp = lax.dynamic_index_in_dim(up_exp_sum, 1 - core, 1, False)
    exp_up_grad, exp_down_grad = scalar_call(
        expert_end_body,
        [shape_of((exp_rows, n_dp * exp_cols), F32), shape_of((exp_cols, width), F32)],
        core_line,
        [own_exp, other_core(sent_exp), exp_sum[up_rows:]],
    )
    tail = after(tail, exp_up_grad, exp_down_grad, tokens_grad, out_total, down_sum)
    up_grad = tail[:, :, qkv_cols + width + LANES :].reshape(n_exp, w_rows, n_dp, dense_rows)
    up_grad = up_grad.transpose(1, 2, 0, 3).reshape(w_rows, n_exp * dense_cols).astype(F32)
    qkv_grad = tail[:, :, :qkv_cols].reshape(n_exp, w_rows, 3, head_cols)
    small_sum = jnp.sum(tail[:, :4, qkv_cols + width : qkv_cols + width + w_rows].astype(F32), axis=0)
    return (
        out_total.astype(BF16),
        tokens_grad,
        small_sum[0],
        qkv_grad.transpose(1, 2, 0, 3).reshape(w_rows, 3 * width).astype(F32),
        jnp.sum(tail[:, :, qkv_cols : qkv_cols + width].astype(F32), axis=0),
        small_sum[1],
        small_sum[2:4].T,
        up_grad,
        down_sum.astype(F32),
        exp_up_grad[None],
        exp_down_grad[None],
    )


def solution(mesh):
    n_dp, n_exp = (mesh.shape["dp"], mesh.shape["expert"])
    fine = Mesh(mesh.devices.reshape(n_dp // 2, 2, n_exp), ("chip", "core", "expert"))
    every = ("chip", "core", "expert")
    rows = P(every, None)
    expert = P("expert", DP, None)
    return jax.shard_map(
        shards,
        mesh=fine,
        in_specs=(
            rows,
            P(every),
            rows,
            rows,
            P(every),
            rows,
            rows,
            rows,
            expert,
            expert,
            rows,
            P(DP, None),
            rows,
        ),
        out_specs=(
            rows,
            rows,
            P(every),
            rows,
            rows,
            P(every),
            rows,
            rows,
            rows,
            expert,
            expert,
        ),
        check_vma=False,
    )
```

```python
import jax
import jax.numpy as jnp
from jax import lax
from jax.experimental import pallas as pl
from jax.experimental.pallas import tpu as pltpu
from jax.sharding import Mesh
from jax.sharding import PartitionSpec as P

HEAD_DIM = 64
EPSILON = 1e-05
SCORE_SCALE = 0.125
MASK_VALUE = -1e30
F32 = jnp.float32
BF16 = jnp.bfloat16
DP = ("chip", "core")
LANES = 128
PAD = 16
TANH_SCALE = 0.7978845608028654
TANH_CUBE = 0.044715
VMEM_LIMIT = 60 << 20
FLOPS_US = 1.15e9
LAST = 0


def dot(left, right):
    return jnp.dot(left, right, preferred_element_type=F32)


def dot_rt(left, right):
    return lax.dot_general(left, right, (((1,), (1,)), ((), ())), preferred_element_type=F32)


def dot_lt(left, right):
    return lax.dot_general(left, right, (((0,), (0,)), ((), ())), preferred_element_type=F32)


def norm_parts(values):
    row_mean = jnp.mean(values, axis=-1, keepdims=True)
    centred = values - row_mean
    spread = jnp.mean(centred * centred, axis=-1, keepdims=True)
    inverse = lax.rsqrt(spread + EPSILON)
    return (centred * inverse, inverse)


def norm_back(grad, normed, inverse, gain):
    scaled = grad * gain
    return inverse * (
        scaled
        - jnp.mean(scaled, axis=-1, keepdims=True)
        - normed * jnp.mean(scaled * normed, axis=-1, keepdims=True)
    )


def after(values, *earlier):
    return lax.optimization_barrier((values,) + earlier)[0]


def swap(values, axis):
    return lax.all_to_all(values, axis, split_axis=0, concat_axis=0, tiled=True)


def share(values, axis):
    copies = lax.axis_size(axis)
    return swap(jnp.broadcast_to(values[None], (copies,) + values.shape), axis)


def turn(values, step):
    count = lax.axis_size("expert")
    return lax.ppermute(values, "expert", [(i, (i + step) % count) for i in range(count)])


def turn_all(pieces):
    return [pieces[0]] + [turn(piece, k) for k, piece in enumerate(pieces) if k]


def other_core(values):
    return lax.ppermute(values, "core", [(0, 1), (1, 0)])


def by_core(core, first, second):
    return (jnp.where(core == 0, first, second), jnp.where(core == 0, second, first))


def flip(values, bit):
    chips = range(lax.axis_size("chip"))
    return lax.ppermute(values, "chip", [(i, i ^ bit) for i in chips])


def by_bit(bit, first, second):
    return by_core(lax.axis_index("chip") & bit, first, second)


def chip_bits():
    bits = []
    while 1 << len(bits) < lax.axis_size("chip"):
        bits.append(1 << len(bits))
    return bits


def gather_small(values, axes, copies):
    count, cols = values.shape
    step = min(count, max(16, ((1 << 20) - 1) // (2 * copies * cols) // 16 * 16))
    return [
        lax.all_gather(values[k : k + step], axes, axis=0, tiled=True).reshape(copies, -1, cols)
        for k in range(0, count, step)
    ]


def sum_core(values, core):
    own, sent = by_core(core, values[:, 0], values[:, 1])
    return own.astype(F32) + other_core(sent).astype(F32)


class Fold:
    def __init__(self, pair):
        bits = chip_bits()
        count = len(pair)
        self.orders = [list(bits[:: 1 - 2 * (k % 2)]) for k in range(count)]
        self.left = [sorted(bits, reverse=True) for k in range(count)]
        self.pair = [v.reshape((2,) * len(bits) + v.shape[1:]) for v in pair]

    def send(self):
        self.keeps, self.gots = ([], [])
        for k in range(len(self.pair)):
            bit = self.orders[k].pop(0)
            at = self.left[k].index(bit)
            self.left[k].remove(bit)
            low, high = (lax.index_in_dim(self.pair[k], side, at, False) for side in (0, 1))
            keep, sent = by_bit(bit, low, high)
            self.keeps.append(keep)
            self.gots.append(flip(sent.astype(BF16), bit))

    def meet(self, *others):
        gots = lax.optimization_barrier((*self.gots, *others))
        self.pair = [
            keep.astype(F32) + got.astype(F32)
            for keep, got in zip(self.keeps, gots[: len(self.keeps)], strict=True)
        ]
        return gots[len(self.keeps) :]


def whole(shape):
    return pl.BlockSpec(shape, lambda *at: (0,) * len(shape), pipeline_mode=pl.Buffered(1))


def by_rows(tile, cols):
    return pl.BlockSpec((tile, cols), lambda t: (t, 0))


def shape_of(shape, kind):
    return jax.ShapeDtypeStruct(shape, kind)


def call(body, weight, out_shape, operands, in_specs, out_specs, grid=(1,), scratch=()):
    return pl.pallas_call(
        body,
        grid=grid,
        in_specs=in_specs,
        out_specs=out_specs,
        out_shape=out_shape,
        scratch_shapes=list(scratch),
        compiler_params=pltpu.CompilerParams(vmem_limit_bytes=VMEM_LIMIT),
        cost_estimate=pl.CostEstimate(
            flops=int(weight * FLOPS_US), bytes_accessed=0, transcendentals=0
        ),
    )(*operands)


def enter_body(x_ref, gain_ref, *refs):
    parts, (qkv_ref, attn_ref, w_ref) = (refs[:-3], refs[-3:])
    width, cols = w_ref.shape
    copies = parts[0].shape[0]
    matrix = jnp.concatenate([p[...] for p in parts], axis=1)[:, : width // copies]
    matrix = matrix.reshape(width, cols)
    w_ref[...] = matrix
    normed, unused = norm_parts(x_ref[...].astype(F32))
    attn_input = (normed * gain_ref[...]).astype(BF16)
    attn_ref[...] = attn_input
    qkv_ref[...] = dot(attn_input, matrix).astype(BF16)


def enter(inputs, gain, parts):
    group, width = inputs.shape
    cols = parts[0].shape[2]
    tile = min(512, group)
    return call(
        enter_body,
        0,
        [
            shape_of((group, cols), BF16),
            shape_of((group, width), BF16),
            shape_of((width, cols), BF16),
        ],
        [inputs, gain] + parts,
        [by_rows(tile, width), whole(gain.shape)] + [whole(p.shape) for p in parts],
        [by_rows(tile, cols), by_rows(tile, width), whole((width, cols))],
        grid=(group // tile,),
    )


def seen(split, query_axis, shape, first_query):
    query = first_query + lax.broadcasted_iota(jnp.int32, shape, query_axis)
    key = lax.broadcasted_iota(jnp.int32, shape, 1 - query_axis)
    return (query >= key) & ((query >= split) == (key >= split))


def attend_body(split_ref, q_ref, k_ref, v_ref, out_ref):
    tile, cols = q_ref.shape
    allowed = seen(split_ref[0], 0, (tile, k_ref.shape[0]), pl.program_id(1) * tile)
    for h in range(cols // HEAD_DIM):
        at = slice(h * HEAD_DIM, (h + 1) * HEAD_DIM)
        scores = dot_rt(q_ref[:, at], k_ref[:, at]) * SCORE_SCALE
        scores = jnp.where(allowed, scores, MASK_VALUE)
        weights = jnp.exp(scores - jnp.max(scores, axis=1, keepdims=True))
        probs = weights * (1.0 / jnp.sum(weights, axis=1, keepdims=True))
        result = dot(probs.astype(BF16), v_ref[:, at]).astype(BF16)
        for j in range(out_ref.shape[0]):
            out_ref[j, :, at] = result


def attend_back_body(
    split_ref, q_ref, k_ref, v_ref, grad_ref, dq_ref, dk_ref, dv_ref, dk_sum, dv_sum
):
    tile, cols = q_ref.shape
    step = pl.program_id(1)
    allowed = seen(split_ref[0], 1, (k_ref.shape[0], tile), step * tile)
    for h in range(cols // HEAD_DIM):
        at = slice(h * HEAD_DIM, (h + 1) * HEAD_DIM)
        query, keys, vals, grad = (r[:, at] for r in (q_ref, k_ref, v_ref, grad_ref))
        scores = jnp.where(allowed, dot_rt(keys, query) * SCORE_SCALE, MASK_VALUE)
        weights = jnp.exp(scores - jnp.max(scores, axis=0, keepdims=True))
        probs = weights * (1.0 / jnp.sum(weights, axis=0, keepdims=True))
        dprobs = dot_rt(vals, grad)
        delta = jnp.sum(probs * dprobs, axis=0, keepdims=True)
        dscores = (probs * (dprobs - delta)).astype(BF16)
        dq_ref[:, at] = (dot_lt(dscores, keys) * SCORE_SCALE).astype(BF16)
        dk_new = dot(dscores, query) * SCORE_SCALE
        dv_new = dot(probs.astype(BF16), grad)

        @pl.when(step == 0)
        def first():
            dk_sum[:, at] = dk_new
            dv_sum[:, at] = dv_new

        @pl.when(step > 0)
        def later():
            dk_sum[:, at] += dk_new
            dv_sum[:, at] += dv_new

    @pl.when(step == pl.num_programs(1) - 1)
    def last():
        dk_ref[...] = dk_sum[...].astype(BF16)
        dv_ref[...] = dv_sum[...].astype(BF16)


def attention_parts(qkv, head_cols):
    group = qkv.shape[0]
    cols = min(LANES, head_cols)
    pairs = head_cols // cols
    tile = min(512, group)
    if head_cols % LANES == 0:
        operands, shift = ([qkv] * 3, pairs)
    else:
        operands = [qkv[:, k * head_cols : (k + 1) * head_cols] for k in range(3)]
        shift = 0
    specs = [
        pl.BlockSpec(memory_space=pltpu.SMEM),
        pl.BlockSpec((tile, cols), lambda p, t: (t, p)),
        pl.BlockSpec((group, cols), lambda p, t: (0, shift + p)),
        pl.BlockSpec((group, cols), lambda p, t: (0, 2 * shift + p)),
    ]
    by_tile = pl.BlockSpec((tile, cols), lambda p, t: (t, p))
    by_pair = pl.BlockSpec((group, cols), lambda p, t: (0, p))
    return (operands, specs, by_tile, by_pair, (pairs, group // tile), cols)


def attend(qkv, split, head_cols, copies):
    group = qkv.shape[0]
    tile = min(512, group)
    operands, specs, unused, unused, grid, cols = attention_parts(qkv, head_cols)
    return call(
        attend_body,
        0,
        [shape_of((copies, group, head_cols), BF16)],
        [split] + operands,
        specs,
        [pl.BlockSpec((copies, tile, cols), lambda p, t: (0, t, p))],
        grid=grid,
    )[0]


def attend_back(qkv, grad, split, head_cols):
    group = qkv.shape[0]
    operands, specs, by_tile, by_pair, grid, cols = attention_parts(qkv, head_cols)
    return call(
        attend_back_body,
        20,
        [shape_of((group, head_cols), BF16)] * 3,
        [split] + operands + [grad],
        specs + [by_tile],
        [by_tile, by_pair, by_pair],
        grid=grid,
        scratch=[pltpu.VMEM((group, cols), F32)] * 2,
    )


def middle_body(att_ref, x_ref, w_ref, gain_ref, mix_ref, middle_ref, ffn_ref, coeff_ref):
    n_exp, unused, head_cols = att_ref.shape
    middle = x_ref[...].astype(F32)
    for j in range(n_exp):
        middle = middle + dot(att_ref[j], w_ref[j * head_cols : (j + 1) * head_cols])
    middle_ref[...] = middle
    normed, unused = norm_parts(middle)
    ffn_input = (normed * gain_ref[...]).astype(BF16)
    ffn_ref[...] = ffn_input
    logits = dot_rt(ffn_input, mix_ref[...])
    first, second = (logits[:, 0:1], logits[:, 1:2])
    top = jnp.maximum(first, second)
    first, second = (jnp.exp(first - top), jnp.exp(second - top))
    coeff_ref[...] = jnp.concatenate([first, second], axis=1) / (first + second)


def to_middle(attended, inputs, matrix, gain, mix):
    n_exp, group, head_cols = attended.shape
    width = matrix.shape[0]
    tile = min(512, group)
    return call(
        middle_body,
        0,
        [shape_of((group, width), F32), shape_of((group, width), BF16), shape_of((group, 2), F32)],
        [attended, inputs, matrix, gain, mix],
        [
            pl.BlockSpec((n_exp, tile, head_cols), lambda t: (0, t, 0)),
            by_rows(tile, width),
            whole(matrix.shape),
            whole(gain.shape),
            whole(mix.shape),
        ],
        [by_rows(tile, width), by_rows(tile, width), by_rows(tile, 2)],
        grid=(group // tile,),
    )


def bend(pre):
    square = pre * pre
    bent = jnp.tanh(TANH_SCALE * pre * (1.0 + TANH_CUBE * square))
    half = 0.5 * (1.0 + bent)
    slope = half + 0.5 * pre * (1.0 - bent * bent) * TANH_SCALE * (1.0 + 3.0 * TANH_CUBE * square)
    return ((pre * half).astype(BF16), slope)


def add_step(total, new):
    @pl.when(pl.program_id(0) == 0)
    def first():
        total[...] = new

    @pl.when(pl.program_id(0) > 0)
    def later():
        total[...] += new


def hidden_back(rows_in, rows_grad, up, down, din_sum):
    act, slope = bend(dot(rows_in, up))
    dpre = (slope * dot_rt(rows_grad, down)).astype(BF16)
    add_step(din_sum, dot_rt(dpre, up))
    return (act, dpre)


def fill_rows(own_ref, got_ref, rows_in, rows_grad):
    capacity = own_ref.shape[1]

    @pl.when(pl.program_id(0) == 0)
    def begin():
        rows_in[:capacity] = own_ref[0]
        rows_in[capacity:] = got_ref[0]
        rows_grad[:capacity] = own_ref[1]
        rows_grad[capacity:] = got_ref[1]


def expert_body(
    own_ref,
    got_ref,
    up_ref,
    down_ref,
    keep_ref,
    send_ref,
    act_ref,
    dpre_ref,
    rows_in,
    rows_grad,
    outs,
    dins,
):
    width = own_ref.shape[2]
    capacity = own_ref.shape[1]
    fill_rows(own_ref, got_ref, rows_in, rows_grad)
    up = up_ref[...].reshape(width, -1)
    act, dpre_ref[...] = hidden_back(rows_in[...], rows_grad[...], up, down_ref[0], dins)
    add_step(outs, dot(act, down_ref[0]))
    act_ref[...] = act

    @pl.when(pl.program_id(0) == pl.num_programs(0) - 1)
    def last():
        for k, total in enumerate((outs, dins)):
            keep_ref[k] = total[:capacity]
            send_ref[k] = total[capacity:].astype(BF16)


def expert_grad_body(own_x, got_x, own_g, got_g, act_ref, dpre_ref, grads_ref):
    width = grads_ref.shape[2]
    rows_in = jnp.concatenate([own_x[0], got_x[0]], axis=0)
    rows_grad = jnp.concatenate([own_g[0], got_g[0]], axis=0)
    dup = dot_lt(rows_in, dpre_ref[...]).astype(BF16)
    pair_rows, hidden = dup.shape
    up_rows = hidden // width * pair_rows
    for k in range(hidden // width):
        at = slice(k * pair_rows, (k + 1) * pair_rows)
        grads_ref[0, at] = dup[:, k * width : (k + 1) * width]
    grads_ref[0, up_rows:] = dot_lt(act_ref[...], rows_grad).astype(BF16)


def expert_ffn(own, got, up, down, pair_rows):
    unused, capacity, width = own.shape
    n_chip, exp_cols, unused = down.shape
    per = width // exp_cols
    count = 2 * capacity
    hidden = n_chip * exp_cols
    by_cols = pl.BlockSpec((count, exp_cols), lambda c: (0, c))
    return call(
        expert_body,
        0,
        [
            shape_of(own.shape, F32),
            shape_of(own.shape, BF16),
            shape_of((count, hidden), BF16),
            shape_of((count, hidden), BF16),
        ],
        [own, got, up, down],
        [
            whole(own.shape),
            whole(own.shape),
            pl.BlockSpec((n_chip, pair_rows, exp_cols), lambda c: (0, c // per, c % per)),
            pl.BlockSpec((1, exp_cols, width), lambda c: (c, 0, 0)),
        ],
        [whole(own.shape), whole(own.shape), by_cols, by_cols],
        grid=(n_chip,),
        scratch=[pltpu.VMEM((count, width), BF16)] * 2 + [pltpu.VMEM((count, width), F32)] * 2,
    )


def expert_grad(own, got, act, dpre, n_chip):
    unused, capacity, width = own.shape
    count, hidden = act.shape
    cols, pair_rows = (hidden // n_chip, width // n_chip)
    rows = hidden // width * pair_rows + cols
    by_width = pl.BlockSpec((1, capacity, pair_rows), lambda d: (0, 0, d))
    second = pl.BlockSpec((1, capacity, width), lambda d: (1, 0, 0))
    return call(
        expert_grad_body,
        0,
        [shape_of((n_chip, rows, width), BF16)],
        [own, got, own, got, act, dpre],
        [
            by_width,
            by_width,
            second,
            second,
            pl.BlockSpec((count, cols), lambda d: (0, d)),
            whole(dpre.shape),
        ],
        [pl.BlockSpec((1, rows, width), lambda d: (d, 0, 0))],
        grid=(n_chip,),
    )[0]


def dense_body(ex_ref, x_ref, g_ref, coeff_ref, slot_ref, up_ref, down_ref, *refs):
    outs, (pay_ref, act_ref, dpre_ref, ddense_ref, own_ref, dense, dins) = (refs[:-7], refs[-7:])
    n_exp, padded, width = pay_ref.shape
    rows = padded - PAD

    @pl.when(pl.program_id(0) == 0)
    def begin():
        grad = g_ref[...].astype(F32)
        ddense_ref[...] = (coeff_ref[:, 0:1] * grad).astype(BF16)
        shape = (own_ref.shape[1], x_ref.shape[0])
        pick = (lax.broadcasted_iota(jnp.int32, shape, 0) == slot_ref[...]).astype(F32)
        pick = pick.astype(BF16)
        own_ref[0] = dot(pick, x_ref[...]).astype(BF16)
        own_ref[1] = dot(pick, (coeff_ref[:, 1:2] * grad).astype(BF16)).astype(BF16)

    up = up_ref[...].reshape(width, -1)
    down = down_ref[...].reshape(-1, width)
    act, dpre_ref[...] = hidden_back(x_ref[...], ddense_ref[...], up, down, dins)
    act_ref[...] = act
    add_step(dense, dot(act, down))

    @pl.when(pl.program_id(0) == pl.num_programs(0) - 1)
    def last():
        for k, out_ref in enumerate(outs):
            to = lax.rem(ex_ref[0] + k, len(outs))
            at = pl.ds(pl.multiple_of(to * rows, rows), rows)
            out_ref[...] = (coeff_ref[at, 0:1] * dense[at]).astype(BF16)
        for j in range(n_exp):
            at = slice(j * rows, (j + 1) * rows)
            pay_ref[j, :rows] = dins[at].astype(BF16)
            sums = jnp.sum(g_ref[at].astype(F32) * dense[at], axis=1, keepdims=True)
            line = jnp.transpose(sums * jnp.ones((1, LANES), F32))[:PAD]
            high = line.astype(BF16).astype(F32)
            index = lax.broadcasted_iota(jnp.int32, (PAD, rows), 0)
            extra = jnp.where(index == 0, high, jnp.where(index == 1, line - high, 0.0))
            pay_ref[j, rows:] = jnp.concatenate(
                [extra, jnp.zeros((PAD, width - rows), F32)], axis=1
            ).astype(BF16)


def dense_grad_body(x_ref, g_ref, act_ref, dpre_ref, dup_ref, ddown_ref):
    dup_ref[...] = dot_lt(x_ref[...], dpre_ref[...]).astype(BF16)
    ddown_ref[...] = dot_lt(act_ref[...], g_ref[...]).astype(BF16)


def dense_ffn(ex, ffn_input, grad, coeffs, slot, capacity, weights, specs, hidden, rows):
    group, width = ffn_input.shape
    step = 2 * LANES
    count = group // rows
    operands = [ffn_input, grad, coeffs, slot]
    own = (2, capacity, width)
    padded = (count, rows + PAD, width)
    by_cols = pl.BlockSpec((group, step), lambda c: (0, c))
    return call(
        dense_body,
        0,
        [shape_of((rows, width), BF16)] * count
        + [shape_of(padded, BF16)]
        + [shape_of((group, hidden), BF16)] * 2
        + [shape_of((group, width), BF16), shape_of(own, BF16)],
        [ex] + operands + weights,
        [pl.BlockSpec(memory_space=pltpu.SMEM)] + [whole(o.shape) for o in operands] + specs,
        [whole((rows, width))] * count
        + [whole(padded), by_cols, by_cols, whole((group, width)), whole(own)],
        grid=(hidden // step,),
        scratch=[pltpu.VMEM((group, width), F32)] * 2,
    )


def dense_pack_body(core_ref, x_ref, g_ref, act_ref, dpre_ref, keep_ref, send_ref):
    n_chip, unused, block, unused = keep_ref.shape
    step = act_ref.shape[1]
    chunk = pl.program_id(0)
    left = pl.ds(pl.multiple_of(chunk * step, step), step)
    first_core = core_ref[0] == 0
    dup = dot_lt(x_ref[...], dpre_ref[...]).astype(BF16).reshape(n_chip, 2, block, step)
    ddown = dot_lt(act_ref[...], g_ref[...]).astype(BF16)
    keep_ref[:, 0, :, left] = jnp.where(first_core, dup[:, 0], dup[:, 1])
    send_ref[:, 0, :, left] = jnp.where(first_core, dup[:, 1], dup[:, 0])
    at = pl.ds(chunk, 1)
    keep_ref[at, 1] = jnp.where(first_core, ddown[:block], ddown[block:])[None]
    send_ref[at, 1] = jnp.where(first_core, ddown[block:], ddown[:block])[None]


def dense_split(core, ffn_input, ddense, act, dpre, shape):
    group, step = (ffn_input.shape[0], 2 * LANES)
    by_cols = pl.BlockSpec((group, step), lambda c: (0, c))
    return call(
        dense_pack_body,
        0,
        [shape_of(shape, BF16)] * 2,
        [core, ffn_input, ddense, act, dpre],
        [
            pl.BlockSpec(memory_space=pltpu.SMEM),
            whole(ffn_input.shape),
            whole(ddense.shape),
            by_cols,
            by_cols,
        ],
        [whole(shape)] * 2,
        grid=(act.shape[1] // step,),
    )


def dense_grad(ffn_input, ddense, act, dpre):
    group, width = ffn_input.shape
    hidden = act.shape[1]
    step = 2 * LANES
    by_cols = pl.BlockSpec((group, step), lambda c: (0, c))
    return call(
        dense_grad_body,
        0,
        [shape_of((width, hidden), BF16), shape_of((hidden, width), BF16)],
        [ffn_input, ddense, act, dpre],
        [whole(ffn_input.shape), whole(ddense.shape), by_cols, by_cols],
        [
            pl.BlockSpec((width, step), lambda c: (0, c)),
            pl.BlockSpec((step, width), lambda c: (c, 0)),
        ],
        grid=(hidden // step,),
    )


def middle_back_body(
    ex_ref, pay_ref, slot_ref, middle_ref, coeff_ref, g_ref, gain_ref, mix_ref, w_ref, *refs
):
    rets, (dmid_ref, low_ref, datt_ref, small_ref, base_ref) = (refs[:-5], refs[-5:])
    rows, width = middle_ref.shape
    n_exp = pay_ref.shape[0]
    head_cols = datt_ref.shape[2]
    total = pay_ref[0].astype(F32)
    for j in range(1, n_exp):
        total = total + pay_ref[j].astype(F32)
    capacity = rets[0].shape[1]
    exp_rows, exp_din = (jnp.zeros((rows, width), F32) for k in range(2))
    index = lax.broadcasted_iota(jnp.int32, (rows, capacity), 1)
    for k, ret_ref in enumerate(rets):
        source = lax.rem(ex_ref[0] + n_exp - k, n_exp)
        place = (index + source * capacity == slot_ref[...]).astype(F32).astype(BF16)
        exp_rows = exp_rows + dot(place, ret_ref[0])
        exp_din = exp_din + dot(place, ret_ref[1])
    dffn = total[:rows] + exp_din
    lines = jnp.concatenate([total[rows:, :rows], jnp.zeros((rows - PAD, rows), F32)], axis=0)
    lines = jnp.transpose(lines)
    grad = g_ref[...].astype(F32)
    dcoeff = [lines[:, 0:1] + lines[:, 1:2], jnp.sum(grad * exp_rows, axis=1, keepdims=True)]
    coeff = [coeff_ref[:, k : k + 1] for k in range(2)]
    base_ref[...] = middle_ref[...] + coeff[1] * exp_rows
    inner = coeff[0] * dcoeff[0] + coeff[1] * dcoeff[1]
    dlogit = [(c * (d - inner)).astype(BF16).astype(F32) for c, d in zip(coeff, dcoeff, strict=True)]
    mix = mix_ref[...].astype(F32)
    dffn = dffn + dlogit[0] * mix[0:1] + dlogit[1] * mix[1:2]
    normed, inverse = norm_parts(middle_ref[...])
    gain = gain_ref[...]
    dmiddle = grad + norm_back(dffn, normed, inverse, gain)
    dmid_ref[...] = dmiddle
    low = dmiddle.astype(BF16)
    low_ref[...] = low
    datt = dot_rt(low, w_ref[...]).astype(BF16)
    for j in range(n_exp):
        datt_ref[j] = datt[:, j * head_cols : (j + 1) * head_cols]
    lane = lax.broadcasted_iota(jnp.int32, (rows, LANES), 1)
    pair = jnp.where(lane == 0, dlogit[0], jnp.where(lane == 1, dlogit[1], 0.0)).astype(BF16)
    dmix = dot_lt(pair, (normed * gain).astype(BF16))
    dgain = jnp.sum(dffn * normed, axis=0, keepdims=True)
    nothing = jnp.zeros((1, width), F32)
    small_ref[...] = jnp.concatenate([nothing, dgain, dmix[:2], jnp.zeros((4, width), F32)], axis=0)


def middle_back(ex, arrived, returned, slot, middle, coeffs, grad, gain, mix, matrix, head_cols):
    rows, width = middle.shape
    n_exp = arrived.shape[0]
    operands = [arrived, slot, middle, coeffs, grad, gain, mix, matrix] + list(returned)
    shapes = [
        shape_of((rows, width), F32),
        shape_of((rows, width), BF16),
        shape_of((n_exp, rows, head_cols), BF16),
        shape_of((8, width), F32),
        shape_of((rows, width), F32),
    ]
    return call(
        middle_back_body,
        0,
        shapes,
        [ex] + operands,
        [pl.BlockSpec(memory_space=pltpu.SMEM)] + [whole(o.shape) for o in operands],
        [whole(o.shape) for o in shapes],
    )


def split_cores(core_ref, grads, keep_ref, send_ref):
    n_chip, block = keep_ref.shape[:2]
    grads = grads.reshape(n_chip, 2, block, grads.shape[-1])
    first_core = core_ref[0] == 0
    keep_ref[...] = jnp.where(first_core, grads[:, 0], grads[:, 1])
    send_ref[...] = jnp.where(first_core, grads[:, 1], grads[:, 0])


def out_grad_body(core_ref, att_ref, low_ref, keep_ref, send_ref):
    grads = [dot_lt(att_ref[j], low_ref[...]).astype(BF16) for j in range(att_ref.shape[0])]
    split_cores(core_ref, jnp.concatenate(grads, axis=0), keep_ref, send_ref)


def attn_input_back_body(ex_ref, dq_ref, dk_ref, dv_ref, w_ref, *pays):
    rows = pays[0].shape[0]
    for k, pay_ref in enumerate(pays):
        to = lax.rem(ex_ref[0] + k, len(pays))
        at = pl.ds(pl.multiple_of(to * rows, rows), rows)
        grads = jnp.concatenate([dq_ref[at], dk_ref[at], dv_ref[at]], axis=1)
        pay_ref[...] = dot_rt(grads, w_ref[...]).astype(BF16)


def qkv_grad_body(
    core_ref, x_ref, w_ref, gain_ref, small_ref, dq_ref, dk_ref, dv_ref, keep_ref, send_ref
):
    n_chip, padded, cols = keep_ref.shape
    block = padded - PAD
    rows_in = x_ref[...]
    grads = jnp.concatenate([dot_lt(rows_in, r[...]) for r in (dq_ref, dk_ref, dv_ref)], axis=1)
    width = grads.shape[0]
    dgain = jnp.sum(grads * w_ref[...].astype(F32), axis=1, keepdims=True)
    dgain = jnp.transpose(dgain * jnp.ones((1, LANES), F32))[:8] / gain_ref[...]
    index = lax.broadcasted_iota(jnp.int32, (8, width), 0)
    small = jnp.where(index == 0, dgain, small_ref[...])
    small = jnp.concatenate([small, jnp.zeros((PAD - 8, width), F32)], axis=0)
    first_core = core_ref[0] == 0
    for chip in range(n_chip):
        pair = []
        for core in range(2):
            low = (2 * chip + core) * block
            edge = jnp.concatenate(
                [small[:, low : low + block], jnp.zeros((PAD, cols - block), F32)], axis=1
            )
            pair.append(jnp.concatenate([grads[low : low + block], edge], axis=0).astype(BF16))
        keep_ref[chip] = jnp.where(first_core, pair[0], pair[1])
        send_ref[chip] = jnp.where(first_core, pair[1], pair[0])


def scalar_call(body, shapes, scalar, operands, weight=0):
    return call(
        body,
        weight,
        shapes,
        [scalar] + operands,
        [pl.BlockSpec(memory_space=pltpu.SMEM)] + [whole(o.shape) for o in operands],
        [whole(o.shape) for o in shapes],
    )


def expert_end_body(core_ref, own_ref, got_ref, down_ref, up_out, down_out):
    cols = down_ref.shape[0]
    per = own_ref.shape[2] // cols
    first_core = core_ref[0] == 0
    for k in range(own_ref.shape[0] * per):
        at = slice(k % per * cols, (k % per + 1) * cols)
        mine, theirs = (r[k // per, :, at].astype(F32) for r in (own_ref, got_ref))
        low = 2 * k * cols
        up_out[:, low : low + cols] = jnp.where(first_core, mine, theirs)
        up_out[:, low + cols : low + 2 * cols] = jnp.where(first_core, theirs, mine)
    down_out[...] = down_ref[...].astype(F32)


def leave_body(x_ref, gain_ref, dmid_ref, *refs):
    pays, out_ref = (refs[:-1], refs[-1])
    dattn = pays[0][...].astype(F32)
    for pay_ref in pays[1:]:
        dattn = dattn + pay_ref[...].astype(F32)
    normed, inverse = norm_parts(x_ref[...].astype(F32))
    out_ref[...] = (dmid_ref[...] + norm_back(dattn, normed, inverse, gain_ref[...])).astype(BF16)


def simple(body, weight, shape, operands):
    return call(
        body,
        weight,
        [shape],
        operands,
        [whole(o.shape) for o in operands],
        [whole(shape.shape)],
    )[0]


def shards(
    tokens,
    first_gain,
    w_qkv,
    w_out,
    second_gain,
    w_mix,
    w_up,
    w_down,
    expert_up,
    expert_down,
    expert_ids,
    doc_lengths,
    out_grad,
):
    rows, width = tokens.shape
    n_chip, n_core, n_exp = (lax.axis_size(a) for a in ("chip", "core", "expert"))
    n_dp = n_chip * n_core
    group = rows * n_exp
    head_cols = width // n_exp
    qkv_cols = 3 * head_cols
    w_rows = w_qkv.shape[0]
    block = n_exp * w_rows
    dense_rows = w_down.shape[0]
    dense_cols = n_dp * dense_rows
    exp_rows = expert_up.shape[1]
    exp_cols = expert_down.shape[1]
    ex = lax.axis_index("expert")
    ex_line = jnp.full((1,), ex, jnp.int32)
    core = lax.axis_index("core")
    core_line = jnp.full((1,), core, jnp.int32)
    share_cap = max(2, 5 * rows // (4 * n_exp))
    capacity = n_exp * share_cap
    bits = chip_bits()

    exp_split = (
        expert_up[0]
        .reshape(exp_rows, n_chip, n_core, exp_cols)
        .transpose(2, 0, 1, 3)
        .reshape(n_core, exp_rows, n_chip * exp_cols)
    )
    own_half, sent_half = by_core(core, exp_split[0], exp_split[1])
    chip_up = jnp.concatenate(by_core(core, own_half, other_core(sent_half)), axis=0)
    pair_rows = n_core * exp_rows
    n_block = n_chip * exp_cols // width
    up_rows = n_block * pair_rows
    chip_up = chip_up.reshape(pair_rows, n_block, width).transpose(1, 0, 2)
    down_all = lax.all_gather(expert_down[0], "chip", axis=0, tiled=True)
    down_all = down_all.reshape(n_chip, exp_cols, width)

    qkv_blocks = w_qkv.reshape(w_rows, 3, n_exp, head_cols).transpose(2, 0, 1, 3)
    small = jnp.stack([first_gain, second_gain, w_mix[:, 0], w_mix[:, 1]])
    small = jnp.concatenate(
        [
            jnp.pad(small, ((0, w_rows - 4), (0, LANES - w_rows))),
            jnp.pad(expert_ids[:, 0].astype(BF16)[None], ((0, w_rows - 1), (0, LANES - rows))),
        ],
        axis=1,
    )
    up_blocks = w_up.reshape(w_rows, n_dp, n_exp, dense_rows).transpose(2, 0, 1, 3)
    others = jnp.concatenate([w_out, small], axis=1)
    dealt = swap(
        jnp.concatenate(
            [
                qkv_blocks.reshape(n_exp, w_rows, qkv_cols),
                up_blocks.reshape(n_exp, w_rows, dense_cols),
                jnp.broadcast_to(others[None], (n_exp,) + others.shape),
            ],
            axis=2,
        ),
        "expert",
    )
    at = [qkv_cols, qkv_cols + dense_cols, qkv_cols + dense_cols + width]
    up_own = dealt[:, :, at[0] : at[1]].reshape(block, dense_cols)
    out_own = dealt[:, :, at[1] : at[2]].reshape(block, width)
    chip_up = chip_up.reshape(up_rows, width)
    grad_copies = jnp.broadcast_to(out_grad[None], (n_exp,) + out_grad.shape)
    dealt, chip_up, grad_copies = lax.optimization_barrier((dealt, chip_up, grad_copies))
    choice = after(dealt[:, 0, at[2] + LANES : at[2] + LANES + rows].astype(F32)).astype(jnp.int32)
    small = dealt[:, :4, at[2] : at[2] + w_rows].transpose(1, 0, 2).reshape(4, block)
    first_own = jnp.concatenate(
        [
            dealt[:, :, :qkv_cols].reshape(block, qkv_cols),
            jnp.pad(small, ((0, 4), (0, qkv_cols - block))),
        ]
    )
    group_tokens = share(after(tokens, dealt), "expert")
    first_parts = gather_small(first_own, DP, n_dp)
    small = first_parts[-1][:, -8:-4, :block].transpose(1, 0, 2).reshape(4, width)
    gain_one = small[0:1].astype(F32)
    gain_two = small[1:2].astype(F32)
    mix_rows = jnp.pad(small[2:4], ((0, PAD - 2), (0, 0)))

    group_tokens = after(group_tokens, first_parts, gain_one)
    inputs = group_tokens.reshape(group, width)
    step = 2 * LANES
    if dense_cols == width and dense_rows == block:
        dense_pack = after(jnp.concatenate([out_own, up_own, w_down], axis=0), inputs, down_all)
        dense_all = lax.all_gather(dense_pack, DP, axis=0, tiled=True)
        dense_all = dense_all.reshape(n_dp, 3, block, width)
        out_matrix = dense_all[:, 0].reshape(width, width)
        up_matrix = down_matrix = dense_all
        up_spec = pl.BlockSpec((n_dp, 1, block, step), lambda c: (0, 1, 0, c))
        down_spec = pl.BlockSpec((step // block, 1, block, width), lambda c: (c, 2, 0, 0))
    else:
        out_matrix, up_matrix, down_matrix = (
            lax.all_gather(w, DP, axis=0, tiled=True) for w in (out_own, up_own, w_down)
        )
        up_spec = pl.BlockSpec((width, step), lambda c: (0, c))
        down_spec = pl.BlockSpec((step, width), lambda c: (c, 0))
    chip_up = after(chip_up, inputs)
    up_all = lax.all_gather(chip_up, "chip", axis=0, tiled=True)
    up_all = up_all.reshape(n_chip, up_rows, width)

    grad_all = swap(after(grad_copies, inputs), "expert").reshape(group, width)

    qkv, attn_input, qkv_matrix = enter(inputs, gain_one, first_parts)
    doc_split = doc_lengths[0, :1]
    attended_own = attend(qkv, doc_split, head_cols, n_exp)
    attended_own, grad_all = lax.optimization_barrier((attended_own, grad_all))
    attended_all = swap(attended_own, "expert")
    same = (choice[:, :, None] == choice[:, None, :]).astype(jnp.int32)
    earlier = jnp.arange(rows)[None, None, :] < jnp.arange(rows)[None, :, None]
    rank = jnp.sum(jnp.where(earlier, same, 0), axis=2)
    first_slot = jnp.arange(n_exp, dtype=jnp.int32)[:, None] * share_cap
    slot = jnp.where(choice == ex, first_slot + rank, -1).reshape(1, group)
    slot_own = lax.dynamic_slice_in_dim(choice * share_cap + rank, ex, 1, 0).reshape(rows, 1)
    slot, slot_own = lax.optimization_barrier((slot, slot_own))
    attended_all = after(attended_all, out_matrix, slot)
    middle, ffn_input, coeffs = to_middle(attended_all, inputs, out_matrix, gain_two, mix_rows)


    weights, specs = ([up_matrix, down_matrix], [up_spec, down_spec])
    *out_parts, payload, dense_act, dense_dpre, ddense, own_rows = dense_ffn(
        ex_line, ffn_input, grad_all, coeffs, slot, capacity, weights, specs, dense_cols, rows
    )
    arrived = swap(payload, "expert")
    joined = dense_cols == width and dense_rows == block and step == 2 * block
    if joined:
        shape = (n_chip, 2, block, width)
        grads = dense_split(core_line, ffn_input, ddense, dense_act, dense_dpre, shape)
    else:
        grads = dense_grad(ffn_input, ddense, dense_act, dense_dpre)
    got_rows, *grads = lax.optimization_barrier((other_core(own_rows), *grads))
    if joined:
        dense_core = (grads[0].astype(F32) + other_core(grads[1]).astype(F32)).astype(BF16)
        got_rows, dense_core = lax.optimization_barrier((got_rows, dense_core))
        dense_sum = lax.psum_scatter(
            dense_core.reshape(-1, width), "chip", scatter_dimension=0, tiled=True
        )
        up_sum, down_sum = (dense_sum[:block], dense_sum[block:])
    else:
        up_sum, down_sum = (
            lax.psum_scatter(g, DP, scatter_dimension=0, tiled=True) for g in grads
        )
    exp_keep, exp_send, exp_act, exp_dpre = expert_ffn(
        own_rows, got_rows, up_all, down_all, pair_rows
    )
    exp_back = other_core(exp_send)
    returned = []
    for k in range(n_exp):
        low = lax.rem(ex + k, n_exp) * share_cap
        piece = [lax.dynamic_slice_in_dim(v, low, share_cap, 1) for v in (exp_keep, exp_back)]
        returned.append((piece[0] + piece[1].astype(F32)).astype(BF16))
    exp_grads = expert_grad(
        own_rows, got_rows, exp_act, exp_dpre, n_chip
    )
    arrived, exp_grads, *returned = lax.optimization_barrier((arrived, exp_grads, *returned))
    returned = turn_all(returned)
    exp_sum = lax.psum_scatter(
        exp_grads.reshape(-1, width), "chip", scatter_dimension=0, tiled=True
    )

    def mine(values, size=rows):
        return lax.dynamic_slice_in_dim(values, ex * size, size, 0)

    middle_own, coeffs_own = (mine(middle), mine(coeffs))
    att_own = lax.dynamic_slice_in_dim(attended_all, ex * rows, rows, 1)
    returned[0] = after(returned[0], middle_own, coeffs_own, att_own)
    dmiddle, dmid_low, datt, small_two, out_base = middle_back(
        ex_line,
        arrived,
        returned,
        slot_own,
        middle_own,
        coeffs_own,
        out_grad,
        gain_two,
        mix_rows,
        out_matrix,
        head_cols,
    )
    dattended = swap(datt, "expert")
    out_keep, out_send = scalar_call(
        out_grad_body,
        [shape_of((n_chip, block, width), BF16)] * 2,
        core_line,
        [att_own, dmid_low],
    )
    dattended, out_keep, out_send = lax.optimization_barrier((dattended, out_keep, out_send))
    dattended = dattended.reshape(group, head_cols)
    out_sums = turn_all([after(piece, dattended) for piece in out_parts])
    out_core = out_keep.astype(F32) + other_core(out_send).astype(F32)
    out_fold = Fold((out_core,))
    out_fold.send()

    dparts = attend_back(qkv, dattended, doc_split, head_cols)
    qkv_shape = shape_of((n_chip, block + PAD, qkv_cols), BF16)
    qkv_keep, qkv_send = scalar_call(
        qkv_grad_body,
        [qkv_shape] * 2,
        core_line,
        [attn_input, qkv_matrix, gain_one, small_two] + list(dparts),
    )
    dparts = [after(dparts[0], qkv_keep), dparts[1], dparts[2]]
    dattn_parts = scalar_call(
        attn_input_back_body,
        [shape_of((rows, width), BF16)] * n_exp,
        ex_line,
        dparts + [qkv_matrix],
    )
    met = out_fold.meet(*dattn_parts, *out_sums)
    dattn_parts, out_sums = (met[:n_exp], met[n_exp:])
    dattn = turn_all(dattn_parts)
    qkv_send = after(qkv_send, dattn_parts[0])
    qkv_core = qkv_keep.astype(F32) + other_core(qkv_send).astype(F32)
    half = qkv_cols // 2
    halves = (qkv_core,)
    if half % LANES == 0:
        halves = (qkv_core[..., :half], qkv_core[..., half:])
    fold = Fold(halves)
    fold.send()
    while out_fold.orders[0]:
        out_fold.send()
        dattn = out_fold.meet(*dattn)
    dattn = fold.meet(*dattn)
    while fold.orders[0]:
        fold.send()
        fold.meet()
    out_weight_sum, qkv_sum = (out_fold.pair[0], jnp.concatenate(fold.pair, axis=-1))
    out_total = out_base
    for piece in out_sums:
        out_total = out_total + piece.astype(F32)
    small_sum = qkv_sum[block : block + 4, :block].reshape(4, n_exp, w_rows).transpose(1, 0, 2)
    small_sum = jnp.pad(small_sum, ((0, 0), (0, w_rows - 4), (0, LANES - w_rows)))
    tail = jnp.concatenate(
        [
            qkv_sum[:block].reshape(n_exp, w_rows, qkv_cols),
            out_weight_sum.reshape(n_exp, w_rows, width),
            small_sum,
            up_sum.astype(F32).reshape(n_exp, w_rows, dense_cols),
        ],
        axis=2,
    ).astype(BF16)
    tail_sent = after(tail, *dattn)
    tail = swap(tail_sent, "expert")
    tokens_grad = simple(
        leave_body, LAST, shape_of((rows, width), BF16), [tokens, gain_one, dmiddle] + list(dattn)
    )

    exp_sum = after(exp_sum, tail_sent)
    up_exp_sum = exp_sum[:up_rows].reshape(n_block, n_core, exp_rows, width)
    own_exp = lax.dynamic_index_in_dim(up_exp_sum, core, 1, False)
    sent_exp = lax.dynamic_index_in_dim(up_exp_sum, 1 - core, 1, False)
    exp_up_grad, exp_down_grad = scalar_call(
        expert_end_body,
        [shape_of((exp_rows, n_dp * exp_cols), F32), shape_of((exp_cols, width), F32)],
        core_line,
        [own_exp, other_core(sent_exp), exp_sum[up_rows:]],
    )
    tail = after(tail, exp_up_grad, exp_down_grad, tokens_grad, out_total, down_sum)
    up_grad = tail[:, :, qkv_cols + width + LANES :].reshape(n_exp, w_rows, n_dp, dense_rows)
    up_grad = up_grad.transpose(1, 2, 0, 3).reshape(w_rows, n_exp * dense_cols).astype(F32)
    qkv_grad = tail[:, :, :qkv_cols].reshape(n_exp, w_rows, 3, head_cols)
    small_sum = jnp.sum(tail[:, :4, qkv_cols + width : qkv_cols + width + w_rows].astype(F32), axis=0)
    return (
        out_total.astype(BF16),
        tokens_grad,
        small_sum[0],
        qkv_grad.transpose(1, 2, 0, 3).reshape(w_rows, 3 * width).astype(F32),
        jnp.sum(tail[:, :, qkv_cols : qkv_cols + width].astype(F32), axis=0),
        small_sum[1],
        small_sum[2:4].T,
        up_grad,
        down_sum.astype(F32),
        exp_up_grad[None],
        exp_down_grad[None],
    )


def solution(mesh):
    n_dp, n_exp = (mesh.shape["dp"], mesh.shape["expert"])
    fine = Mesh(mesh.devices.reshape(n_dp // 2, 2, n_exp), ("chip", "core", "expert"))
    every = ("chip", "core", "expert")
    rows = P(every, None)
    expert = P("expert", DP, None)
    return jax.shard_map(
        shards,
        mesh=fine,
        in_specs=(
            rows,
            P(every),
            rows,
            rows,
            P(every),
            rows,
            rows,
            rows,
            expert,
            expert,
            rows,
            P(DP, None),
            rows,
        ),
        out_specs=(
            rows,
            rows,
            P(every),
            rows,
            rows,
            P(every),
            rows,
            rows,
            rows,
            expert,
            expert,
        ),
        check_vma=False,
    )
```

```python
import jax
import jax.numpy as jnp
from jax import lax
from jax.experimental import pallas as pl
from jax.experimental.pallas import tpu as pltpu
from jax.sharding import Mesh
from jax.sharding import PartitionSpec as P

HEAD_DIM = 64
EPSILON = 1e-05
SCORE_SCALE = 0.125
MASK_VALUE = -1e30
F32 = jnp.float32
BF16 = jnp.bfloat16
DP = ("chip", "core")
LANES = 128
PAD = 16
TANH_SCALE = 0.7978845608028654
TANH_CUBE = 0.044715
VMEM_LIMIT = 60 << 20
FLOPS_US = 1.15e9
LAST = 0


def dot(left, right):
    return jnp.dot(left, right, preferred_element_type=F32)


def dot_rt(left, right):
    return lax.dot_general(left, right, (((1,), (1,)), ((), ())), preferred_element_type=F32)


def dot_lt(left, right):
    return lax.dot_general(left, right, (((0,), (0,)), ((), ())), preferred_element_type=F32)


def norm_parts(values):
    row_mean = jnp.mean(values, axis=-1, keepdims=True)
    centred = values - row_mean
    spread = jnp.mean(centred * centred, axis=-1, keepdims=True)
    inverse = lax.rsqrt(spread + EPSILON)
    return (centred * inverse, inverse)


def norm_back(grad, normed, inverse, gain):
    scaled = grad * gain
    return inverse * (
        scaled
        - jnp.mean(scaled, axis=-1, keepdims=True)
        - normed * jnp.mean(scaled * normed, axis=-1, keepdims=True)
    )


def after(values, *earlier):
    return lax.optimization_barrier((values,) + earlier)[0]


def swap(values, axis):
    return lax.all_to_all(values, axis, split_axis=0, concat_axis=0, tiled=True)


def share(values, axis):
    copies = lax.axis_size(axis)
    return swap(jnp.broadcast_to(values[None], (copies,) + values.shape), axis)


def turn(values, step):
    count = lax.axis_size("expert")
    return lax.ppermute(values, "expert", [(i, (i + step) % count) for i in range(count)])


def turn_all(pieces):
    return [pieces[0]] + [turn(piece, k) for k, piece in enumerate(pieces) if k]


def other_core(values):
    return lax.ppermute(values, "core", [(0, 1), (1, 0)])


def by_core(core, first, second):
    return (jnp.where(core == 0, first, second), jnp.where(core == 0, second, first))


def flip(values, bit):
    chips = range(lax.axis_size("chip"))
    return lax.ppermute(values, "chip", [(i, i ^ bit) for i in chips])


def by_bit(bit, first, second):
    return by_core(lax.axis_index("chip") & bit, first, second)


def chip_bits():
    bits = []
    while 1 << len(bits) < lax.axis_size("chip"):
        bits.append(1 << len(bits))
    return bits


def gather_small(values, axes, copies):
    count, cols = values.shape
    step = min(count, max(16, ((1 << 20) - 1) // (2 * copies * cols) // 16 * 16))
    return [
        lax.all_gather(values[k : k + step], axes, axis=0, tiled=True).reshape(copies, -1, cols)
        for k in range(0, count, step)
    ]


def sum_core(values, core):
    own, sent = by_core(core, values[:, 0], values[:, 1])
    return own.astype(F32) + other_core(sent).astype(F32)


class Fold:
    def __init__(self, pair):
        bits = chip_bits()
        count = len(pair)
        self.orders = [list(bits[:: 1 - 2 * (k % 2)]) for k in range(count)]
        self.left = [sorted(bits, reverse=True) for k in range(count)]
        self.pair = [v.reshape((2,) * len(bits) + v.shape[1:]) for v in pair]

    def send(self):
        self.keeps, self.gots = ([], [])
        for k in range(len(self.pair)):
            bit = self.orders[k].pop(0)
            at = self.left[k].index(bit)
            self.left[k].remove(bit)
            low, high = (lax.index_in_dim(self.pair[k], side, at, False) for side in (0, 1))
            keep, sent = by_bit(bit, low, high)
            self.keeps.append(keep)
            self.gots.append(flip(sent.astype(BF16), bit))

    def meet(self, *others):
        gots = lax.optimization_barrier((*self.gots, *others))
        self.pair = [
            keep.astype(F32) + got.astype(F32)
            for keep, got in zip(self.keeps, gots[: len(self.keeps)], strict=True)
        ]
        return gots[len(self.keeps) :]


def whole(shape):
    return pl.BlockSpec(shape, lambda *at: (0,) * len(shape), pipeline_mode=pl.Buffered(1))


def by_rows(tile, cols):
    return pl.BlockSpec((tile, cols), lambda t: (t, 0))


def shape_of(shape, kind):
    return jax.ShapeDtypeStruct(shape, kind)


def call(body, weight, out_shape, operands, in_specs, out_specs, grid=(1,), scratch=()):
    return pl.pallas_call(
        body,
        grid=grid,
        in_specs=in_specs,
        out_specs=out_specs,
        out_shape=out_shape,
        scratch_shapes=list(scratch),
        compiler_params=pltpu.CompilerParams(vmem_limit_bytes=VMEM_LIMIT),
        cost_estimate=pl.CostEstimate(
            flops=int(weight * FLOPS_US), bytes_accessed=0, transcendentals=0
        ),
    )(*operands)


def enter_body(x_ref, gain_ref, *refs):
    parts, (qkv_ref, attn_ref, w_ref) = (refs[:-3], refs[-3:])
    width, cols = w_ref.shape
    copies = parts[0].shape[0]
    matrix = jnp.concatenate([p[...] for p in parts], axis=1)[:, : width // copies]
    matrix = matrix.reshape(width, cols)
    w_ref[...] = matrix
    normed, unused = norm_parts(x_ref[...].astype(F32))
    attn_input = (normed * gain_ref[...]).astype(BF16)
    attn_ref[...] = attn_input
    qkv_ref[...] = dot(attn_input, matrix).astype(BF16)


def enter(inputs, gain, parts):
    group, width = inputs.shape
    cols = parts[0].shape[2]
    tile = min(512, group)
    return call(
        enter_body,
        0,
        [
            shape_of((group, cols), BF16),
            shape_of((group, width), BF16),
            shape_of((width, cols), BF16),
        ],
        [inputs, gain] + parts,
        [by_rows(tile, width), whole(gain.shape)] + [whole(p.shape) for p in parts],
        [by_rows(tile, cols), by_rows(tile, width), whole((width, cols))],
        grid=(group // tile,),
    )


def seen(split, query_axis, shape, first_query):
    query = first_query + lax.broadcasted_iota(jnp.int32, shape, query_axis)
    key = lax.broadcasted_iota(jnp.int32, shape, 1 - query_axis)
    return (query >= key) & ((query >= split) == (key >= split))


def attend_body(split_ref, q_ref, k_ref, v_ref, out_ref):
    tile, cols = q_ref.shape
    allowed = seen(split_ref[0], 0, (tile, k_ref.shape[0]), pl.program_id(1) * tile)
    for h in range(cols // HEAD_DIM):
        at = slice(h * HEAD_DIM, (h + 1) * HEAD_DIM)
        scores = dot_rt(q_ref[:, at], k_ref[:, at]) * SCORE_SCALE
        scores = jnp.where(allowed, scores, MASK_VALUE)
        weights = jnp.exp(scores - jnp.max(scores, axis=1, keepdims=True))
        probs = weights * (1.0 / jnp.sum(weights, axis=1, keepdims=True))
        result = dot(probs.astype(BF16), v_ref[:, at]).astype(BF16)
        for j in range(out_ref.shape[0]):
            out_ref[j, :, at] = result


def attend_back_body(
    split_ref, q_ref, k_ref, v_ref, grad_ref, dq_ref, dk_ref, dv_ref, dk_sum, dv_sum
):
    tile, cols = q_ref.shape
    step = pl.program_id(1)
    allowed = seen(split_ref[0], 1, (k_ref.shape[0], tile), step * tile)
    for h in range(cols // HEAD_DIM):
        at = slice(h * HEAD_DIM, (h + 1) * HEAD_DIM)
        query, keys, vals, grad = (r[:, at] for r in (q_ref, k_ref, v_ref, grad_ref))
        scores = jnp.where(allowed, dot_rt(keys, query) * SCORE_SCALE, MASK_VALUE)
        weights = jnp.exp(scores - jnp.max(scores, axis=0, keepdims=True))
        probs = weights * (1.0 / jnp.sum(weights, axis=0, keepdims=True))
        dprobs = dot_rt(vals, grad)
        delta = jnp.sum(probs * dprobs, axis=0, keepdims=True)
        dscores = (probs * (dprobs - delta)).astype(BF16)
        dq_ref[:, at] = (dot_lt(dscores, keys) * SCORE_SCALE).astype(BF16)
        dk_new = dot(dscores, query) * SCORE_SCALE
        dv_new = dot(probs.astype(BF16), grad)

        @pl.when(step == 0)
        def first():
            dk_sum[:, at] = dk_new
            dv_sum[:, at] = dv_new

        @pl.when(step > 0)
        def later():
            dk_sum[:, at] += dk_new
            dv_sum[:, at] += dv_new

    @pl.when(step == pl.num_programs(1) - 1)
    def last():
        dk_ref[...] = dk_sum[...].astype(BF16)
        dv_ref[...] = dv_sum[...].astype(BF16)


def attention_parts(qkv, head_cols):
    group = qkv.shape[0]
    cols = min(LANES, head_cols)
    pairs = head_cols // cols
    tile = min(512, group)
    if head_cols % LANES == 0:
        operands, shift = ([qkv] * 3, pairs)
    else:
        operands = [qkv[:, k * head_cols : (k + 1) * head_cols] for k in range(3)]
        shift = 0
    specs = [
        pl.BlockSpec(memory_space=pltpu.SMEM),
        pl.BlockSpec((tile, cols), lambda p, t: (t, p)),
        pl.BlockSpec((group, cols), lambda p, t: (0, shift + p)),
        pl.BlockSpec((group, cols), lambda p, t: (0, 2 * shift + p)),
    ]
    by_tile = pl.BlockSpec((tile, cols), lambda p, t: (t, p))
    by_pair = pl.BlockSpec((group, cols), lambda p, t: (0, p))
    return (operands, specs, by_tile, by_pair, (pairs, group // tile), cols)


def attend(qkv, split, head_cols, copies):
    group = qkv.shape[0]
    tile = min(512, group)
    operands, specs, unused, unused, grid, cols = attention_parts(qkv, head_cols)
    return call(
        attend_body,
        0,
        [shape_of((copies, group, head_cols), BF16)],
        [split] + operands,
        specs,
        [pl.BlockSpec((copies, tile, cols), lambda p, t: (0, t, p))],
        grid=grid,
    )[0]


def attend_back(qkv, grad, split, head_cols):
    group = qkv.shape[0]
    operands, specs, by_tile, by_pair, grid, cols = attention_parts(qkv, head_cols)
    return call(
        attend_back_body,
        20,
        [shape_of((group, head_cols), BF16)] * 3,
        [split] + operands + [grad],
        specs + [by_tile],
        [by_tile, by_pair, by_pair],
        grid=grid,
        scratch=[pltpu.VMEM((group, cols), F32)] * 2,
    )


def middle_body(att_ref, x_ref, w_ref, gain_ref, mix_ref, middle_ref, ffn_ref, coeff_ref):
    n_exp, unused, head_cols = att_ref.shape
    middle = x_ref[...].astype(F32)
    for j in range(n_exp):
        middle = middle + dot(att_ref[j], w_ref[j * head_cols : (j + 1) * head_cols])
    middle_ref[...] = middle
    normed, unused = norm_parts(middle)
    ffn_input = (normed * gain_ref[...]).astype(BF16)
    ffn_ref[...] = ffn_input
    logits = dot_rt(ffn_input, mix_ref[...])
    first, second = (logits[:, 0:1], logits[:, 1:2])
    top = jnp.maximum(first, second)
    first, second = (jnp.exp(first - top), jnp.exp(second - top))
    coeff_ref[...] = jnp.concatenate([first, second], axis=1) / (first + second)


def to_middle(attended, inputs, matrix, gain, mix):
    n_exp, group, head_cols = attended.shape
    width = matrix.shape[0]
    tile = min(512, group)
    return call(
        middle_body,
        0,
        [shape_of((group, width), F32), shape_of((group, width), BF16), shape_of((group, 2), F32)],
        [attended, inputs, matrix, gain, mix],
        [
            pl.BlockSpec((n_exp, tile, head_cols), lambda t: (0, t, 0)),
            by_rows(tile, width),
            whole(matrix.shape),
            whole(gain.shape),
            whole(mix.shape),
        ],
        [by_rows(tile, width), by_rows(tile, width), by_rows(tile, 2)],
        grid=(group // tile,),
    )


def bend(pre):
    square = pre * pre
    bent = jnp.tanh(TANH_SCALE * pre * (1.0 + TANH_CUBE * square))
    half = 0.5 * (1.0 + bent)
    slope = half + 0.5 * pre * (1.0 - bent * bent) * TANH_SCALE * (1.0 + 3.0 * TANH_CUBE * square)
    return ((pre * half).astype(BF16), slope)


def add_step(total, new):
    @pl.when(pl.program_id(0) == 0)
    def first():
        total[...] = new

    @pl.when(pl.program_id(0) > 0)
    def later():
        total[...] += new


def hidden_back(rows_in, rows_grad, up, down, din_sum):
    act, slope = bend(dot(rows_in, up))
    dpre = (slope * dot_rt(rows_grad, down)).astype(BF16)
    add_step(din_sum, dot_rt(dpre, up))
    return (act, dpre)


def fill_rows(own_ref, got_ref, rows_in, rows_grad):
    capacity = own_ref.shape[1]

    @pl.when(pl.program_id(0) == 0)
    def begin():
        rows_in[:capacity] = own_ref[0]
        rows_in[capacity:] = got_ref[0]
        rows_grad[:capacity] = own_ref[1]
        rows_grad[capacity:] = got_ref[1]


def expert_body(
    own_ref,
    got_ref,
    up_ref,
    down_ref,
    keep_ref,
    send_ref,
    act_ref,
    dpre_ref,
    rows_in,
    rows_grad,
    outs,
    dins,
):
    width = own_ref.shape[2]
    capacity = own_ref.shape[1]
    fill_rows(own_ref, got_ref, rows_in, rows_grad)
    up = up_ref[...].reshape(width, -1)
    act, dpre_ref[...] = hidden_back(rows_in[...], rows_grad[...], up, down_ref[0], dins)
    add_step(outs, dot(act, down_ref[0]))
    act_ref[...] = act

    @pl.when(pl.program_id(0) == pl.num_programs(0) - 1)
    def last():
        for k, total in enumerate((outs, dins)):
            keep_ref[k] = total[:capacity]
            send_ref[k] = total[capacity:].astype(BF16)


def expert_grad_body(own_x, got_x, own_g, got_g, act_ref, dpre_ref, grads_ref):
    width = grads_ref.shape[2]
    rows_in = jnp.concatenate([own_x[0], got_x[0]], axis=0)
    rows_grad = jnp.concatenate([own_g[0], got_g[0]], axis=0)
    dup = dot_lt(rows_in, dpre_ref[...]).astype(BF16)
    pair_rows, hidden = dup.shape
    up_rows = hidden // width * pair_rows
    for k in range(hidden // width):
        at = slice(k * pair_rows, (k + 1) * pair_rows)
        grads_ref[0, at] = dup[:, k * width : (k + 1) * width]
    grads_ref[0, up_rows:] = dot_lt(act_ref[...], rows_grad).astype(BF16)


def expert_ffn(own, got, up, down, pair_rows):
    unused, capacity, width = own.shape
    n_chip, exp_cols, unused = down.shape
    per = width // exp_cols
    count = 2 * capacity
    hidden = n_chip * exp_cols
    by_cols = pl.BlockSpec((count, exp_cols), lambda c: (0, c))
    return call(
        expert_body,
        0,
        [
            shape_of(own.shape, F32),
            shape_of(own.shape, BF16),
            shape_of((count, hidden), BF16),
            shape_of((count, hidden), BF16),
        ],
        [own, got, up, down],
        [
            whole(own.shape),
            whole(own.shape),
            pl.BlockSpec((n_chip, pair_rows, exp_cols), lambda c: (0, c // per, c % per)),
            pl.BlockSpec((1, exp_cols, width), lambda c: (c, 0, 0)),
        ],
        [whole(own.shape), whole(own.shape), by_cols, by_cols],
        grid=(n_chip,),
        scratch=[pltpu.VMEM((count, width), BF16)] * 2 + [pltpu.VMEM((count, width), F32)] * 2,
    )


def expert_grad(own, got, act, dpre, n_chip):
    unused, capacity, width = own.shape
    count, hidden = act.shape
    cols, pair_rows = (hidden // n_chip, width // n_chip)
    rows = hidden // width * pair_rows + cols
    by_width = pl.BlockSpec((1, capacity, pair_rows), lambda d: (0, 0, d))
    second = pl.BlockSpec((1, capacity, width), lambda d: (1, 0, 0))
    return call(
        expert_grad_body,
        0,
        [shape_of((n_chip, rows, width), BF16)],
        [own, got, own, got, act, dpre],
        [
            by_width,
            by_width,
            second,
            second,
            pl.BlockSpec((count, cols), lambda d: (0, d)),
            whole(dpre.shape),
        ],
        [pl.BlockSpec((1, rows, width), lambda d: (d, 0, 0))],
        grid=(n_chip,),
    )[0]


def dense_body(ex_ref, x_ref, g_ref, coeff_ref, slot_ref, up_ref, down_ref, *refs):
    outs, (pay_ref, act_ref, dpre_ref, ddense_ref, own_ref, dense, dins) = (refs[:-7], refs[-7:])
    n_exp, padded, width = pay_ref.shape
    rows = padded - PAD

    @pl.when(pl.program_id(0) == 0)
    def begin():
        grad = g_ref[...].astype(F32)
        ddense_ref[...] = (coeff_ref[:, 0:1] * grad).astype(BF16)
        shape = (own_ref.shape[1], x_ref.shape[0])
        pick = (lax.broadcasted_iota(jnp.int32, shape, 0) == slot_ref[...]).astype(F32)
        pick = pick.astype(BF16)
        own_ref[0] = dot(pick, x_ref[...]).astype(BF16)
        own_ref[1] = dot(pick, (coeff_ref[:, 1:2] * grad).astype(BF16)).astype(BF16)

    up = up_ref[...].reshape(width, -1)
    down = down_ref[...].reshape(-1, width)
    act, dpre_ref[...] = hidden_back(x_ref[...], ddense_ref[...], up, down, dins)
    act_ref[...] = act
    add_step(dense, dot(act, down))

    @pl.when(pl.program_id(0) == pl.num_programs(0) - 1)
    def last():
        for k, out_ref in enumerate(outs):
            to = lax.rem(ex_ref[0] + k, len(outs))
            at = pl.ds(pl.multiple_of(to * rows, rows), rows)
            out_ref[...] = (coeff_ref[at, 0:1] * dense[at]).astype(BF16)
        for j in range(n_exp):
            at = slice(j * rows, (j + 1) * rows)
            pay_ref[j, :rows] = dins[at].astype(BF16)
            sums = jnp.sum(g_ref[at].astype(F32) * dense[at], axis=1, keepdims=True)
            line = jnp.transpose(sums * jnp.ones((1, LANES), F32))[:PAD]
            high = line.astype(BF16).astype(F32)
            index = lax.broadcasted_iota(jnp.int32, (PAD, rows), 0)
            extra = jnp.where(index == 0, high, jnp.where(index == 1, line - high, 0.0))
            pay_ref[j, rows:] = jnp.concatenate(
                [extra, jnp.zeros((PAD, width - rows), F32)], axis=1
            ).astype(BF16)


def dense_grad_body(x_ref, g_ref, act_ref, dpre_ref, dup_ref, ddown_ref):
    dup_ref[...] = dot_lt(x_ref[...], dpre_ref[...]).astype(BF16)
    ddown_ref[...] = dot_lt(act_ref[...], g_ref[...]).astype(BF16)


def dense_ffn(ex, ffn_input, grad, coeffs, slot, capacity, weights, specs, hidden, rows):
    group, width = ffn_input.shape
    step = 2 * LANES
    count = group // rows
    operands = [ffn_input, grad, coeffs, slot]
    own = (2, capacity, width)
    padded = (count, rows + PAD, width)
    by_cols = pl.BlockSpec((group, step), lambda c: (0, c))
    return call(
        dense_body,
        0,
        [shape_of((rows, width), BF16)] * count
        + [shape_of(padded, BF16)]
        + [shape_of((group, hidden), BF16)] * 2
        + [shape_of((group, width), BF16), shape_of(own, BF16)],
        [ex] + operands + weights,
        [pl.BlockSpec(memory_space=pltpu.SMEM)] + [whole(o.shape) for o in operands] + specs,
        [whole((rows, width))] * count
        + [whole(padded), by_cols, by_cols, whole((group, width)), whole(own)],
        grid=(hidden // step,),
        scratch=[pltpu.VMEM((group, width), F32)] * 2,
    )


def dense_pack_body(core_ref, x_ref, g_ref, act_ref, dpre_ref, keep_ref, send_ref):
    n_chip, unused, block, unused = keep_ref.shape
    step = act_ref.shape[1]
    chunk = pl.program_id(0)
    left = pl.ds(pl.multiple_of(chunk * step, step), step)
    first_core = core_ref[0] == 0
    dup = dot_lt(x_ref[...], dpre_ref[...]).astype(BF16).reshape(n_chip, 2, block, step)
    ddown = dot_lt(act_ref[...], g_ref[...]).astype(BF16)
    keep_ref[:, 0, :, left] = jnp.where(first_core, dup[:, 0], dup[:, 1])
    send_ref[:, 0, :, left] = jnp.where(first_core, dup[:, 1], dup[:, 0])
    at = pl.ds(chunk, 1)
    keep_ref[at, 1] = jnp.where(first_core, ddown[:block], ddown[block:])[None]
    send_ref[at, 1] = jnp.where(first_core, ddown[block:], ddown[:block])[None]


def dense_split(core, ffn_input, ddense, act, dpre, shape):
    group, step = (ffn_input.shape[0], 2 * LANES)
    by_cols = pl.BlockSpec((group, step), lambda c: (0, c))
    return call(
        dense_pack_body,
        0,
        [shape_of(shape, BF16)] * 2,
        [core, ffn_input, ddense, act, dpre],
        [
            pl.BlockSpec(memory_space=pltpu.SMEM),
            whole(ffn_input.shape),
            whole(ddense.shape),
            by_cols,
            by_cols,
        ],
        [whole(shape)] * 2,
        grid=(act.shape[1] // step,),
    )


def dense_grad(ffn_input, ddense, act, dpre):
    group, width = ffn_input.shape
    hidden = act.shape[1]
    step = 2 * LANES
    by_cols = pl.BlockSpec((group, step), lambda c: (0, c))
    return call(
        dense_grad_body,
        0,
        [shape_of((width, hidden), BF16), shape_of((hidden, width), BF16)],
        [ffn_input, ddense, act, dpre],
        [whole(ffn_input.shape), whole(ddense.shape), by_cols, by_cols],
        [
            pl.BlockSpec((width, step), lambda c: (0, c)),
            pl.BlockSpec((step, width), lambda c: (c, 0)),
        ],
        grid=(hidden // step,),
    )


def middle_back_body(
    ex_ref, pay_ref, slot_ref, middle_ref, coeff_ref, g_ref, gain_ref, mix_ref, w_ref, *refs
):
    rets, (dmid_ref, low_ref, datt_ref, small_ref, base_ref) = (refs[:-5], refs[-5:])
    rows, width = middle_ref.shape
    n_exp = pay_ref.shape[0]
    head_cols = datt_ref.shape[2]
    total = pay_ref[0].astype(F32)
    for j in range(1, n_exp):
        total = total + pay_ref[j].astype(F32)
    capacity = rets[0].shape[1]
    exp_rows, exp_din = (jnp.zeros((rows, width), F32) for k in range(2))
    index = lax.broadcasted_iota(jnp.int32, (rows, capacity), 1)
    for k, ret_ref in enumerate(rets):
        source = lax.rem(ex_ref[0] + n_exp - k, n_exp)
        place = (index + source * capacity == slot_ref[...]).astype(F32).astype(BF16)
        exp_rows = exp_rows + dot(place, ret_ref[0])
        exp_din = exp_din + dot(place, ret_ref[1])
    dffn = total[:rows] + exp_din
    lines = jnp.concatenate([total[rows:, :rows], jnp.zeros((rows - PAD, rows), F32)], axis=0)
    lines = jnp.transpose(lines)
    grad = g_ref[...].astype(F32)
    dcoeff = [lines[:, 0:1] + lines[:, 1:2], jnp.sum(grad * exp_rows, axis=1, keepdims=True)]
    coeff = [coeff_ref[:, k : k + 1] for k in range(2)]
    base_ref[...] = middle_ref[...] + coeff[1] * exp_rows
    inner = coeff[0] * dcoeff[0] + coeff[1] * dcoeff[1]
    dlogit = [(c * (d - inner)).astype(BF16).astype(F32) for c, d in zip(coeff, dcoeff, strict=True)]
    mix = mix_ref[...].astype(F32)
    dffn = dffn + dlogit[0] * mix[0:1] + dlogit[1] * mix[1:2]
    normed, inverse = norm_parts(middle_ref[...])
    gain = gain_ref[...]
    dmiddle = grad + norm_back(dffn, normed, inverse, gain)
    dmid_ref[...] = dmiddle
    low = dmiddle.astype(BF16)
    low_ref[...] = low
    datt = dot_rt(low, w_ref[...]).astype(BF16)
    for j in range(n_exp):
        datt_ref[j] = datt[:, j * head_cols : (j + 1) * head_cols]
    lane = lax.broadcasted_iota(jnp.int32, (rows, LANES), 1)
    pair = jnp.where(lane == 0, dlogit[0], jnp.where(lane == 1, dlogit[1], 0.0)).astype(BF16)
    dmix = dot_lt(pair, (normed * gain).astype(BF16))
    dgain = jnp.sum(dffn * normed, axis=0, keepdims=True)
    nothing = jnp.zeros((1, width), F32)
    small_ref[...] = jnp.concatenate([nothing, dgain, dmix[:2], jnp.zeros((4, width), F32)], axis=0)


def middle_back(ex, arrived, returned, slot, middle, coeffs, grad, gain, mix, matrix, head_cols):
    rows, width = middle.shape
    n_exp = arrived.shape[0]
    operands = [arrived, slot, middle, coeffs, grad, gain, mix, matrix] + list(returned)
    shapes = [
        shape_of((rows, width), F32),
        shape_of((rows, width), BF16),
        shape_of((n_exp, rows, head_cols), BF16),
        shape_of((8, width), F32),
        shape_of((rows, width), F32),
    ]
    return call(
        middle_back_body,
        0,
        shapes,
        [ex] + operands,
        [pl.BlockSpec(memory_space=pltpu.SMEM)] + [whole(o.shape) for o in operands],
        [whole(o.shape) for o in shapes],
    )


def split_cores(core_ref, grads, keep_ref, send_ref):
    n_chip, block = keep_ref.shape[:2]
    grads = grads.reshape(n_chip, 2, block, grads.shape[-1])
    first_core = core_ref[0] == 0
    keep_ref[...] = jnp.where(first_core, grads[:, 0], grads[:, 1])
    send_ref[...] = jnp.where(first_core, grads[:, 1], grads[:, 0])


def out_grad_body(core_ref, att_ref, low_ref, keep_ref, send_ref):
    grads = [dot_lt(att_ref[j], low_ref[...]).astype(BF16) for j in range(att_ref.shape[0])]
    split_cores(core_ref, jnp.concatenate(grads, axis=0), keep_ref, send_ref)


def attn_input_back_body(ex_ref, dq_ref, dk_ref, dv_ref, w_ref, *pays):
    rows = pays[0].shape[0]
    for k, pay_ref in enumerate(pays):
        to = lax.rem(ex_ref[0] + k, len(pays))
        at = pl.ds(pl.multiple_of(to * rows, rows), rows)
        grads = jnp.concatenate([dq_ref[at], dk_ref[at], dv_ref[at]], axis=1)
        pay_ref[...] = dot_rt(grads, w_ref[...]).astype(BF16)


def qkv_grad_body(
    core_ref, x_ref, w_ref, gain_ref, small_ref, dq_ref, dk_ref, dv_ref, keep_ref, send_ref
):
    n_chip, padded, cols = keep_ref.shape
    block = padded - PAD
    rows_in = x_ref[...]
    grads = jnp.concatenate([dot_lt(rows_in, r[...]) for r in (dq_ref, dk_ref, dv_ref)], axis=1)
    width = grads.shape[0]
    dgain = jnp.sum(grads * w_ref[...].astype(F32), axis=1, keepdims=True)
    dgain = jnp.transpose(dgain * jnp.ones((1, LANES), F32))[:8] / gain_ref[...]
    index = lax.broadcasted_iota(jnp.int32, (8, width), 0)
    small = jnp.where(index == 0, dgain, small_ref[...])
    small = jnp.concatenate([small, jnp.zeros((PAD - 8, width), F32)], axis=0)
    first_core = core_ref[0] == 0
    for chip in range(n_chip):
        pair = []
        for core in range(2):
            low = (2 * chip + core) * block
            edge = jnp.concatenate(
                [small[:, low : low + block], jnp.zeros((PAD, cols - block), F32)], axis=1
            )
            pair.append(jnp.concatenate([grads[low : low + block], edge], axis=0).astype(BF16))
        keep_ref[chip] = jnp.where(first_core, pair[0], pair[1])
        send_ref[chip] = jnp.where(first_core, pair[1], pair[0])


def scalar_call(body, shapes, scalar, operands, weight=0):
    return call(
        body,
        weight,
        shapes,
        [scalar] + operands,
        [pl.BlockSpec(memory_space=pltpu.SMEM)] + [whole(o.shape) for o in operands],
        [whole(o.shape) for o in shapes],
    )


def expert_end_body(core_ref, own_ref, got_ref, down_ref, up_out, down_out):
    cols = down_ref.shape[0]
    per = own_ref.shape[2] // cols
    first_core = core_ref[0] == 0
    for k in range(own_ref.shape[0] * per):
        at = slice(k % per * cols, (k % per + 1) * cols)
        mine, theirs = (r[k // per, :, at].astype(F32) for r in (own_ref, got_ref))
        low = 2 * k * cols
        up_out[:, low : low + cols] = jnp.where(first_core, mine, theirs)
        up_out[:, low + cols : low + 2 * cols] = jnp.where(first_core, theirs, mine)
    down_out[...] = down_ref[...].astype(F32)


def leave_body(x_ref, gain_ref, dmid_ref, *refs):
    pays, out_ref = (refs[:-1], refs[-1])
    dattn = pays[0][...].astype(F32)
    for pay_ref in pays[1:]:
        dattn = dattn + pay_ref[...].astype(F32)
    normed, inverse = norm_parts(x_ref[...].astype(F32))
    out_ref[...] = (dmid_ref[...] + norm_back(dattn, normed, inverse, gain_ref[...])).astype(BF16)


def simple(body, weight, shape, operands):
    return call(
        body,
        weight,
        [shape],
        operands,
        [whole(o.shape) for o in operands],
        [whole(shape.shape)],
    )[0]


def shards(
    tokens,
    first_gain,
    w_qkv,
    w_out,
    second_gain,
    w_mix,
    w_up,
    w_down,
    expert_up,
    expert_down,
    expert_ids,
    doc_lengths,
    out_grad,
):
    rows, width = tokens.shape
    n_chip, n_core, n_exp = (lax.axis_size(a) for a in ("chip", "core", "expert"))
    n_dp = n_chip * n_core
    group = rows * n_exp
    head_cols = width // n_exp
    qkv_cols = 3 * head_cols
    w_rows = w_qkv.shape[0]
    block = n_exp * w_rows
    dense_rows = w_down.shape[0]
    dense_cols = n_dp * dense_rows
    exp_rows = expert_up.shape[1]
    exp_cols = expert_down.shape[1]
    ex = lax.axis_index("expert")
    ex_line = jnp.full((1,), ex, jnp.int32)
    core = lax.axis_index("core")
    core_line = jnp.full((1,), core, jnp.int32)
    share_cap = max(2, 5 * rows // (4 * n_exp))
    capacity = n_exp * share_cap
    bits = chip_bits()

    exp_split = (
        expert_up[0]
        .reshape(exp_rows, n_chip, n_core, exp_cols)
        .transpose(2, 0, 1, 3)
        .reshape(n_core, exp_rows, n_chip * exp_cols)
    )
    own_half, sent_half = by_core(core, exp_split[0], exp_split[1])
    chip_up = jnp.concatenate(by_core(core, own_half, other_core(sent_half)), axis=0)
    pair_rows = n_core * exp_rows
    n_block = n_chip * exp_cols // width
    up_rows = n_block * pair_rows
    chip_up = chip_up.reshape(pair_rows, n_block, width).transpose(1, 0, 2)
    down_all = lax.all_gather(expert_down[0], "chip", axis=0, tiled=True)
    down_all = down_all.reshape(n_chip, exp_cols, width)

    qkv_blocks = w_qkv.reshape(w_rows, 3, n_exp, head_cols).transpose(2, 0, 1, 3)
    small = jnp.stack([first_gain, second_gain, w_mix[:, 0], w_mix[:, 1]])
    small = jnp.concatenate(
        [
            jnp.pad(small, ((0, w_rows - 4), (0, LANES - w_rows))),
            jnp.pad(expert_ids[:, 0].astype(BF16)[None], ((0, w_rows - 1), (0, LANES - rows))),
        ],
        axis=1,
    )
    up_blocks = w_up.reshape(w_rows, n_dp, n_exp, dense_rows).transpose(2, 0, 1, 3)
    others = jnp.concatenate([w_out, small], axis=1)
    dealt = swap(
        jnp.concatenate(
            [
                qkv_blocks.reshape(n_exp, w_rows, qkv_cols),
                up_blocks.reshape(n_exp, w_rows, dense_cols),
                jnp.broadcast_to(others[None], (n_exp,) + others.shape),
            ],
            axis=2,
        ),
        "expert",
    )
    at = [qkv_cols, qkv_cols + dense_cols, qkv_cols + dense_cols + width]
    up_own = dealt[:, :, at[0] : at[1]].reshape(block, dense_cols)
    out_own = dealt[:, :, at[1] : at[2]].reshape(block, width)
    chip_up = chip_up.reshape(up_rows, width)
    grad_copies = jnp.broadcast_to(out_grad[None], (n_exp,) + out_grad.shape)
    dealt, chip_up, grad_copies = lax.optimization_barrier((dealt, chip_up, grad_copies))
    choice = after(dealt[:, 0, at[2] + LANES : at[2] + LANES + rows].astype(F32)).astype(jnp.int32)
    small = dealt[:, :4, at[2] : at[2] + w_rows].transpose(1, 0, 2).reshape(4, block)
    first_own = jnp.concatenate(
        [
            dealt[:, :, :qkv_cols].reshape(block, qkv_cols),
            jnp.pad(small, ((0, 4), (0, qkv_cols - block))),
        ]
    )
    group_tokens = share(after(tokens, dealt), "expert")
    first_parts = gather_small(first_own, DP, n_dp)
    small = first_parts[-1][:, -8:-4, :block].transpose(1, 0, 2).reshape(4, width)
    gain_one = small[0:1].astype(F32)
    gain_two = small[1:2].astype(F32)
    mix_rows = jnp.pad(small[2:4], ((0, PAD - 2), (0, 0)))

    group_tokens = after(group_tokens, first_parts, gain_one)
    inputs = group_tokens.reshape(group, width)
    step = 2 * LANES
    if dense_cols == width and dense_rows == block:
        dense_pack = after(jnp.concatenate([out_own, up_own, w_down], axis=0), inputs, down_all)
        dense_all = lax.all_gather(dense_pack, DP, axis=0, tiled=True)
        dense_all = dense_all.reshape(n_dp, 3, block, width)
        out_matrix = dense_all[:, 0].reshape(width, width)
        up_matrix = down_matrix = dense_all
        up_spec = pl.BlockSpec((n_dp, 1, block, step), lambda c: (0, 1, 0, c))
        down_spec = pl.BlockSpec((step // block, 1, block, width), lambda c: (c, 2, 0, 0))
    else:
        out_matrix, up_matrix, down_matrix = (
            lax.all_gather(w, DP, axis=0, tiled=True) for w in (out_own, up_own, w_down)
        )
        up_spec = pl.BlockSpec((width, step), lambda c: (0, c))
        down_spec = pl.BlockSpec((step, width), lambda c: (c, 0))
    chip_up = after(chip_up, inputs)
    up_all = lax.all_gather(chip_up, "chip", axis=0, tiled=True)
    up_all = up_all.reshape(n_chip, up_rows, width)

    grad_all = swap(after(grad_copies, inputs), "expert").reshape(group, width)

    qkv, attn_input, qkv_matrix = enter(inputs, gain_one, first_parts)
    doc_split = doc_lengths[0, :1]
    attended_own = attend(qkv, doc_split, head_cols, n_exp)
    attended_own, grad_all = lax.optimization_barrier((attended_own, grad_all))
    attended_all = swap(attended_own, "expert")
    same = (choice[:, :, None] == choice[:, None, :]).astype(jnp.int32)
    earlier = jnp.arange(rows)[None, None, :] < jnp.arange(rows)[None, :, None]
    rank = jnp.sum(jnp.where(earlier, same, 0), axis=2)
    first_slot = jnp.arange(n_exp, dtype=jnp.int32)[:, None] * share_cap
    slot = jnp.where(choice == ex, first_slot + rank, -1).reshape(1, group)
    slot_own = lax.dynamic_slice_in_dim(choice * share_cap + rank, ex, 1, 0).reshape(rows, 1)
    slot, slot_own = lax.optimization_barrier((slot, slot_own))
    attended_all = after(attended_all, out_matrix, slot)
    middle, ffn_input, coeffs = to_middle(attended_all, inputs, out_matrix, gain_two, mix_rows)


    weights, specs = ([up_matrix, down_matrix], [up_spec, down_spec])
    *out_parts, payload, dense_act, dense_dpre, ddense, own_rows = dense_ffn(
        ex_line, ffn_input, grad_all, coeffs, slot, capacity, weights, specs, dense_cols, rows
    )
    arrived = swap(payload, "expert")
    joined = dense_cols == width and dense_rows == block and step == 2 * block
    if joined:
        shape = (n_chip, 2, block, width)
        grads = dense_split(core_line, ffn_input, ddense, dense_act, dense_dpre, shape)
    else:
        grads = dense_grad(ffn_input, ddense, dense_act, dense_dpre)
    got_rows, *grads = lax.optimization_barrier((other_core(own_rows), *grads))
    if joined:
        dense_core = (grads[0].astype(F32) + other_core(grads[1]).astype(F32)).astype(BF16)
        got_rows, dense_core = lax.optimization_barrier((got_rows, dense_core))
        dense_sum = lax.psum_scatter(
            dense_core.reshape(-1, width), "chip", scatter_dimension=0, tiled=True
        )
        up_sum, down_sum = (dense_sum[:block], dense_sum[block:])
    else:
        up_sum, down_sum = (
            lax.psum_scatter(g, DP, scatter_dimension=0, tiled=True) for g in grads
        )
    exp_keep, exp_send, exp_act, exp_dpre = expert_ffn(
        own_rows, got_rows, up_all, down_all, pair_rows
    )
    exp_back = other_core(exp_send)
    returned = []
    for k in range(n_exp):
        low = lax.rem(ex + k, n_exp) * share_cap
        piece = [lax.dynamic_slice_in_dim(v, low, share_cap, 1) for v in (exp_keep, exp_back)]
        returned.append((piece[0] + piece[1].astype(F32)).astype(BF16))
    exp_grads = expert_grad(
        own_rows, got_rows, exp_act, exp_dpre, n_chip
    )
    arrived, exp_grads, *returned = lax.optimization_barrier((arrived, exp_grads, *returned))
    returned = turn_all(returned)
    exp_sum = lax.psum_scatter(
        exp_grads.reshape(-1, width), "chip", scatter_dimension=0, tiled=True
    )

    def mine(values, size=rows):
        return lax.dynamic_slice_in_dim(values, ex * size, size, 0)

    middle_own, coeffs_own = (mine(middle), mine(coeffs))
    att_own = lax.dynamic_slice_in_dim(attended_all, ex * rows, rows, 1)
    returned[0] = after(returned[0], middle_own, coeffs_own, att_own)
    dmiddle, dmid_low, datt, small_two, out_base = middle_back(
        ex_line,
        arrived,
        returned,
        slot_own,
        middle_own,
        coeffs_own,
        out_grad,
        gain_two,
        mix_rows,
        out_matrix,
        head_cols,
    )
    dattended = swap(datt, "expert")
    out_keep, out_send = scalar_call(
        out_grad_body,
        [shape_of((n_chip, block, width), BF16)] * 2,
        core_line,
        [att_own, dmid_low],
    )
    dattended, out_keep, out_send = lax.optimization_barrier((dattended, out_keep, out_send))
    dattended = dattended.reshape(group, head_cols)
    out_sums = turn_all([after(piece, dattended) for piece in out_parts])
    out_core = out_keep.astype(F32) + other_core(out_send).astype(F32)
    out_fold = Fold((out_core,))
    out_fold.send()

    dparts = attend_back(qkv, dattended, doc_split, head_cols)
    qkv_shape = shape_of((n_chip, block + PAD, qkv_cols), BF16)
    qkv_keep, qkv_send = scalar_call(
        qkv_grad_body,
        [qkv_shape] * 2,
        core_line,
        [attn_input, qkv_matrix, gain_one, small_two] + list(dparts),
    )
    dparts = [after(dparts[0], qkv_keep), dparts[1], dparts[2]]
    dattn_parts = scalar_call(
        attn_input_back_body,
        [shape_of((rows, width), BF16)] * n_exp,
        ex_line,
        dparts + [qkv_matrix],
    )
    met = out_fold.meet(*dattn_parts, *out_sums)
    dattn_parts, out_sums = (met[:n_exp], met[n_exp:])
    dattn = turn_all(dattn_parts)
    qkv_send = after(qkv_send, dattn_parts[0])
    qkv_core = qkv_keep.astype(F32) + other_core(qkv_send).astype(F32)
    half = qkv_cols // 2
    halves = (qkv_core,)
    if half % LANES == 0:
        halves = (qkv_core[..., :half], qkv_core[..., half:])
    fold = Fold(halves)
    fold.send()
    while out_fold.orders[0]:
        out_fold.send()
        out_fold.meet()
    fold.meet()
    while fold.orders[0]:
        fold.send()
        dattn = fold.meet(*dattn)
    out_weight_sum, qkv_sum = (out_fold.pair[0], jnp.concatenate(fold.pair, axis=-1))
    out_total = out_base
    for piece in out_sums:
        out_total = out_total + piece.astype(F32)
    small_sum = qkv_sum[block : block + 4, :block].reshape(4, n_exp, w_rows).transpose(1, 0, 2)
    small_sum = jnp.pad(small_sum, ((0, 0), (0, w_rows - 4), (0, LANES - w_rows)))
    tail = jnp.concatenate(
        [
            qkv_sum[:block].reshape(n_exp, w_rows, qkv_cols),
            out_weight_sum.reshape(n_exp, w_rows, width),
            small_sum,
            up_sum.astype(F32).reshape(n_exp, w_rows, dense_cols),
        ],
        axis=2,
    ).astype(BF16)
    tail_sent = after(tail, *dattn)
    tail = swap(tail_sent, "expert")
    tokens_grad = simple(
        leave_body, LAST, shape_of((rows, width), BF16), [tokens, gain_one, dmiddle] + list(dattn)
    )

    exp_sum = after(exp_sum, tail_sent)
    up_exp_sum = exp_sum[:up_rows].reshape(n_block, n_core, exp_rows, width)
    own_exp = lax.dynamic_index_in_dim(up_exp_sum, core, 1, False)
    sent_exp = lax.dynamic_index_in_dim(up_exp_sum, 1 - core, 1, False)
    exp_up_grad, exp_down_grad = scalar_call(
        expert_end_body,
        [shape_of((exp_rows, n_dp * exp_cols), F32), shape_of((exp_cols, width), F32)],
        core_line,
        [own_exp, other_core(sent_exp), exp_sum[up_rows:]],
    )
    tail = after(tail, exp_up_grad, exp_down_grad, tokens_grad, out_total, down_sum)
    up_grad = tail[:, :, qkv_cols + width + LANES :].reshape(n_exp, w_rows, n_dp, dense_rows)
    up_grad = up_grad.transpose(1, 2, 0, 3).reshape(w_rows, n_exp * dense_cols).astype(F32)
    qkv_grad = tail[:, :, :qkv_cols].reshape(n_exp, w_rows, 3, head_cols)
    small_sum = jnp.sum(tail[:, :4, qkv_cols + width : qkv_cols + width + w_rows].astype(F32), axis=0)
    return (
        out_total.astype(BF16),
        tokens_grad,
        small_sum[0],
        qkv_grad.transpose(1, 2, 0, 3).reshape(w_rows, 3 * width).astype(F32),
        jnp.sum(tail[:, :, qkv_cols : qkv_cols + width].astype(F32), axis=0),
        small_sum[1],
        small_sum[2:4].T,
        up_grad,
        down_sum.astype(F32),
        exp_up_grad[None],
        exp_down_grad[None],
    )


def solution(mesh):
    n_dp, n_exp = (mesh.shape["dp"], mesh.shape["expert"])
    fine = Mesh(mesh.devices.reshape(n_dp // 2, 2, n_exp), ("chip", "core", "expert"))
    every = ("chip", "core", "expert")
    rows = P(every, None)
    expert = P("expert", DP, None)
    return jax.shard_map(
        shards,
        mesh=fine,
        in_specs=(
            rows,
            P(every),
            rows,
            rows,
            P(every),
            rows,
            rows,
            rows,
            expert,
            expert,
            rows,
            P(DP, None),
            rows,
        ),
        out_specs=(
            rows,
            rows,
            P(every),
            rows,
            rows,
            P(every),
            rows,
            rows,
            rows,
            expert,
            expert,
        ),
        check_vma=False,
    )
```

```python
import jax
import jax.numpy as jnp
from jax import lax
from jax.experimental import pallas as pl
from jax.experimental.pallas import tpu as pltpu
from jax.sharding import Mesh
from jax.sharding import PartitionSpec as P

HEAD_DIM = 64
EPSILON = 1e-05
SCORE_SCALE = 0.125
MASK_VALUE = -1e30
F32 = jnp.float32
BF16 = jnp.bfloat16
DP = ("chip", "core")
LANES = 128
PAD = 16
TANH_SCALE = 0.7978845608028654
TANH_CUBE = 0.044715
VMEM_LIMIT = 60 << 20
FLOPS_US = 1.15e9
LAST = 0


def dot(left, right):
    return jnp.dot(left, right, preferred_element_type=F32)


def dot_rt(left, right):
    return lax.dot_general(left, right, (((1,), (1,)), ((), ())), preferred_element_type=F32)


def dot_lt(left, right):
    return lax.dot_general(left, right, (((0,), (0,)), ((), ())), preferred_element_type=F32)


def norm_parts(values):
    row_mean = jnp.mean(values, axis=-1, keepdims=True)
    centred = values - row_mean
    spread = jnp.mean(centred * centred, axis=-1, keepdims=True)
    inverse = lax.rsqrt(spread + EPSILON)
    return (centred * inverse, inverse)


def norm_back(grad, normed, inverse, gain):
    scaled = grad * gain
    return inverse * (
        scaled
        - jnp.mean(scaled, axis=-1, keepdims=True)
        - normed * jnp.mean(scaled * normed, axis=-1, keepdims=True)
    )


def after(values, *earlier):
    return lax.optimization_barrier((values,) + earlier)[0]


def swap(values, axis):
    return lax.all_to_all(values, axis, split_axis=0, concat_axis=0, tiled=True)


def share(values, axis):
    copies = lax.axis_size(axis)
    return swap(jnp.broadcast_to(values[None], (copies,) + values.shape), axis)


def turn(values, step):
    count = lax.axis_size("expert")
    return lax.ppermute(values, "expert", [(i, (i + step) % count) for i in range(count)])


def turn_all(pieces):
    return [pieces[0]] + [turn(piece, k) for k, piece in enumerate(pieces) if k]


def other_core(values):
    return lax.ppermute(values, "core", [(0, 1), (1, 0)])


def by_core(core, first, second):
    return (jnp.where(core == 0, first, second), jnp.where(core == 0, second, first))


def flip(values, bit):
    chips = range(lax.axis_size("chip"))
    return lax.ppermute(values, "chip", [(i, i ^ bit) for i in chips])


def by_bit(bit, first, second):
    return by_core(lax.axis_index("chip") & bit, first, second)


def chip_bits():
    bits = []
    while 1 << len(bits) < lax.axis_size("chip"):
        bits.append(1 << len(bits))
    return bits


def gather_small(values, axes, copies):
    count, cols = values.shape
    step = min(count, max(16, ((1 << 20) - 1) // (2 * copies * cols) // 16 * 16))
    return [
        lax.all_gather(values[k : k + step], axes, axis=0, tiled=True).reshape(copies, -1, cols)
        for k in range(0, count, step)
    ]


def sum_core(values, core):
    own, sent = by_core(core, values[:, 0], values[:, 1])
    return own.astype(F32) + other_core(sent).astype(F32)


class Fold:
    def __init__(self, pair):
        bits = chip_bits()
        count = len(pair)
        self.orders = [list(bits[:: 1 - 2 * (k % 2)]) for k in range(count)]
        self.left = [sorted(bits, reverse=True) for k in range(count)]
        self.pair = [v.reshape((2,) * len(bits) + v.shape[1:]) for v in pair]

    def send(self):
        self.keeps, self.gots = ([], [])
        for k in range(len(self.pair)):
            bit = self.orders[k].pop(0)
            at = self.left[k].index(bit)
            self.left[k].remove(bit)
            low, high = (lax.index_in_dim(self.pair[k], side, at, False) for side in (0, 1))
            keep, sent = by_bit(bit, low, high)
            self.keeps.append(keep)
            self.gots.append(flip(sent.astype(BF16), bit))

    def meet(self, *others):
        gots = lax.optimization_barrier((*self.gots, *others))
        self.pair = [
            keep.astype(F32) + got.astype(F32)
            for keep, got in zip(self.keeps, gots[: len(self.keeps)], strict=True)
        ]
        return gots[len(self.keeps) :]


def whole(shape):
    return pl.BlockSpec(shape, lambda *at: (0,) * len(shape), pipeline_mode=pl.Buffered(1))


def by_rows(tile, cols):
    return pl.BlockSpec((tile, cols), lambda t: (t, 0))


def shape_of(shape, kind):
    return jax.ShapeDtypeStruct(shape, kind)


def call(body, weight, out_shape, operands, in_specs, out_specs, grid=(1,), scratch=()):
    return pl.pallas_call(
        body,
        grid=grid,
        in_specs=in_specs,
        out_specs=out_specs,
        out_shape=out_shape,
        scratch_shapes=list(scratch),
        compiler_params=pltpu.CompilerParams(vmem_limit_bytes=VMEM_LIMIT),
        cost_estimate=pl.CostEstimate(
            flops=int(weight * FLOPS_US), bytes_accessed=0, transcendentals=0
        ),
    )(*operands)


def enter_body(x_ref, gain_ref, *refs):
    parts, (qkv_ref, attn_ref, w_ref) = (refs[:-3], refs[-3:])
    width, cols = w_ref.shape
    copies = parts[0].shape[0]
    matrix = jnp.concatenate([p[...] for p in parts], axis=1)[:, : width // copies]
    matrix = matrix.reshape(width, cols)
    w_ref[...] = matrix
    normed, unused = norm_parts(x_ref[...].astype(F32))
    attn_input = (normed * gain_ref[...]).astype(BF16)
    attn_ref[...] = attn_input
    qkv_ref[...] = dot(attn_input, matrix).astype(BF16)


def enter(inputs, gain, parts):
    group, width = inputs.shape
    cols = parts[0].shape[2]
    tile = min(512, group)
    return call(
        enter_body,
        0,
        [
            shape_of((group, cols), BF16),
            shape_of((group, width), BF16),
            shape_of((width, cols), BF16),
        ],
        [inputs, gain] + parts,
        [by_rows(tile, width), whole(gain.shape)] + [whole(p.shape) for p in parts],
        [by_rows(tile, cols), by_rows(tile, width), whole((width, cols))],
        grid=(group // tile,),
    )


def seen(split, query_axis, shape, first_query):
    query = first_query + lax.broadcasted_iota(jnp.int32, shape, query_axis)
    key = lax.broadcasted_iota(jnp.int32, shape, 1 - query_axis)
    return (query >= key) & ((query >= split) == (key >= split))


def attend_body(split_ref, q_ref, k_ref, v_ref, out_ref):
    tile, cols = q_ref.shape
    allowed = seen(split_ref[0], 0, (tile, k_ref.shape[0]), pl.program_id(1) * tile)
    for h in range(cols // HEAD_DIM):
        at = slice(h * HEAD_DIM, (h + 1) * HEAD_DIM)
        scores = dot_rt(q_ref[:, at], k_ref[:, at]) * SCORE_SCALE
        scores = jnp.where(allowed, scores, MASK_VALUE)
        weights = jnp.exp(scores - jnp.max(scores, axis=1, keepdims=True))
        probs = weights * (1.0 / jnp.sum(weights, axis=1, keepdims=True))
        result = dot(probs.astype(BF16), v_ref[:, at]).astype(BF16)
        for j in range(out_ref.shape[0]):
            out_ref[j, :, at] = result


def attend_back_body(
    split_ref, q_ref, k_ref, v_ref, grad_ref, dq_ref, dk_ref, dv_ref, dk_sum, dv_sum
):
    tile, cols = q_ref.shape
    step = pl.program_id(1)
    allowed = seen(split_ref[0], 1, (k_ref.shape[0], tile), step * tile)
    for h in range(cols // HEAD_DIM):
        at = slice(h * HEAD_DIM, (h + 1) * HEAD_DIM)
        query, keys, vals, grad = (r[:, at] for r in (q_ref, k_ref, v_ref, grad_ref))
        scores = jnp.where(allowed, dot_rt(keys, query) * SCORE_SCALE, MASK_VALUE)
        weights = jnp.exp(scores - jnp.max(scores, axis=0, keepdims=True))
        probs = weights * (1.0 / jnp.sum(weights, axis=0, keepdims=True))
        dprobs = dot_rt(vals, grad)
        delta = jnp.sum(probs * dprobs, axis=0, keepdims=True)
        dscores = (probs * (dprobs - delta)).astype(BF16)
        dq_ref[:, at] = (dot_lt(dscores, keys) * SCORE_SCALE).astype(BF16)
        dk_new = dot(dscores, query) * SCORE_SCALE
        dv_new = dot(probs.astype(BF16), grad)

        @pl.when(step == 0)
        def first():
            dk_sum[:, at] = dk_new
            dv_sum[:, at] = dv_new

        @pl.when(step > 0)
        def later():
            dk_sum[:, at] += dk_new
            dv_sum[:, at] += dv_new

    @pl.when(step == pl.num_programs(1) - 1)
    def last():
        dk_ref[...] = dk_sum[...].astype(BF16)
        dv_ref[...] = dv_sum[...].astype(BF16)


def attention_parts(qkv, head_cols):
    group = qkv.shape[0]
    cols = min(LANES, head_cols)
    pairs = head_cols // cols
    tile = min(512, group)
    if head_cols % LANES == 0:
        operands, shift = ([qkv] * 3, pairs)
    else:
        operands = [qkv[:, k * head_cols : (k + 1) * head_cols] for k in range(3)]
        shift = 0
    specs = [
        pl.BlockSpec(memory_space=pltpu.SMEM),
        pl.BlockSpec((tile, cols), lambda p, t: (t, p)),
        pl.BlockSpec((group, cols), lambda p, t: (0, shift + p)),
        pl.BlockSpec((group, cols), lambda p, t: (0, 2 * shift + p)),
    ]
    by_tile = pl.BlockSpec((tile, cols), lambda p, t: (t, p))
    by_pair = pl.BlockSpec((group, cols), lambda p, t: (0, p))
    return (operands, specs, by_tile, by_pair, (pairs, group // tile), cols)


def attend(qkv, split, head_cols, copies):
    group = qkv.shape[0]
    tile = min(512, group)
    operands, specs, unused, unused, grid, cols = attention_parts(qkv, head_cols)
    return call(
        attend_body,
        0,
        [shape_of((copies, group, head_cols), BF16)],
        [split] + operands,
        specs,
        [pl.BlockSpec((copies, tile, cols), lambda p, t: (0, t, p))],
        grid=grid,
    )[0]


def attend_back(qkv, grad, split, head_cols):
    group = qkv.shape[0]
    operands, specs, by_tile, by_pair, grid, cols = attention_parts(qkv, head_cols)
    return call(
        attend_back_body,
        20,
        [shape_of((group, head_cols), BF16)] * 3,
        [split] + operands + [grad],
        specs + [by_tile],
        [by_tile, by_pair, by_pair],
        grid=grid,
        scratch=[pltpu.VMEM((group, cols), F32)] * 2,
    )


def middle_body(att_ref, x_ref, w_ref, gain_ref, mix_ref, middle_ref, ffn_ref, coeff_ref):
    n_exp, unused, head_cols = att_ref.shape
    middle = x_ref[...].astype(F32)
    for j in range(n_exp):
        middle = middle + dot(att_ref[j], w_ref[j * head_cols : (j + 1) * head_cols])
    middle_ref[...] = middle
    normed, unused = norm_parts(middle)
    ffn_input = (normed * gain_ref[...]).astype(BF16)
    ffn_ref[...] = ffn_input
    logits = dot_rt(ffn_input, mix_ref[...])
    first, second = (logits[:, 0:1], logits[:, 1:2])
    top = jnp.maximum(first, second)
    first, second = (jnp.exp(first - top), jnp.exp(second - top))
    coeff_ref[...] = jnp.concatenate([first, second], axis=1) / (first + second)


def to_middle(attended, inputs, matrix, gain, mix):
    n_exp, group, head_cols = attended.shape
    width = matrix.shape[0]
    tile = min(512, group)
    return call(
        middle_body,
        0,
        [shape_of((group, width), F32), shape_of((group, width), BF16), shape_of((group, 2), F32)],
        [attended, inputs, matrix, gain, mix],
        [
            pl.BlockSpec((n_exp, tile, head_cols), lambda t: (0, t, 0)),
            by_rows(tile, width),
            whole(matrix.shape),
            whole(gain.shape),
            whole(mix.shape),
        ],
        [by_rows(tile, width), by_rows(tile, width), by_rows(tile, 2)],
        grid=(group // tile,),
    )


def bend(pre):
    square = pre * pre
    bent = jnp.tanh(TANH_SCALE * pre * (1.0 + TANH_CUBE * square))
    half = 0.5 * (1.0 + bent)
    slope = half + 0.5 * pre * (1.0 - bent * bent) * TANH_SCALE * (1.0 + 3.0 * TANH_CUBE * square)
    return ((pre * half).astype(BF16), slope)


def add_step(total, new):
    @pl.when(pl.program_id(0) == 0)
    def first():
        total[...] = new

    @pl.when(pl.program_id(0) > 0)
    def later():
        total[...] += new


def hidden_back(rows_in, rows_grad, up, down, din_sum):
    act, slope = bend(dot(rows_in, up))
    dpre = (slope * dot_rt(rows_grad, down)).astype(BF16)
    add_step(din_sum, dot_rt(dpre, up))
    return (act, dpre)


def fill_rows(own_ref, got_ref, rows_in, rows_grad):
    capacity = own_ref.shape[1]

    @pl.when(pl.program_id(0) == 0)
    def begin():
        rows_in[:capacity] = own_ref[0]
        rows_in[capacity:] = got_ref[0]
        rows_grad[:capacity] = own_ref[1]
        rows_grad[capacity:] = got_ref[1]


def expert_body(
    own_ref,
    got_ref,
    up_ref,
    down_ref,
    keep_ref,
    send_ref,
    act_ref,
    dpre_ref,
    rows_in,
    rows_grad,
    outs,
    dins,
):
    width = own_ref.shape[2]
    capacity = own_ref.shape[1]
    fill_rows(own_ref, got_ref, rows_in, rows_grad)
    up = up_ref[...].reshape(width, -1)
    act, dpre_ref[...] = hidden_back(rows_in[...], rows_grad[...], up, down_ref[0], dins)
    add_step(outs, dot(act, down_ref[0]))
    act_ref[...] = act

    @pl.when(pl.program_id(0) == pl.num_programs(0) - 1)
    def last():
        for k, total in enumerate((outs, dins)):
            keep_ref[k] = total[:capacity]
            send_ref[k] = total[capacity:].astype(BF16)


def expert_grad_body(own_x, got_x, own_g, got_g, act_ref, dpre_ref, grads_ref):
    width = grads_ref.shape[2]
    rows_in = jnp.concatenate([own_x[0], got_x[0]], axis=0)
    rows_grad = jnp.concatenate([own_g[0], got_g[0]], axis=0)
    dup = dot_lt(rows_in, dpre_ref[...]).astype(BF16)
    pair_rows, hidden = dup.shape
    up_rows = hidden // width * pair_rows
    for k in range(hidden // width):
        at = slice(k * pair_rows, (k + 1) * pair_rows)
        grads_ref[0, at] = dup[:, k * width : (k + 1) * width]
    grads_ref[0, up_rows:] = dot_lt(act_ref[...], rows_grad).astype(BF16)


def expert_ffn(own, got, up, down, pair_rows):
    unused, capacity, width = own.shape
    n_chip, exp_cols, unused = down.shape
    per = width // exp_cols
    count = 2 * capacity
    hidden = n_chip * exp_cols
    by_cols = pl.BlockSpec((count, exp_cols), lambda c: (0, c))
    return call(
        expert_body,
        0,
        [
            shape_of(own.shape, F32),
            shape_of(own.shape, BF16),
            shape_of((count, hidden), BF16),
            shape_of((count, hidden), BF16),
        ],
        [own, got, up, down],
        [
            whole(own.shape),
            whole(own.shape),
            pl.BlockSpec((n_chip, pair_rows, exp_cols), lambda c: (0, c // per, c % per)),
            pl.BlockSpec((1, exp_cols, width), lambda c: (c, 0, 0)),
        ],
        [whole(own.shape), whole(own.shape), by_cols, by_cols],
        grid=(n_chip,),
        scratch=[pltpu.VMEM((count, width), BF16)] * 2 + [pltpu.VMEM((count, width), F32)] * 2,
    )


def expert_grad(own, got, act, dpre, n_chip):
    unused, capacity, width = own.shape
    count, hidden = act.shape
    cols, pair_rows = (hidden // n_chip, width // n_chip)
    rows = hidden // width * pair_rows + cols
    by_width = pl.BlockSpec((1, capacity, pair_rows), lambda d: (0, 0, d))
    second = pl.BlockSpec((1, capacity, width), lambda d: (1, 0, 0))
    return call(
        expert_grad_body,
        0,
        [shape_of((n_chip, rows, width), BF16)],
        [own, got, own, got, act, dpre],
        [
            by_width,
            by_width,
            second,
            second,
            pl.BlockSpec((count, cols), lambda d: (0, d)),
            whole(dpre.shape),
        ],
        [pl.BlockSpec((1, rows, width), lambda d: (d, 0, 0))],
        grid=(n_chip,),
    )[0]


def dense_body(ex_ref, x_ref, g_ref, coeff_ref, slot_ref, up_ref, down_ref, *refs):
    outs, (pay_ref, act_ref, dpre_ref, ddense_ref, own_ref, dense, dins) = (refs[:-7], refs[-7:])
    n_exp, padded, width = pay_ref.shape
    rows = padded - PAD

    @pl.when(pl.program_id(0) == 0)
    def begin():
        grad = g_ref[...].astype(F32)
        ddense_ref[...] = (coeff_ref[:, 0:1] * grad).astype(BF16)
        shape = (own_ref.shape[1], x_ref.shape[0])
        pick = (lax.broadcasted_iota(jnp.int32, shape, 0) == slot_ref[...]).astype(F32)
        pick = pick.astype(BF16)
        own_ref[0] = dot(pick, x_ref[...]).astype(BF16)
        own_ref[1] = dot(pick, (coeff_ref[:, 1:2] * grad).astype(BF16)).astype(BF16)

    up = up_ref[...].reshape(width, -1)
    down = down_ref[...].reshape(-1, width)
    act, dpre_ref[...] = hidden_back(x_ref[...], ddense_ref[...], up, down, dins)
    act_ref[...] = act
    add_step(dense, dot(act, down))

    @pl.when(pl.program_id(0) == pl.num_programs(0) - 1)
    def last():
        for k, out_ref in enumerate(outs):
            to = lax.rem(ex_ref[0] + k, len(outs))
            at = pl.ds(pl.multiple_of(to * rows, rows), rows)
            out_ref[...] = (coeff_ref[at, 0:1] * dense[at]).astype(BF16)
        for j in range(n_exp):
            at = slice(j * rows, (j + 1) * rows)
            pay_ref[j, :rows] = dins[at].astype(BF16)
            sums = jnp.sum(g_ref[at].astype(F32) * dense[at], axis=1, keepdims=True)
            line = jnp.transpose(sums * jnp.ones((1, LANES), F32))[:PAD]
            high = line.astype(BF16).astype(F32)
            index = lax.broadcasted_iota(jnp.int32, (PAD, rows), 0)
            extra = jnp.where(index == 0, high, jnp.where(index == 1, line - high, 0.0))
            pay_ref[j, rows:] = jnp.concatenate(
                [extra, jnp.zeros((PAD, width - rows), F32)], axis=1
            ).astype(BF16)


def dense_grad_body(x_ref, g_ref, act_ref, dpre_ref, dup_ref, ddown_ref):
    dup_ref[...] = dot_lt(x_ref[...], dpre_ref[...]).astype(BF16)
    ddown_ref[...] = dot_lt(act_ref[...], g_ref[...]).astype(BF16)


def dense_ffn(ex, ffn_input, grad, coeffs, slot, capacity, weights, specs, hidden, rows):
    group, width = ffn_input.shape
    step = 2 * LANES
    count = group // rows
    operands = [ffn_input, grad, coeffs, slot]
    own = (2, capacity, width)
    padded = (count, rows + PAD, width)
    by_cols = pl.BlockSpec((group, step), lambda c: (0, c))
    return call(
        dense_body,
        0,
        [shape_of((rows, width), BF16)] * count
        + [shape_of(padded, BF16)]
        + [shape_of((group, hidden), BF16)] * 2
        + [shape_of((group, width), BF16), shape_of(own, BF16)],
        [ex] + operands + weights,
        [pl.BlockSpec(memory_space=pltpu.SMEM)] + [whole(o.shape) for o in operands] + specs,
        [whole((rows, width))] * count
        + [whole(padded), by_cols, by_cols, whole((group, width)), whole(own)],
        grid=(hidden // step,),
        scratch=[pltpu.VMEM((group, width), F32)] * 2,
    )


def dense_pack_body(core_ref, x_ref, g_ref, act_ref, dpre_ref, keep_ref, send_ref):
    n_chip, unused, block, unused = keep_ref.shape
    step = act_ref.shape[1]
    chunk = pl.program_id(0)
    left = pl.ds(pl.multiple_of(chunk * step, step), step)
    first_core = core_ref[0] == 0
    dup = dot_lt(x_ref[...], dpre_ref[...]).astype(BF16).reshape(n_chip, 2, block, step)
    ddown = dot_lt(act_ref[...], g_ref[...]).astype(BF16)
    keep_ref[:, 0, :, left] = jnp.where(first_core, dup[:, 0], dup[:, 1])
    send_ref[:, 0, :, left] = jnp.where(first_core, dup[:, 1], dup[:, 0])
    at = pl.ds(chunk, 1)
    keep_ref[at, 1] = jnp.where(first_core, ddown[:block], ddown[block:])[None]
    send_ref[at, 1] = jnp.where(first_core, ddown[block:], ddown[:block])[None]


def dense_split(core, ffn_input, ddense, act, dpre, shape):
    group, step = (ffn_input.shape[0], 2 * LANES)
    by_cols = pl.BlockSpec((group, step), lambda c: (0, c))
    return call(
        dense_pack_body,
        0,
        [shape_of(shape, BF16)] * 2,
        [core, ffn_input, ddense, act, dpre],
        [
            pl.BlockSpec(memory_space=pltpu.SMEM),
            whole(ffn_input.shape),
            whole(ddense.shape),
            by_cols,
            by_cols,
        ],
        [whole(shape)] * 2,
        grid=(act.shape[1] // step,),
    )


def dense_grad(ffn_input, ddense, act, dpre):
    group, width = ffn_input.shape
    hidden = act.shape[1]
    step = 2 * LANES
    by_cols = pl.BlockSpec((group, step), lambda c: (0, c))
    return call(
        dense_grad_body,
        0,
        [shape_of((width, hidden), BF16), shape_of((hidden, width), BF16)],
        [ffn_input, ddense, act, dpre],
        [whole(ffn_input.shape), whole(ddense.shape), by_cols, by_cols],
        [
            pl.BlockSpec((width, step), lambda c: (0, c)),
            pl.BlockSpec((step, width), lambda c: (c, 0)),
        ],
        grid=(hidden // step,),
    )


def middle_back_body(
    ex_ref, pay_ref, slot_ref, middle_ref, coeff_ref, g_ref, gain_ref, mix_ref, w_ref, *refs
):
    rets, (dmid_ref, low_ref, datt_ref, small_ref, base_ref) = (refs[:-5], refs[-5:])
    rows, width = middle_ref.shape
    n_exp = pay_ref.shape[0]
    head_cols = datt_ref.shape[2]
    total = pay_ref[0].astype(F32)
    for j in range(1, n_exp):
        total = total + pay_ref[j].astype(F32)
    capacity = rets[0].shape[1]
    exp_rows, exp_din = (jnp.zeros((rows, width), F32) for k in range(2))
    index = lax.broadcasted_iota(jnp.int32, (rows, capacity), 1)
    for k, ret_ref in enumerate(rets):
        source = lax.rem(ex_ref[0] + n_exp - k, n_exp)
        place = (index + source * capacity == slot_ref[...]).astype(F32).astype(BF16)
        exp_rows = exp_rows + dot(place, ret_ref[0])
        exp_din = exp_din + dot(place, ret_ref[1])
    dffn = total[:rows] + exp_din
    lines = jnp.concatenate([total[rows:, :rows], jnp.zeros((rows - PAD, rows), F32)], axis=0)
    lines = jnp.transpose(lines)
    grad = g_ref[...].astype(F32)
    dcoeff = [lines[:, 0:1] + lines[:, 1:2], jnp.sum(grad * exp_rows, axis=1, keepdims=True)]
    coeff = [coeff_ref[:, k : k + 1] for k in range(2)]
    base_ref[...] = middle_ref[...] + coeff[1] * exp_rows
    inner = coeff[0] * dcoeff[0] + coeff[1] * dcoeff[1]
    dlogit = [(c * (d - inner)).astype(BF16).astype(F32) for c, d in zip(coeff, dcoeff, strict=True)]
    mix = mix_ref[...].astype(F32)
    dffn = dffn + dlogit[0] * mix[0:1] + dlogit[1] * mix[1:2]
    normed, inverse = norm_parts(middle_ref[...])
    gain = gain_ref[...]
    dmiddle = grad + norm_back(dffn, normed, inverse, gain)
    dmid_ref[...] = dmiddle
    low = dmiddle.astype(BF16)
    low_ref[...] = low
    datt = dot_rt(low, w_ref[...]).astype(BF16)
    for j in range(n_exp):
        datt_ref[j] = datt[:, j * head_cols : (j + 1) * head_cols]
    lane = lax.broadcasted_iota(jnp.int32, (rows, LANES), 1)
    pair = jnp.where(lane == 0, dlogit[0], jnp.where(lane == 1, dlogit[1], 0.0)).astype(BF16)
    dmix = dot_lt(pair, (normed * gain).astype(BF16))
    dgain = jnp.sum(dffn * normed, axis=0, keepdims=True)
    nothing = jnp.zeros((1, width), F32)
    small_ref[...] = jnp.concatenate([nothing, dgain, dmix[:2], jnp.zeros((4, width), F32)], axis=0)


def middle_back(ex, arrived, returned, slot, middle, coeffs, grad, gain, mix, matrix, head_cols):
    rows, width = middle.shape
    n_exp = arrived.shape[0]
    operands = [arrived, slot, middle, coeffs, grad, gain, mix, matrix] + list(returned)
    shapes = [
        shape_of((rows, width), F32),
        shape_of((rows, width), BF16),
        shape_of((n_exp, rows, head_cols), BF16),
        shape_of((8, width), F32),
        shape_of((rows, width), F32),
    ]
    return call(
        middle_back_body,
        0,
        shapes,
        [ex] + operands,
        [pl.BlockSpec(memory_space=pltpu.SMEM)] + [whole(o.shape) for o in operands],
        [whole(o.shape) for o in shapes],
    )


def split_cores(core_ref, grads, keep_ref, send_ref):
    n_chip, block = keep_ref.shape[:2]
    grads = grads.reshape(n_chip, 2, block, grads.shape[-1])
    first_core = core_ref[0] == 0
    keep_ref[...] = jnp.where(first_core, grads[:, 0], grads[:, 1])
    send_ref[...] = jnp.where(first_core, grads[:, 1], grads[:, 0])


def out_grad_body(core_ref, att_ref, low_ref, keep_ref, send_ref):
    grads = [dot_lt(att_ref[j], low_ref[...]).astype(BF16) for j in range(att_ref.shape[0])]
    split_cores(core_ref, jnp.concatenate(grads, axis=0), keep_ref, send_ref)


def attn_input_back_body(ex_ref, dq_ref, dk_ref, dv_ref, w_ref, *pays):
    rows = pays[0].shape[0]
    for k, pay_ref in enumerate(pays):
        to = lax.rem(ex_ref[0] + k, len(pays))
        at = pl.ds(pl.multiple_of(to * rows, rows), rows)
        grads = jnp.concatenate([dq_ref[at], dk_ref[at], dv_ref[at]], axis=1)
        pay_ref[...] = dot_rt(grads, w_ref[...]).astype(BF16)


def qkv_grad_body(
    core_ref, x_ref, w_ref, gain_ref, small_ref, dq_ref, dk_ref, dv_ref, keep_ref, send_ref
):
    n_chip, padded, cols = keep_ref.shape
    block = padded - PAD
    rows_in = x_ref[...]
    grads = jnp.concatenate([dot_lt(rows_in, r[...]) for r in (dq_ref, dk_ref, dv_ref)], axis=1)
    width = grads.shape[0]
    dgain = jnp.sum(grads * w_ref[...].astype(F32), axis=1, keepdims=True)
    dgain = jnp.transpose(dgain * jnp.ones((1, LANES), F32))[:8] / gain_ref[...]
    index = lax.broadcasted_iota(jnp.int32, (8, width), 0)
    small = jnp.where(index == 0, dgain, small_ref[...])
    small = jnp.concatenate([small, jnp.zeros((PAD - 8, width), F32)], axis=0)
    first_core = core_ref[0] == 0
    for chip in range(n_chip):
        pair = []
        for core in range(2):
            low = (2 * chip + core) * block
            edge = jnp.concatenate(
                [small[:, low : low + block], jnp.zeros((PAD, cols - block), F32)], axis=1
            )
            pair.append(jnp.concatenate([grads[low : low + block], edge], axis=0).astype(BF16))
        keep_ref[chip] = jnp.where(first_core, pair[0], pair[1])
        send_ref[chip] = jnp.where(first_core, pair[1], pair[0])


def scalar_call(body, shapes, scalar, operands, weight=0):
    return call(
        body,
        weight,
        shapes,
        [scalar] + operands,
        [pl.BlockSpec(memory_space=pltpu.SMEM)] + [whole(o.shape) for o in operands],
        [whole(o.shape) for o in shapes],
    )


def expert_end_body(core_ref, own_ref, got_ref, down_ref, up_out, down_out):
    cols = down_ref.shape[0]
    per = own_ref.shape[2] // cols
    first_core = core_ref[0] == 0
    for k in range(own_ref.shape[0] * per):
        at = slice(k % per * cols, (k % per + 1) * cols)
        mine, theirs = (r[k // per, :, at].astype(F32) for r in (own_ref, got_ref))
        low = 2 * k * cols
        up_out[:, low : low + cols] = jnp.where(first_core, mine, theirs)
        up_out[:, low + cols : low + 2 * cols] = jnp.where(first_core, theirs, mine)
    down_out[...] = down_ref[...].astype(F32)


def leave_body(x_ref, gain_ref, dmid_ref, *refs):
    pays, out_ref = (refs[:-1], refs[-1])
    dattn = pays[0][...].astype(F32)
    for pay_ref in pays[1:]:
        dattn = dattn + pay_ref[...].astype(F32)
    normed, inverse = norm_parts(x_ref[...].astype(F32))
    out_ref[...] = (dmid_ref[...] + norm_back(dattn, normed, inverse, gain_ref[...])).astype(BF16)


def simple(body, weight, shape, operands):
    return call(
        body,
        weight,
        [shape],
        operands,
        [whole(o.shape) for o in operands],
        [whole(shape.shape)],
    )[0]


def shards(
    tokens,
    first_gain,
    w_qkv,
    w_out,
    second_gain,
    w_mix,
    w_up,
    w_down,
    expert_up,
    expert_down,
    expert_ids,
    doc_lengths,
    out_grad,
):
    rows, width = tokens.shape
    n_chip, n_core, n_exp = (lax.axis_size(a) for a in ("chip", "core", "expert"))
    n_dp = n_chip * n_core
    group = rows * n_exp
    head_cols = width // n_exp
    qkv_cols = 3 * head_cols
    w_rows = w_qkv.shape[0]
    block = n_exp * w_rows
    dense_rows = w_down.shape[0]
    dense_cols = n_dp * dense_rows
    exp_rows = expert_up.shape[1]
    exp_cols = expert_down.shape[1]
    ex = lax.axis_index("expert")
    ex_line = jnp.full((1,), ex, jnp.int32)
    core = lax.axis_index("core")
    core_line = jnp.full((1,), core, jnp.int32)
    share_cap = max(2, 5 * rows // (4 * n_exp))
    capacity = n_exp * share_cap
    bits = chip_bits()

    exp_split = (
        expert_up[0]
        .reshape(exp_rows, n_chip, n_core, exp_cols)
        .transpose(2, 0, 1, 3)
        .reshape(n_core, exp_rows, n_chip * exp_cols)
    )
    own_half, sent_half = by_core(core, exp_split[0], exp_split[1])
    chip_up = jnp.concatenate(by_core(core, own_half, other_core(sent_half)), axis=0)
    pair_rows = n_core * exp_rows
    n_block = n_chip * exp_cols // width
    up_rows = n_block * pair_rows
    chip_up = chip_up.reshape(pair_rows, n_block, width).transpose(1, 0, 2)
    down_all = lax.all_gather(expert_down[0], "chip", axis=0, tiled=True)
    down_all = down_all.reshape(n_chip, exp_cols, width)

    qkv_blocks = w_qkv.reshape(w_rows, 3, n_exp, head_cols).transpose(2, 0, 1, 3)
    small = jnp.stack([first_gain, second_gain, w_mix[:, 0], w_mix[:, 1]])
    small = jnp.concatenate(
        [
            jnp.pad(small, ((0, w_rows - 4), (0, LANES - w_rows))),
            jnp.pad(expert_ids[:, 0].astype(BF16)[None], ((0, w_rows - 1), (0, LANES - rows))),
        ],
        axis=1,
    )
    up_blocks = w_up.reshape(w_rows, n_dp, n_exp, dense_rows).transpose(2, 0, 1, 3)
    others = jnp.concatenate([w_out, small], axis=1)
    dealt = swap(
        jnp.concatenate(
            [
                qkv_blocks.reshape(n_exp, w_rows, qkv_cols),
                up_blocks.reshape(n_exp, w_rows, dense_cols),
                jnp.broadcast_to(others[None], (n_exp,) + others.shape),
            ],
            axis=2,
        ),
        "expert",
    )
    at = [qkv_cols, qkv_cols + dense_cols, qkv_cols + dense_cols + width]
    up_own = dealt[:, :, at[0] : at[1]].reshape(block, dense_cols)
    out_own = dealt[:, :, at[1] : at[2]].reshape(block, width)
    chip_up = chip_up.reshape(up_rows, width)
    grad_copies = jnp.broadcast_to(out_grad[None], (n_exp,) + out_grad.shape)
    dealt, chip_up, grad_copies = lax.optimization_barrier((dealt, chip_up, grad_copies))
    choice = after(dealt[:, 0, at[2] + LANES : at[2] + LANES + rows].astype(F32)).astype(jnp.int32)
    small = dealt[:, :4, at[2] : at[2] + w_rows].transpose(1, 0, 2).reshape(4, block)
    first_own = jnp.concatenate(
        [
            dealt[:, :, :qkv_cols].reshape(block, qkv_cols),
            jnp.pad(small, ((0, 4), (0, qkv_cols - block))),
        ]
    )
    group_tokens = share(after(tokens, dealt), "expert")
    first_parts = gather_small(first_own, DP, n_dp)
    small = first_parts[-1][:, -8:-4, :block].transpose(1, 0, 2).reshape(4, width)
    gain_one = small[0:1].astype(F32)
    gain_two = small[1:2].astype(F32)
    mix_rows = jnp.pad(small[2:4], ((0, PAD - 2), (0, 0)))

    group_tokens = after(group_tokens, first_parts, gain_one)
    inputs = group_tokens.reshape(group, width)
    step = 2 * LANES
    if dense_cols == width and dense_rows == block:
        dense_pack = after(jnp.concatenate([out_own, up_own, w_down], axis=0), inputs, down_all)
        dense_all = lax.all_gather(dense_pack, DP, axis=0, tiled=True)
        dense_all = dense_all.reshape(n_dp, 3, block, width)
        out_matrix = dense_all[:, 0].reshape(width, width)
        up_matrix = down_matrix = dense_all
        up_spec = pl.BlockSpec((n_dp, 1, block, step), lambda c: (0, 1, 0, c))
        down_spec = pl.BlockSpec((step // block, 1, block, width), lambda c: (c, 2, 0, 0))
    else:
        out_matrix, up_matrix, down_matrix = (
            lax.all_gather(w, DP, axis=0, tiled=True) for w in (out_own, up_own, w_down)
        )
        up_spec = pl.BlockSpec((width, step), lambda c: (0, c))
        down_spec = pl.BlockSpec((step, width), lambda c: (c, 0))
    chip_up = after(chip_up, inputs)
    up_all = lax.all_gather(chip_up, "chip", axis=0, tiled=True)
    up_all = up_all.reshape(n_chip, up_rows, width)

    grad_all = swap(after(grad_copies, inputs), "expert").reshape(group, width)

    qkv, attn_input, qkv_matrix = enter(inputs, gain_one, first_parts)
    doc_split = doc_lengths[0, :1]
    attended_own = attend(qkv, doc_split, head_cols, n_exp)
    attended_own, grad_all = lax.optimization_barrier((attended_own, grad_all))
    attended_all = swap(attended_own, "expert")
    same = (choice[:, :, None] == choice[:, None, :]).astype(jnp.int32)
    earlier = jnp.arange(rows)[None, None, :] < jnp.arange(rows)[None, :, None]
    rank = jnp.sum(jnp.where(earlier, same, 0), axis=2)
    first_slot = jnp.arange(n_exp, dtype=jnp.int32)[:, None] * share_cap
    slot = jnp.where(choice == ex, first_slot + rank, -1).reshape(1, group)
    slot_own = lax.dynamic_slice_in_dim(choice * share_cap + rank, ex, 1, 0).reshape(rows, 1)
    slot, slot_own = lax.optimization_barrier((slot, slot_own))
    attended_all = after(attended_all, out_matrix, slot)
    middle, ffn_input, coeffs = to_middle(attended_all, inputs, out_matrix, gain_two, mix_rows)


    weights, specs = ([up_matrix, down_matrix], [up_spec, down_spec])
    *out_parts, payload, dense_act, dense_dpre, ddense, own_rows = dense_ffn(
        ex_line, ffn_input, grad_all, coeffs, slot, capacity, weights, specs, dense_cols, rows
    )
    arrived = swap(payload, "expert")
    joined = dense_cols == width and dense_rows == block and step == 2 * block
    if joined:
        shape = (n_chip, 2, block, width)
        grads = dense_split(core_line, ffn_input, ddense, dense_act, dense_dpre, shape)
    else:
        grads = dense_grad(ffn_input, ddense, dense_act, dense_dpre)
    got_rows, *grads = lax.optimization_barrier((other_core(own_rows), *grads))
    if joined:
        dense_core = (grads[0].astype(F32) + other_core(grads[1]).astype(F32)).astype(BF16)
        got_rows, dense_core = lax.optimization_barrier((got_rows, dense_core))
        dense_sum = lax.psum_scatter(
            dense_core.reshape(-1, width), "chip", scatter_dimension=0, tiled=True
        )
        up_sum, down_sum = (dense_sum[:block], dense_sum[block:])
    else:
        up_sum, down_sum = (
            lax.psum_scatter(g, DP, scatter_dimension=0, tiled=True) for g in grads
        )
    exp_keep, exp_send, exp_act, exp_dpre = expert_ffn(
        own_rows, got_rows, up_all, down_all, pair_rows
    )
    exp_back = other_core(exp_send)
    returned = []
    for k in range(n_exp):
        low = lax.rem(ex + k, n_exp) * share_cap
        piece = [lax.dynamic_slice_in_dim(v, low, share_cap, 1) for v in (exp_keep, exp_back)]
        returned.append((piece[0] + piece[1].astype(F32)).astype(BF16))
    exp_grads = expert_grad(
        own_rows, got_rows, exp_act, exp_dpre, n_chip
    )
    arrived, exp_grads, *returned = lax.optimization_barrier((arrived, exp_grads, *returned))
    returned = turn_all(returned)
    exp_sum = lax.psum_scatter(
        exp_grads.reshape(-1, width), "chip", scatter_dimension=0, tiled=True
    )

    def mine(values, size=rows):
        return lax.dynamic_slice_in_dim(values, ex * size, size, 0)

    middle_own, coeffs_own = (mine(middle), mine(coeffs))
    att_own = lax.dynamic_slice_in_dim(attended_all, ex * rows, rows, 1)
    returned[0] = after(returned[0], middle_own, coeffs_own, att_own)
    dmiddle, dmid_low, datt, small_two, out_base = middle_back(
        ex_line,
        arrived,
        returned,
        slot_own,
        middle_own,
        coeffs_own,
        out_grad,
        gain_two,
        mix_rows,
        out_matrix,
        head_cols,
    )
    dattended = swap(datt, "expert")
    out_keep, out_send = scalar_call(
        out_grad_body,
        [shape_of((n_chip, block, width), BF16)] * 2,
        core_line,
        [att_own, dmid_low],
    )
    dattended, out_keep, out_send = lax.optimization_barrier((dattended, out_keep, out_send))
    dattended = dattended.reshape(group, head_cols)
    out_sums = turn_all([after(piece, dattended) for piece in out_parts])
    out_core = out_keep.astype(F32) + other_core(out_send).astype(F32)
    out_fold = Fold((out_core,))
    out_fold.orders = [chip_bits()[::-1]]
    out_fold.send()

    dparts = attend_back(qkv, dattended, doc_split, head_cols)
    qkv_shape = shape_of((n_chip, block + PAD, qkv_cols), BF16)
    qkv_keep, qkv_send = scalar_call(
        qkv_grad_body,
        [qkv_shape] * 2,
        core_line,
        [attn_input, qkv_matrix, gain_one, small_two] + list(dparts),
    )
    dparts = [after(dparts[0], qkv_keep), dparts[1], dparts[2]]
    dattn_parts = scalar_call(
        attn_input_back_body,
        [shape_of((rows, width), BF16)] * n_exp,
        ex_line,
        dparts + [qkv_matrix],
    )
    met = out_fold.meet(*dattn_parts, *out_sums)
    dattn_parts, out_sums = (met[:n_exp], met[n_exp:])
    dattn = turn_all(dattn_parts)
    qkv_send = after(qkv_send, dattn_parts[0])
    qkv_core = qkv_keep.astype(F32) + other_core(qkv_send).astype(F32)
    half = qkv_cols // 2
    halves = (qkv_core,)
    if half % LANES == 0:
        halves = (qkv_core[..., :half], qkv_core[..., half:])
    fold = Fold(halves)
    fold.send()
    while out_fold.orders[0]:
        out_fold.send()
        out_fold.meet()
    fold.meet()
    while fold.orders[0]:
        fold.send()
        dattn = fold.meet(*dattn)
    out_weight_sum, qkv_sum = (out_fold.pair[0], jnp.concatenate(fold.pair, axis=-1))
    out_total = out_base
    for piece in out_sums:
        out_total = out_total + piece.astype(F32)
    small_sum = qkv_sum[block : block + 4, :block].reshape(4, n_exp, w_rows).transpose(1, 0, 2)
    small_sum = jnp.pad(small_sum, ((0, 0), (0, w_rows - 4), (0, LANES - w_rows)))
    tail = jnp.concatenate(
        [
            qkv_sum[:block].reshape(n_exp, w_rows, qkv_cols),
            out_weight_sum.reshape(n_exp, w_rows, width),
            small_sum,
            up_sum.astype(F32).reshape(n_exp, w_rows, dense_cols),
        ],
        axis=2,
    ).astype(BF16)
    tail_sent = after(tail, *dattn)
    tail = swap(tail_sent, "expert")
    tokens_grad = simple(
        leave_body, LAST, shape_of((rows, width), BF16), [tokens, gain_one, dmiddle] + list(dattn)
    )

    exp_sum = after(exp_sum, tail_sent)
    up_exp_sum = exp_sum[:up_rows].reshape(n_block, n_core, exp_rows, width)
    own_exp = lax.dynamic_index_in_dim(up_exp_sum, core, 1, False)
    sent_exp = lax.dynamic_index_in_dim(up_exp_sum, 1 - core, 1, False)
    exp_up_grad, exp_down_grad = scalar_call(
        expert_end_body,
        [shape_of((exp_rows, n_dp * exp_cols), F32), shape_of((exp_cols, width), F32)],
        core_line,
        [own_exp, other_core(sent_exp), exp_sum[up_rows:]],
    )
    tail = after(tail, exp_up_grad, exp_down_grad, tokens_grad, out_total, down_sum)
    up_grad = tail[:, :, qkv_cols + width + LANES :].reshape(n_exp, w_rows, n_dp, dense_rows)
    up_grad = up_grad.transpose(1, 2, 0, 3).reshape(w_rows, n_exp * dense_cols).astype(F32)
    qkv_grad = tail[:, :, :qkv_cols].reshape(n_exp, w_rows, 3, head_cols)
    small_sum = jnp.sum(tail[:, :4, qkv_cols + width : qkv_cols + width + w_rows].astype(F32), axis=0)
    return (
        out_total.astype(BF16),
        tokens_grad,
        small_sum[0],
        qkv_grad.transpose(1, 2, 0, 3).reshape(w_rows, 3 * width).astype(F32),
        jnp.sum(tail[:, :, qkv_cols : qkv_cols + width].astype(F32), axis=0),
        small_sum[1],
        small_sum[2:4].T,
        up_grad,
        down_sum.astype(F32),
        exp_up_grad[None],
        exp_down_grad[None],
    )


def solution(mesh):
    n_dp, n_exp = (mesh.shape["dp"], mesh.shape["expert"])
    fine = Mesh(mesh.devices.reshape(n_dp // 2, 2, n_exp), ("chip", "core", "expert"))
    every = ("chip", "core", "expert")
    rows = P(every, None)
    expert = P("expert", DP, None)
    return jax.shard_map(
        shards,
        mesh=fine,
        in_specs=(
            rows,
            P(every),
            rows,
            rows,
            P(every),
            rows,
            rows,
            rows,
            expert,
            expert,
            rows,
            P(DP, None),
            rows,
        ),
        out_specs=(
            rows,
            rows,
            P(every),
            rows,
            rows,
            P(every),
            rows,
            rows,
            rows,
            expert,
            expert,
        ),
        check_vma=False,
    )
```
